32 devices in a mesh: seq: 8 (over z, core), dp: 4 (over y, x).
Axes of the slice: x: 2, y: 2, z: 4, core: 2. Of those that a mesh axis runs over, the one named last changes fastest.
Arguments:
- queries: bfloat16 [4, 1024, 1024], P('dp', 'seq'), may hold values from -6 to 6
- key_vectors: bfloat16 [4, 1024, 1024], P('dp', 'seq'), may hold values from -6 to 6
- value_vectors: bfloat16 [4, 1024, 1024], P('dp', 'seq'), may hold values from -64 to 64
- log_decay: float32 [4, 1024, 16], P('dp', 'seq'), may hold values from -1 to 0, as said below
- restart: int32 [4, 1024], P('dp', 'seq'), may hold values 0 or 1
- norm_gain: float32 [1024], replicated, may hold values from 0.5 to 1.5
- upstream: bfloat16 [4, 1024, 1024], P('dp', 'seq'), may hold values from -6 to 6
Outputs:
- layer_out: bfloat16 [4, 1024, 1024], P('dp', 'seq')
- grad_query: bfloat16 [4, 1024, 1024], P('dp', 'seq')
- grad_key: bfloat16 [4, 1024, 1024], P('dp', 'seq')
- grad_value: bfloat16 [4, 1024, 1024], P('dp', 'seq')
- grad_decay: float32 [4, 1024, 16], P('dp', 'seq')
- grad_gain: float32 [1024], replicated
The draws below stay inside these ranges and needn't reach their ends.
Inputs may be any that keep to these rules, and one draw needn't show every extreme that they name: `log_decay`: never positive. `restart`: 1 marks a sample before which the state is cleared.
All inputs are finite; a program needn't handle non-finite values. No bound on the sum of `restart` on one device may be relied on, other than what follows from the above.
Results may differ from the reference program's by a relative error of at most 0.0096.
Values sent between devices are 32-bit elements; how exact they have to be, the bound alone decides.
No kernel may reach another device: no remote copies, remote signals or barrier semaphores. Data moves between devices by JAX's collectives and lax.ppermute only.
A program may use at most 128 MiB of HBM per device.

```python
import math
import jax
import jax.numpy as jnp
from jax import lax

HEAD_TOTAL = 16
D = 1024
TOK_DEV = 128
SCAN_LENGTH = 1024
SCAN_COUNT = 4


def draw_value_vectors(key, part):
    key_base, key_rows, key_columns = jax.random.split(key, 3)
    base = jnp.clip(jax.random.normal(key_base, (SCAN_COUNT, SCAN_LENGTH, D), jnp.float32), -6.0, 6.0)
    row_scale = jnp.exp(jax.random.uniform(key_rows, (SCAN_COUNT, SCAN_LENGTH, 1), jnp.float32, -1.15, 1.15))
    column_scale = jnp.exp(jax.random.uniform(key_columns, (1, 1, D), jnp.float32, -1.15, 1.15))
    return (base * row_scale * column_scale).astype(jnp.bfloat16)


def draw_log_decay(key, part):
    key_quick, key_token, key_block, key_where, key_width = jax.random.split(key, 5)
    quick_share = 0.45
    quick = jax.random.uniform(key_quick, (SCAN_COUNT, 1, HEAD_TOTAL), jnp.float32) < quick_share
    decay_floor = jnp.where(quick, 6.0 / TOK_DEV, 0.4 / SCAN_LENGTH)
    token_decay_factor = jax.random.uniform(key_token, (SCAN_COUNT, SCAN_LENGTH, HEAD_TOTAL), jnp.float32, 0.5, 1.5)
    block_draw = jax.random.uniform(key_block, (SCAN_COUNT, SCAN_LENGTH // TOK_DEV, 1, HEAD_TOTAL), jnp.float32, 0.7, 1.4)
    block_decay_factor = jnp.repeat(block_draw, TOK_DEV, axis=2).reshape(SCAN_COUNT, SCAN_LENGTH, HEAD_TOTAL)
    places = jax.random.randint(key_where, (SCAN_COUNT, 1, 2), 0, SCAN_LENGTH)
    positions = jnp.arange(SCAN_LENGTH, dtype=jnp.int32)[None, :, None]
    reset_marks = jnp.any(positions == places, axis=2)
    reset_flags = jax.random.uniform(key_width, (SCAN_COUNT, SCAN_LENGTH, HEAD_TOTAL), jnp.float32, math.log(0.5), math.log(0.8))
    return -decay_floor * token_decay_factor * block_decay_factor + jnp.where(reset_marks[..., None], reset_flags, 0.0)


def touch_ends(drawn, own_key, low, top_value):
    dims = drawn.shape
    place = [jax.random.randint(jax.random.fold_in(own_key, axis), (), 0, dims[axis]) for axis in range(len(dims))]
    drawn = drawn.at[tuple(place)].set(low)
    longest = dims.index(max(dims))
    place[longest] = (place[longest] + 1) % dims[longest]
    return drawn.at[tuple(place)].set(top_value)


def raised(drawn, rng, source, target, blocks, factor):
    def block_of(position):
        return (jnp.arange(drawn.shape[position]) // (drawn.shape[position] // blocks)).reshape((-1,) + (1,) * (drawn.ndim - 1 - position))

    one_side = jax.random.permutation(rng, blocks)[block_of(target)]
    other_side = (block_of(target) + blocks // 2) % blocks
    return jnp.where((block_of(source) == one_side) | (block_of(source) == other_side), factor * drawn, drawn)


def block_levels(rng, dims, cuts, smallest, top_value):
    loudness, own = 1.0, jax.random.fold_in(rng, 6)
    for dim, blocks in cuts:
        heights = jnp.exp(jax.random.uniform(jax.random.fold_in(own, dim), (blocks,), jnp.float32, smallest / len(cuts), top_value / len(cuts)))
        loudness = loudness * jnp.repeat(heights, dims[dim] // blocks).reshape([-1 if axis == dim else 1 for axis in range(len(dims))])
    return loudness


def scatter_about(rng, extent, deviation, bound, cuts=(), kind=jnp.bfloat16):
    factor_of = block_levels(rng, extent, cuts, -0.22, 0.18) if cuts else 1.0
    result = jax.random.normal(rng, extent, jnp.float32) * deviation * factor_of
    return jnp.minimum(jnp.maximum(result, -bound), bound).astype(kind)


def bell_draw_with(rng, shape, scale, bound, cuts, heavy, kind=jnp.bfloat16):
    values = scale * jax.random.normal(rng, shape, jnp.float32)
    if cuts:
        values = values * block_levels(rng, shape, cuts, -0.22, 0.18)
    return jnp.clip(raised(values, jax.random.fold_in(rng, 3), *heavy), -bound, bound).astype(kind)


def setup_inputs(seed: int = 0) -> dict:
    streams_of = jax.random.split(jax.random.key(seed), 8)
    return {
        "queries": scatter_about(streams_of[0], (SCAN_COUNT, SCAN_LENGTH, D), 1.0, 6.0, ((0, 4), (1, 8))),
        "key_vectors": scatter_about(streams_of[1], (SCAN_COUNT, SCAN_LENGTH, D), 1.0, 6.0, ((0, 4), (1, 8))),
        "value_vectors": draw_value_vectors(jax.random.fold_in(streams_of[7], 71), 0),
        "log_decay": draw_log_decay(jax.random.fold_in(streams_of[7], 71), 0),
        "restart": touch_ends((jax.random.randint(streams_of[4], (SCAN_COUNT, SCAN_LENGTH), 0, 16 * TOK_DEV) < 1).astype(jnp.int32), jax.random.fold_in(streams_of[4], 1), 0, 1),
        "norm_gain": jnp.clip(1.0 + 0.1 * jax.random.normal(streams_of[5], (D,), jnp.float32), 0.5, 1.5),
        "upstream": bell_draw_with(streams_of[6], (SCAN_COUNT, SCAN_LENGTH, D), 1.0, 6.0, ((0, 4), (1, 8)), (1, 2, 8, 2.0)),
    }


EPSILON = 1e-06
EXACT = lax.Precision.HIGHEST

def blend(pattern, first_operand, second_operand):
    return jnp.einsum(pattern, first_operand.astype(jnp.float32), second_operand.astype(jnp.float32), precision=EXACT)

def exact(pattern, first_operand, second_operand):
    return jnp.einsum(pattern, first_operand, second_operand, precision=EXACT)

def split_heads(row_data, head_count):
    return row_data.reshape(row_data.shape[0], row_data.shape[1], head_count, row_data.shape[2] // head_count)

def decay_tables(log_decay, restart):
    summed = jnp.cumsum(log_decay, axis=1)
    resets = jnp.cumsum(restart, axis=1, dtype=jnp.int32)
    last_total = summed[:, -1, :]
    last_reset = resets[:, -1:]
    entry_decay = jnp.where((resets == 0)[:, :, None], jnp.exp(summed), 0.0)
    exit_decay = jnp.where((resets == last_reset)[:, :, None], jnp.exp(last_total[:, None, :] - summed), 0.0)
    block_carry = jnp.where(last_reset == 0, jnp.exp(last_total), 0.0)
    by_head = jnp.transpose(summed, (0, 2, 1))
    spread = by_head[:, :, :, None] - by_head[:, :, None, :]
    row_index = lax.broadcasted_iota(jnp.int32, spread.shape, 2)
    col_index = lax.broadcasted_iota(jnp.int32, spread.shape, 3)
    allowed = (row_index >= col_index) & (resets[:, None, :, None] == resets[:, None, None, :])
    pair_decay = jnp.exp(jnp.where(allowed, spread, -1e+30))
    return (entry_decay, exit_decay, block_carry, pair_decay)

def block_state(key_heads, value_heads, exit_decay):
    decayed_keys = key_heads.astype(jnp.float32) * exit_decay[..., None]
    return (exact('bjhe,bjhf->bhef', decayed_keys, value_heads.astype(jnp.float32)), decayed_keys)

def block_forward(query_heads, key_heads, value_heads, entry_decay, pair_decay, state_in, norm_gain, upstream_heads):
    head_count = query_heads.shape[2]
    scores = blend('bihe,bjhe->bhij', query_heads, key_heads)
    weights = (scores * pair_decay).astype(jnp.bfloat16)
    local_part = blend('bhij,bjhe->bihe', weights, value_heads)
    decayed_queries = query_heads.astype(jnp.float32) * entry_decay[..., None]
    carried_part = exact('bihe,bhef->bihf', decayed_queries, state_in)
    mixture = local_part + carried_part
    inverse = lax.rsqrt(lax.optimization_barrier(jnp.mean(mixture * mixture, axis=-1, keepdims=True)) + EPSILON)
    normed = mixture * inverse
    gain_heads = norm_gain.reshape(head_count, -1)
    layer_out = (normed * gain_heads).astype(jnp.bfloat16)
    upstream_float = upstream_heads.astype(jnp.float32)
    gain_part = lax.optimization_barrier(jnp.sum(upstream_float * normed, axis=(0, 1)))
    grad_normed = upstream_float * gain_heads
    grad_mixed = (inverse * (grad_normed - normed * lax.optimization_barrier(jnp.mean(grad_normed * normed, axis=-1, keepdims=True)))).astype(jnp.bfloat16)
    query_state = exact('bihe,bihf->bhef', decayed_queries, grad_mixed.astype(jnp.float32))
    flat_out = layer_out.reshape(layer_out.shape[0], layer_out.shape[1], -1)
    return (scores, weights, carried_part, flat_out, gain_part, grad_mixed, query_state)

def block_backward(query_heads, key_heads, value_heads, entry_decay, exit_decay, block_carry, pair_decay, scores, weights, carried_part, decayed_keys, grad_mixed, state_in, state_grad):
    grad_pairs = blend('bihe,bjhe->bhij', grad_mixed, value_heads)
    grad_weights = (grad_pairs * pair_decay).astype(jnp.bfloat16)
    mixed_float = grad_mixed.astype(jnp.float32)
    values_float = value_heads.astype(jnp.float32)
    grad_query = blend('bhij,bjhe->bihe', grad_weights, key_heads) + exact('bihf,bhef->bihe', mixed_float * entry_decay[..., None], state_in)
    grad_key = blend('bhij,bihe->bjhe', grad_weights, query_heads) + exact('bjhf,bhef->bjhe', values_float * exit_decay[..., None], state_grad)
    carried_value = exact('bjhe,bhef->bjhf', decayed_keys, state_grad)
    grad_value = blend('bhij,bihe->bjhe', weights, grad_mixed) + carried_value
    pair_terms = scores * grad_pairs * pair_decay
    balance = lax.optimization_barrier(jnp.sum(pair_terms, axis=3)) - lax.optimization_barrier(jnp.sum(pair_terms, axis=2))
    later_terms = jnp.transpose(balance, (0, 2, 1)) + lax.optimization_barrier(jnp.sum(carried_part * mixed_float, axis=-1))
    earlier_terms = lax.optimization_barrier(jnp.sum(carried_value * values_float, axis=-1))
    through = block_carry * lax.optimization_barrier(jnp.sum(state_in * state_grad, axis=(2, 3)))
    grad_decay = jnp.flip(jnp.cumsum(jnp.flip(later_terms, 1), axis=1), 1) + (jnp.cumsum(earlier_terms, axis=1) - earlier_terms) + through[:, None, :]
    row_shape = (grad_query.shape[0], grad_query.shape[1], -1)
    return (grad_query.reshape(row_shape).astype(jnp.bfloat16), grad_key.reshape(row_shape).astype(jnp.bfloat16), grad_value.reshape(row_shape).astype(jnp.bfloat16), grad_decay)

def reference(queries, key_vectors, value_vectors, log_decay, restart, norm_gain, upstream):
    block_total = SCAN_LENGTH // TOK_DEV

    def to_blocks(array):
        shaped = array.reshape((SCAN_COUNT, block_total, TOK_DEV) + array.shape[2:])
        return jnp.swapaxes(shaped, 0, 1)

    def from_blocks(array):
        return jnp.swapaxes(array, 0, 1).reshape((SCAN_COUNT, SCAN_LENGTH) + array.shape[3:])
    inputs = tuple((to_blocks(array) for array in (queries, key_vectors, value_vectors, log_decay, restart, upstream)))

    def prepare(package):
        query_rows, key_rows, value_rows, decay_rows, restart_rows, upstream_rows = package
        tables = decay_tables(decay_rows, restart_rows)
        heads_all = (split_heads(query_rows, HEAD_TOTAL), split_heads(key_rows, HEAD_TOTAL), split_heads(value_rows, HEAD_TOTAL), split_heads(upstream_rows, HEAD_TOTAL))
        return (tables, heads_all)

    def first_pass(package):
        tables, heads_all = prepare(package)
        state_part, unused_keys = block_state(heads_all[1], heads_all[2], tables[1])
        return (tables[2], state_part)
    carries, parts = lax.map(first_pass, inputs)
    zero_state = jnp.zeros(parts.shape[1:], jnp.float32)

    def forward_step(state, element):
        return (element[0][..., None, None] * state + element[1], state)
    unused_end, states_in = lax.scan(forward_step, zero_state, (carries, parts))

    def second_pass(package):
        tables, heads_all = prepare(package[:6])
        results = block_forward(heads_all[0], heads_all[1], heads_all[2], tables[0], tables[3], package[6], norm_gain, heads_all[3])
        return (results[3], results[4], results[6])
    outputs_all, gain_parts, query_states = lax.map(second_pass, inputs + (states_in,))

    def backward_step(gradient, element):
        return (element[1] + element[0][..., None, None] * gradient, gradient)
    unused_start, states_grad = lax.scan(backward_step, zero_state, (carries, query_states), reverse=True)

    def third_pass(package):
        tables, heads_all = prepare(package[:6])
        state_in = package[6]
        state_grad = package[7]
        unused_part, decayed_keys = block_state(heads_all[1], heads_all[2], tables[1])
        results = block_forward(heads_all[0], heads_all[1], heads_all[2], tables[0], tables[3], state_in, norm_gain, heads_all[3])
        return block_backward(heads_all[0], heads_all[1], heads_all[2], tables[0], tables[1], tables[2], tables[3], results[0], results[1], results[2], decayed_keys, results[5], state_in, state_grad)
    grad_query, grad_key, grad_value, grad_decay = lax.map(third_pass, inputs + (states_in, states_grad))
    grad_gain = lax.optimization_barrier(jnp.sum(gain_parts, axis=0)).reshape(-1)
    return (from_blocks(outputs_all), from_blocks(grad_query), from_blocks(grad_key), from_blocks(grad_value), from_blocks(grad_decay), grad_gain)
```

```python
import functools

import jax
import jax.numpy as jnp
from jax import lax
from jax.experimental import pallas as pl
from jax.experimental.pallas import tpu as pltpu
from jax.sharding import PartitionSpec as P

HEAD_TOTAL = 16
EPSILON = 1e-06
LANES = 128
F32 = jnp.float32
BF16 = jnp.bfloat16
COLUMNS, MASK, CUM_ROWS, CARRY_ROWS, TABLE_ROWS = 0, 128, 256, 272, 288


def dot(a, b, contract_a=1, contract_b=0):
    return lax.dot_general(
        a, b, (((contract_a,), (contract_b,)), ((), ())), preferred_element_type=F32
    )


def halves(x):
    high = x.astype(BF16)
    return high, (x - high.astype(F32)).astype(BF16)


def stacked(x, axis):
    return jnp.concatenate(halves(x), axis=axis)


def twice(x, axis):
    return jnp.concatenate([x, x], axis=axis)


def left_lanes(shape):
    return lax.broadcasted_iota(jnp.int32, shape, 1) < LANES // 2


def triangle(tokens, keep):
    rows = lax.broadcasted_iota(jnp.int32, (tokens, tokens), 0)
    columns = lax.broadcasted_iota(jnp.int32, (tokens, tokens), 1)
    return keep(rows, columns)


def by_head(x, axis):
    left = left_lanes(x.shape)
    zero = jnp.zeros_like(x)
    return jnp.concatenate([jnp.where(left, x, zero), jnp.where(left, zero, x)], axis=axis)


def fold(x):
    rows = x.shape[0] // 2
    return jnp.where(left_lanes((rows, LANES)), x[:rows], x[rows:])


def pair_columns(table, first, tokens):
    return jnp.where(
        left_lanes((tokens, LANES)),
        jnp.broadcast_to(table[:, first : first + 1], (tokens, LANES)),
        jnp.broadcast_to(table[:, first + 1 : first + 2], (tokens, LANES)),
    )


def make_tables(log_decay, restart):
    tokens = log_decay.shape[0]
    heads = log_decay.shape[1]
    lower = triangle(tokens, lambda t, s: s <= t).astype(F32).astype(BF16)
    upper = triangle(tokens, lambda t, s: t <= s).astype(F32).astype(BF16)
    marks = jnp.broadcast_to(restart.astype(F32), (tokens, tokens)).astype(BF16)
    resets_column = dot(lower, marks, 1, 1)
    resets_row = dot(marks, upper)
    padded = jnp.concatenate(
        [log_decay, jnp.zeros((tokens, LANES - heads), F32)], axis=1
    )
    first, rest = halves(padded)
    third = (padded - first.astype(F32) - rest.astype(F32)).astype(BF16)
    cum = dot(
        jnp.concatenate([lower, lower, lower], axis=1),
        jnp.concatenate([first, rest, third], axis=0),
    )
    last = cum[tokens - 1 :, :]
    last_reset = resets_column[tokens - 1 :, :]
    entry = jnp.where(resets_column == 0.0, jnp.exp(cum), 0.0)
    leave = jnp.where(resets_column == last_reset, jnp.exp(last - cum), 0.0)
    lane = lax.broadcasted_iota(jnp.int32, (tokens, LANES), 1)
    columns = jnp.where(
        lane < heads,
        cum,
        jnp.where(lane < 2 * heads, pltpu.roll(entry, heads, 1), pltpu.roll(leave, 2 * heads, 1)),
    )
    allowed = triangle(tokens, lambda t, s: t >= s) & (resets_column == resets_row)
    mask = jnp.where(allowed, 0.0, -1e30)
    cum_rows = jnp.transpose(cum)[:heads]
    carry = jnp.where(last_reset[:, :1] == 0.0, jnp.exp(cum_rows[:, tokens - 1 :]), 0.0)
    return columns, mask, cum_rows, jnp.broadcast_to(carry, (heads, LANES))


def pick_columns(columns, half):
    return jnp.where(half == 0, columns, pltpu.roll(columns, LANES - HEAD_TOTAL // 2, 1))


def pick_rows(rows, half):
    count = HEAD_TOTAL // 2
    return jnp.where(half == 0, rows[:count], rows[count:])


def write_states(half, columns, carry_rows, key_ref, value_ref, out_ref):
    tokens = key_ref.shape[1]
    table = pick_columns(columns, half)
    carry = pick_rows(carry_rows, half)
    left = left_lanes((1, LANES))
    rows = []
    for pair in range(HEAD_TOTAL // 4):
        lanes = pl.ds(pair * LANES, LANES)
        leave = pair_columns(table, 2 * HEAD_TOTAL + 2 * pair, tokens)
        decayed = key_ref[0, :, lanes].astype(F32) * leave
        state = dot(stacked(decayed, 0), twice(value_ref[0, :, lanes], 0), 0, 0)
        out_ref[pl.ds(pair * 64, 64), :] = fold(state)
        rows.append(jnp.where(left, carry[2 * pair : 2 * pair + 1], carry[2 * pair + 1 : 2 * pair + 2]))
    rows.append(jnp.zeros((8 - len(rows), LANES), F32))
    out_ref[pl.ds(HEAD_TOTAL // 4 * 64, 8), :] = jnp.concatenate(rows, axis=0)


def first_state_kernel(half_ref, key_ref, value_ref, decay_ref, restart_ref, out_ref, table_ref):
    columns, mask, cum_rows, carry_rows = make_tables(decay_ref[0], restart_ref[...])
    table_ref[pl.ds(COLUMNS, 128), :] = columns
    table_ref[pl.ds(MASK, 128), :] = mask
    table_ref[pl.ds(CUM_ROWS, 16), :] = cum_rows
    table_ref[pl.ds(CARRY_ROWS, 16), :] = carry_rows
    write_states(half_ref[0], columns, carry_rows, key_ref, value_ref, out_ref)


def second_state_kernel(half_ref, key_ref, value_ref, table_ref, out_ref):
    write_states(
        half_ref[0],
        table_ref[pl.ds(COLUMNS, 128), :],
        table_ref[pl.ds(CARRY_ROWS, 16), :],
        key_ref,
        value_ref,
        out_ref,
    )


def pair_decays(table, cum_rows, mask, pair, tokens):
    parts = []
    for head in (2 * pair, 2 * pair + 1):
        column = jnp.broadcast_to(table[:, head : head + 1], (tokens, tokens))
        parts.append(jnp.exp(column - cum_rows[head : head + 1] + mask))
    return jnp.concatenate(parts, axis=0)


def side_by_side(x):
    rows = x.shape[0] // 2
    return jnp.concatenate([x[:rows], x[rows:]], axis=1)


def mixture_kernel(half_ref, query_ref, key_ref, value_ref, table_ref, out_ref):
    tokens = query_ref.shape[1]
    half = half_ref[0]
    table = pick_columns(table_ref[pl.ds(COLUMNS, 128), :], half)
    cum_rows = pick_rows(table_ref[pl.ds(CUM_ROWS, 16), :], half)
    mask = table_ref[pl.ds(MASK, 128), :]
    for pair in range(HEAD_TOTAL // 4):
        lanes = pl.ds(pair * LANES, LANES)
        scores = dot(by_head(query_ref[0, :, lanes], 0), key_ref[0, :, lanes], 1, 1)
        weights = (scores * pair_decays(table, cum_rows, mask, pair, tokens)).astype(BF16)
        out_ref[:, lanes] = dot(side_by_side(weights), by_head(value_ref[0, :, lanes], 0))


def forward_kernel(
    half_ref,
    mixed_ref,
    query_ref,
    upstream_ref,
    gain_ref,
    state_ref,
    table_ref,
    before_ref,
    unused_ref,
    layer_ref,
    grad_mixed_ref,
    out_ref,
):
    tokens = query_ref.shape[1]
    half = half_ref[0]
    table = pick_columns(table_ref[pl.ds(COLUMNS, 128), :], half)
    pairs = HEAD_TOTAL // 4
    gains = jnp.where(half == 0, gain_ref[:pairs, :], gain_ref[pairs:, :])
    own = left_lanes((LANES, LANES)) == (lax.broadcasted_iota(jnp.int32, (LANES, LANES), 0) < 64)
    average = twice(jnp.where(own, 1.0 / 64.0, 0.0).astype(BF16), 0)
    gain_parts = []
    for pair in range(pairs):
        lanes = pl.ds(pair * LANES, LANES)
        query = query_ref[0, :, lanes]
        entry = pair_columns(table, HEAD_TOTAL + 2 * pair, tokens)
        state = by_head(state_ref[pl.ds(pair * 64, 64), :], 0)
        mixture = mixed_ref[:, lanes] + entry * dot(twice(query, 1), stacked(state, 0))
        square = dot(stacked(mixture * mixture, 1), average)
        inverse = lax.rsqrt(square + EPSILON)
        normed = mixture * inverse
        gain = gains[pair : pair + 1]
        layer_ref[0, :, lanes] = (normed * gain).astype(BF16)
        upstream = upstream_ref[0, :, lanes].astype(F32)
        gain_parts.append(jnp.sum(upstream * normed, axis=0, keepdims=True))
        grad_normed = upstream * gain
        shared = dot(stacked(grad_normed * normed, 1), average)
        grad_mixed = (inverse * (grad_normed - normed * shared)).astype(BF16)
        grad_mixed_ref[:, lanes] = grad_mixed
        decayed = query.astype(F32) * entry
        out_ref[pl.ds(pair * 64, 64), :] = fold(
            dot(stacked(decayed, 0), twice(grad_mixed, 0), 0, 0)
        )
    part = jnp.concatenate(gain_parts, axis=0)
    blank = jnp.zeros_like(part)
    part = jnp.where(
        half == 0,
        jnp.concatenate([part, blank], axis=0),
        jnp.concatenate([blank, part], axis=0),
    )
    out_ref[pl.ds(pairs * 64, 8), :] = part + before_ref[...]


def backward_kernel(
    half_ref,
    query_ref,
    key_ref,
    value_ref,
    grad_mixed_ref,
    state_ref,
    table_ref,
    unused_ref,
    grad_query_ref,
    grad_key_ref,
    grad_value_ref,
    later_ref,
):
    tokens = query_ref.shape[1]
    half = half_ref[0]
    table = pick_columns(table_ref[pl.ds(COLUMNS, 128), :], half)
    cum_rows = pick_rows(table_ref[pl.ds(CUM_ROWS, 16), :], half)
    mask = table_ref[pl.ds(MASK, 128), :]
    earlier = twice(triangle(tokens, lambda s, t: s < t).astype(F32).astype(BF16), 0)
    reached = triangle(tokens, lambda u, t: u >= t)
    chooser = twice(head_chooser(), 1)
    balance_rows = []
    entry_rows = []
    for pair in range(HEAD_TOTAL // 4):
        lanes = pl.ds(pair * LANES, LANES)
        query = query_ref[0, :, lanes]
        key = key_ref[0, :, lanes]
        value = value_ref[0, :, lanes]
        grad_mixed = grad_mixed_ref[:, lanes]
        query_rows = by_head(query, 0)
        mixed_rows = by_head(grad_mixed, 0)
        decay = pair_decays(table, cum_rows, mask, pair, tokens)
        decayed_scores = dot(query_rows, key, 1, 1) * decay
        grad_pairs = dot(mixed_rows, value, 1, 1)
        weights = decayed_scores.astype(BF16)
        grad_weights = (grad_pairs * decay).astype(BF16)
        entry = pair_columns(table, HEAD_TOTAL + 2 * pair, tokens)
        state = by_head(state_ref[pl.ds(pair * 64, 64), :], 0)
        carried = entry * dot(twice(grad_mixed, 1), stacked(state, 1), 1, 1)
        grad_query_ref[0, :, lanes] = (
            dot(side_by_side(grad_weights), by_head(key, 0)) + carried
        ).astype(BF16)
        grad_key_ref[:, lanes] = dot(grad_weights, query_rows, 0, 0)
        grad_value_ref[:, lanes] = dot(weights, mixed_rows, 0, 0)
        before = dot(stacked(decayed_scores * grad_pairs, 1), earlier)
        for head in range(2):
            part = before[head * tokens : (head + 1) * tokens]
            balance_rows.append(jnp.sum(jnp.where(reached, part, 0.0), axis=0, keepdims=True))
        terms = dot(chooser, stacked(query.astype(F32) * carried, 1), 1, 1)
        entry_rows.append(terms[:2])
    later_ref[...] = jnp.concatenate(balance_rows, axis=0) + row_sums(
        jnp.concatenate(entry_rows, axis=0), reached
    )


def head_chooser():
    rows = lax.broadcasted_iota(jnp.int32, (8, LANES), 0)
    left = left_lanes((8, LANES))
    chosen = ((rows == 0) & left) | ((rows == 1) & ~left)
    return jnp.where(chosen, 1.0, 0.0).astype(BF16)


def row_sums(rows, keep):
    first, second = halves(rows)
    third = (rows - first.astype(F32) - second.astype(F32)).astype(BF16)
    weight = jnp.where(keep, 1.0, 0.0).astype(BF16)
    return dot(
        jnp.concatenate([first, second, third], axis=1),
        jnp.concatenate([weight, weight, weight], axis=0),
    )


def final_kernel(
    half_ref,
    key_ref,
    value_ref,
    grad_key_part_ref,
    grad_value_part_ref,
    later_ref,
    state_ref,
    grad_ref,
    table_ref,
    other_ref,
    unused_key_ref,
    unused_value_ref,
    grad_key_ref,
    grad_value_ref,
    rows_ref,
    decay_ref,
):
    tokens = key_ref.shape[1]
    half = half_ref[0]
    table = pick_columns(table_ref[pl.ds(COLUMNS, 128), :], half)
    carry = pick_rows(table_ref[pl.ds(CARRY_ROWS, 16), :], half)
    chooser = twice(head_chooser(), 1)
    left = left_lanes((1, LANES))
    earlier_rows = []
    through_rows = []
    for pair in range(HEAD_TOTAL // 4):
        lanes = pl.ds(pair * LANES, LANES)
        key = key_ref[0, :, lanes]
        value = value_ref[0, :, lanes]
        leave = pair_columns(table, 2 * HEAD_TOTAL + 2 * pair, tokens)
        packed = grad_ref[pl.ds(pair * 64, 64), :]
        high, low = halves(by_head(packed, 0))
        key_part = leave * dot(twice(value, 1), jnp.concatenate([high, low], axis=1), 1, 1)
        carried = leave * dot(twice(key, 1), jnp.concatenate([high, low], axis=0))
        grad_key_ref[0, :, lanes] = (grad_key_part_ref[:, lanes] + key_part).astype(BF16)
        grad_value_ref[0, :, lanes] = (grad_value_part_ref[:, lanes] + carried).astype(BF16)
        terms = dot(chooser, stacked(carried * value.astype(F32), 1), 1, 1)
        earlier_rows.append(terms[:2])
        product = jnp.sum(packed * state_ref[pl.ds(pair * 64, 64), :], axis=0, keepdims=True)
        for side in (left, ~left):
            through_rows.append(jnp.sum(jnp.where(side, product, 0.0), axis=1, keepdims=True))
    rows = (
        later_ref[...]
        + row_sums(
            jnp.concatenate(earlier_rows, axis=0), triangle(tokens, lambda u, t: u < t)
        )
        + carry * jnp.concatenate(through_rows, axis=0)
    )
    rows_ref[...] = rows
    other = other_ref[...]
    every = jnp.where(
        half == 0,
        jnp.concatenate([rows, other], axis=0),
        jnp.concatenate([other, rows], axis=0),
    )
    square = jnp.concatenate([every, jnp.zeros((LANES - HEAD_TOTAL, LANES), F32)], axis=0)
    decay_ref[0] = jnp.transpose(square)[:, :HEAD_TOTAL]


def call(kernel, half, operands, results, aliases=None, flops=0):
    def spec(shape, kind):
        if kind == "columns":
            return pl.BlockSpec((1, shape[1], shape[2] // 2), lambda i, h: (0, 0, h[0]))
        if kind == "unread":
            return pl.BlockSpec(memory_space=pl.ANY)
        if kind == "top":
            return pl.BlockSpec((8, shape[1]), lambda i, h: (shape[0] // 8 - 1, 0))
        return pl.BlockSpec(shape, lambda i, h: (0,) * len(shape))

    read = sum(a.size * a.dtype.itemsize for a, kind in operands if kind != "unread")
    return pl.pallas_call(
        kernel,
        grid_spec=pltpu.PrefetchScalarGridSpec(
            num_scalar_prefetch=1,
            grid=(1,),
            in_specs=[spec(a.shape, kind) for a, kind in operands],
            out_specs=[spec(shape, kind) for shape, dtype, kind in results],
        ),
        out_shape=[jax.ShapeDtypeStruct(shape, dtype) for shape, dtype, kind in results],
        input_output_aliases=aliases or {},
        compiler_params=pltpu.CompilerParams(vmem_limit_bytes=32 * 1024 * 1024),
        cost_estimate=pl.CostEstimate(flops=flops, bytes_accessed=read, transcendentals=0),
    )(half, *[a for a, kind in operands])


def local(queries, key_vectors, value_vectors, log_decay, restart, norm_gain, upstream):
    tokens, width = queries.shape[1], queries.shape[2]
    pairs = HEAD_TOTAL // 4
    state_rows = pairs * 64
    buffer_rows = state_rows + 8
    blocks = lax.axis_size("seq")
    scans = lax.axis_size("dp")
    position = lax.axis_index("seq")
    core = position & 1
    on_first = core == 0
    own = core.reshape(1).astype(jnp.int32)
    other = 1 - own
    half_width = width // 2

    def exchange(x, bit, axis="seq"):
        size = blocks if axis == "seq" else scans
        return lax.ppermute(x, axis, [(i, i ^ bit) for i in range(size)])

    def parts(buffer):
        state = buffer[:state_rows].reshape(pairs, 64, LANES)
        return state, buffer[state_rows : state_rows + pairs].reshape(pairs, 1, LANES)

    def joined(state, carry):
        return jnp.concatenate(
            [
                state.reshape(state_rows, LANES),
                carry.reshape(pairs, LANES),
                jnp.zeros((8 - pairs, LANES), F32),
            ],
            axis=0,
        )

    def flat(state):
        return state.reshape(state_rows, LANES)

    whole = (1, tokens, width)
    part = (tokens, half_width)
    buffer = (buffer_rows, LANES)

    state_other, tables = call(
        first_state_kernel,
        other,
        [
            (key_vectors, "columns"),
            (value_vectors, "columns"),
            (log_decay, "all"),
            (restart, "all"),
        ],
        [(buffer, F32, "all"), ((TABLE_ROWS, LANES), F32, "all")],
    )
    swapped = exchange(state_other, 1)
    (state_own,) = call(
        second_state_kernel,
        own,
        [(key_vectors, "columns"), (value_vectors, "columns"), (tables, "all")],
        [(buffer, F32, "all")],
    )
    first_state, first_carry = parts(jnp.where(on_first, state_own, swapped))
    second_state, second_carry = parts(jnp.where(on_first, swapped, state_own))
    total = second_carry * first_state + second_state
    carry = first_carry * second_carry
    prefix = jnp.zeros_like(total)
    prefix_carry = jnp.ones_like(carry)
    levels = []
    bit = 2
    while bit < blocks:
        is_upper = (position & bit) != 0
        theirs, their_carry = parts(exchange(joined(total, carry), bit))
        prefix = jnp.where(is_upper, prefix_carry * theirs + prefix, prefix)
        prefix_carry = jnp.where(is_upper, prefix_carry * their_carry, prefix_carry)
        levels.append((bit, is_upper, carry, their_carry))
        total = jnp.where(is_upper, carry * theirs + total, their_carry * total + theirs)
        carry = carry * their_carry
        bit *= 2
    after_first = first_carry * prefix + first_state
    state_in_own = flat(jnp.where(on_first, prefix, after_first))
    state_in_other = exchange(flat(jnp.where(on_first, after_first, prefix)), 1)

    mixed = {}
    for name, half in (("own", own), ("other", other)):
        (mixed[name],) = call(
            mixture_kernel,
            half,
            [
                (queries, "columns"),
                (key_vectors, "columns"),
                (value_vectors, "columns"),
                (tables, "all"),
            ],
            [(part, F32, "all")],
        )

    gain_rows = norm_gain.reshape(2 * pairs, LANES)
    layer_out = None
    results = {}
    before = jnp.zeros((8, LANES), F32)
    for name, half, state_in in (("own", own, state_in_own), ("other", other, state_in_other)):
        operands = [
            (mixed[name], "all"),
            (queries, "columns"),
            (upstream, "columns"),
            (gain_rows, "all"),
            (state_in, "all"),
            (tables, "all"),
            (before, "all" if name == "own" else "top"),
        ]
        if name == "own":
            kernel = lambda *refs: forward_kernel(*refs[:8], None, *refs[8:])
            aliases = None
        else:
            operands.append((layer_out, "unread"))
            kernel = forward_kernel
            aliases = {len(operands): 0}
        layer_out, grad_mixed, query_state = call(
            kernel,
            half,
            operands,
            [(whole, BF16, "columns"), (part, BF16, "all"), (buffer, F32, "all")],
            aliases,
        )
        before = query_state
        results[name] = (grad_mixed, query_state, state_in)

    query_state_own = results["own"][1]
    query_state_other = results["other"][1]
    swapped = exchange(query_state_other, 1)
    first_query, _ = parts(jnp.where(on_first, query_state_own, swapped))
    second_query, _ = parts(jnp.where(on_first, swapped, query_state_own))
    gain = query_state_other[state_rows:] + swapped[state_rows:]
    total = first_query + first_carry * second_query
    suffix = jnp.zeros_like(total)
    suffix_carry = jnp.ones_like(carry)
    for bit, is_upper, carry, their_carry in levels:
        received = exchange(jnp.concatenate([flat(total), gain], axis=0), bit)
        theirs, _ = parts(received)
        gain = gain + received[state_rows:]
        suffix = jnp.where(is_upper, suffix, suffix_carry * theirs + suffix)
        suffix_carry = jnp.where(is_upper, suffix_carry, suffix_carry * their_carry)
        total = jnp.where(is_upper, theirs + their_carry * total, total + carry * theirs)
    before_second = second_query + second_carry * suffix
    state_grad_own = flat(jnp.where(on_first, before_second, suffix))
    state_grad_other = exchange(flat(jnp.where(on_first, suffix, before_second)), 1)
    bit = 1
    while bit < scans:
        gain = gain + sum(exchange(gain, k * bit, "dp") for k in range(1, min(4, scans // bit)))
        bit *= 4

    grad_query = None
    local_parts = {}
    for name, half in (("own", own), ("other", other)):
        grad_mixed, _, state_in = results[name]
        operands = [
            (queries, "columns"),
            (key_vectors, "columns"),
            (value_vectors, "columns"),
            (grad_mixed, "all"),
            (state_in, "all"),
            (tables, "all"),
        ]
        if name == "own":
            kernel = lambda *refs: backward_kernel(*refs[:7], None, *refs[7:])
            aliases = None
        else:
            operands.append((grad_query, "unread"))
            kernel = backward_kernel
            aliases = {len(operands): 0}
        grad_query, *local_parts[name] = call(
            kernel,
            half,
            operands,
            [
                (whole, BF16, "columns"),
                (part, F32, "all"),
                (part, F32, "all"),
                ((HEAD_TOTAL // 2, LANES), F32, "all"),
            ],
            aliases,
        )

    rows = jnp.zeros((HEAD_TOTAL // 2, LANES), F32)
    for name, half, state_grad in (
        ("own", own, state_grad_own),
        ("other", other, state_grad_other),
    ):
        grad_key_part, grad_value_part, later = local_parts[name]
        operands = [
            (key_vectors, "columns"),
            (value_vectors, "columns"),
            (grad_key_part, "all"),
            (grad_value_part, "all"),
            (later, "all"),
            (results[name][2], "all"),
            (state_grad, "all"),
            (tables, "all"),
            (rows, "all"),
        ]
        if name == "own":
            kernel = lambda *refs: final_kernel(*refs[:10], None, None, *refs[10:])
            aliases = None
        else:
            operands += [(grad_key, "unread"), (grad_value, "unread")]
            kernel = final_kernel
            aliases = {len(operands) - 1: 0, len(operands): 1}
        grad_key, grad_value, rows, grad_decay = call(
            kernel,
            half,
            operands,
            [
                (whole, BF16, "columns"),
                (whole, BF16, "columns"),
                ((HEAD_TOTAL // 2, LANES), F32, "all"),
                ((1, tokens, HEAD_TOTAL), F32, "all"),
            ],
            aliases,
        )
    return (layer_out, grad_query, grad_key, grad_value, grad_decay, gain.reshape(-1))


def solution(mesh):
    rows = P("dp", "seq", None)
    return jax.shard_map(
        local,
        mesh=mesh,
        in_specs=(rows, rows, rows, rows, P("dp", "seq"), P(), rows),
        out_specs=(rows, rows, rows, rows, rows, P()),
        check_vma=False,
    )
```

```python
import functools

import jax
import jax.numpy as jnp
from jax import lax
from jax.experimental import pallas as pl
from jax.experimental.pallas import tpu as pltpu
from jax.sharding import PartitionSpec as P

HEAD_TOTAL = 16
EPSILON = 1e-06
LANES = 128
F32 = jnp.float32
BF16 = jnp.bfloat16
COLUMNS, MASK, CUM_ROWS, CARRY_ROWS, TABLE_ROWS = 0, 128, 256, 272, 288


def dot(a, b, contract_a=1, contract_b=0):
    return lax.dot_general(
        a, b, (((contract_a,), (contract_b,)), ((), ())), preferred_element_type=F32
    )


def halves(x):
    high = x.astype(BF16)
    return high, (x - high.astype(F32)).astype(BF16)


def stacked(x, axis):
    return jnp.concatenate(halves(x), axis=axis)


def twice(x, axis):
    return jnp.concatenate([x, x], axis=axis)


def left_lanes(shape):
    return lax.broadcasted_iota(jnp.int32, shape, 1) < LANES // 2


def triangle(tokens, keep):
    rows = lax.broadcasted_iota(jnp.int32, (tokens, tokens), 0)
    columns = lax.broadcasted_iota(jnp.int32, (tokens, tokens), 1)
    return keep(rows, columns)


def by_head(x, axis):
    left = left_lanes(x.shape)
    zero = jnp.zeros_like(x)
    return jnp.concatenate([jnp.where(left, x, zero), jnp.where(left, zero, x)], axis=axis)


def fold(x):
    rows = x.shape[0] // 2
    return jnp.where(left_lanes((rows, LANES)), x[:rows], x[rows:])


def pair_columns(table, first, tokens):
    return jnp.where(
        left_lanes((tokens, LANES)),
        jnp.broadcast_to(table[:, first : first + 1], (tokens, LANES)),
        jnp.broadcast_to(table[:, first + 1 : first + 2], (tokens, LANES)),
    )


def make_tables(decay_rows, restart):
    heads, tokens = decay_rows.shape
    lower = triangle(tokens, lambda t, s: s <= t).astype(F32).astype(BF16)
    upper = triangle(tokens, lambda t, s: t <= s).astype(F32).astype(BF16)
    marks = jnp.broadcast_to(restart.astype(F32), (tokens, tokens)).astype(BF16)
    resets_column = dot(lower, marks, 1, 1)
    resets_row = dot(marks, upper)
    cum_rows = row_sums(decay_rows, triangle(tokens, lambda s, t: s <= t))
    cum = jnp.transpose(
        jnp.concatenate([cum_rows, jnp.zeros((LANES - heads, tokens), F32)], axis=0)
    )
    last = cum[tokens - 1 :, :]
    last_reset = resets_column[tokens - 1 :, :]
    entry = jnp.where(resets_column == 0.0, jnp.exp(cum), 0.0)
    leave = jnp.where(resets_column == last_reset, jnp.exp(last - cum), 0.0)
    lane = lax.broadcasted_iota(jnp.int32, (tokens, LANES), 1)
    columns = jnp.where(
        lane < heads,
        cum,
        jnp.where(lane < 2 * heads, pltpu.roll(entry, heads, 1), pltpu.roll(leave, 2 * heads, 1)),
    )
    allowed = triangle(tokens, lambda t, s: t >= s) & (resets_column == resets_row)
    mask = jnp.where(allowed, 0.0, -1e30)
    carry = jnp.where(last_reset[:, :1] == 0.0, jnp.exp(cum_rows[:, tokens - 1 :]), 0.0)
    return columns, mask, cum_rows, jnp.broadcast_to(carry, (heads, LANES))


def pick_columns(columns, half):
    return jnp.where(half == 0, columns, pltpu.roll(columns, LANES - HEAD_TOTAL // 2, 1))


def pick_rows(rows, half):
    count = HEAD_TOTAL // 2
    return jnp.where(half == 0, rows[:count], rows[count:])


def write_states(half, columns, carry_rows, key_ref, value_ref, out_ref):
    tokens = key_ref.shape[1]
    table = pick_columns(columns, half)
    carry = pick_rows(carry_rows, half)
    left = left_lanes((1, LANES))
    rows = []
    for pair in range(HEAD_TOTAL // 4):
        lanes = pl.ds(pair * LANES, LANES)
        leave = pair_columns(table, 2 * HEAD_TOTAL + 2 * pair, tokens)
        decayed = key_ref[0, :, lanes].astype(F32) * leave
        state = dot(stacked(decayed, 0), twice(value_ref[0, :, lanes], 0), 0, 0)
        out_ref[pl.ds(pair * 64, 64), :] = fold(state)
        rows.append(jnp.where(left, carry[2 * pair : 2 * pair + 1], carry[2 * pair + 1 : 2 * pair + 2]))
    rows.append(jnp.zeros((8 - len(rows), LANES), F32))
    out_ref[pl.ds(HEAD_TOTAL // 4 * 64, 8), :] = jnp.concatenate(rows, axis=0)


def first_state_kernel(half_ref, key_ref, value_ref, decay_ref, restart_ref, out_ref, table_ref):
    columns, mask, cum_rows, carry_rows = make_tables(decay_ref[0], restart_ref[...])
    table_ref[pl.ds(COLUMNS, 128), :] = columns
    table_ref[pl.ds(MASK, 128), :] = mask
    table_ref[pl.ds(CUM_ROWS, 16), :] = cum_rows
    table_ref[pl.ds(CARRY_ROWS, 16), :] = carry_rows
    write_states(half_ref[0], columns, carry_rows, key_ref, value_ref, out_ref)


def second_state_kernel(half_ref, key_ref, value_ref, table_ref, out_ref):
    write_states(
        half_ref[0],
        table_ref[pl.ds(COLUMNS, 128), :],
        table_ref[pl.ds(CARRY_ROWS, 16), :],
        key_ref,
        value_ref,
        out_ref,
    )


def pair_decays(table, cum_rows, mask, pair, tokens):
    parts = []
    for head in (2 * pair, 2 * pair + 1):
        column = jnp.broadcast_to(table[:, head : head + 1], (tokens, tokens))
        parts.append(jnp.exp(column - cum_rows[head : head + 1] + mask))
    return jnp.concatenate(parts, axis=0)


def side_by_side(x):
    rows = x.shape[0] // 2
    return jnp.concatenate([x[:rows], x[rows:]], axis=1)


def mixture_kernel(half_ref, query_ref, key_ref, value_ref, table_ref, out_ref):
    tokens = query_ref.shape[1]
    half = half_ref[0]
    table = pick_columns(table_ref[pl.ds(COLUMNS, 128), :], half)
    cum_rows = pick_rows(table_ref[pl.ds(CUM_ROWS, 16), :], half)
    mask = table_ref[pl.ds(MASK, 128), :]
    for pair in range(HEAD_TOTAL // 4):
        lanes = pl.ds(pair * LANES, LANES)
        scores = dot(by_head(query_ref[0, :, lanes], 0), key_ref[0, :, lanes], 1, 1)
        weights = (scores * pair_decays(table, cum_rows, mask, pair, tokens)).astype(BF16)
        out_ref[:, lanes] = dot(side_by_side(weights), by_head(value_ref[0, :, lanes], 0))


def forward_kernel(
    half_ref,
    mixed_ref,
    query_ref,
    upstream_ref,
    gain_ref,
    state_ref,
    table_ref,
    before_ref,
    unused_ref,
    layer_ref,
    grad_mixed_ref,
    out_ref,
):
    tokens = query_ref.shape[1]
    half = half_ref[0]
    table = pick_columns(table_ref[pl.ds(COLUMNS, 128), :], half)
    pairs = HEAD_TOTAL // 4
    gains = jnp.where(half == 0, gain_ref[:pairs, :], gain_ref[pairs:, :])
    own = left_lanes((LANES, LANES)) == (lax.broadcasted_iota(jnp.int32, (LANES, LANES), 0) < 64)
    average = twice(jnp.where(own, 1.0 / 64.0, 0.0).astype(BF16), 0)
    gain_parts = []
    for pair in range(pairs):
        lanes = pl.ds(pair * LANES, LANES)
        query = query_ref[0, :, lanes]
        entry = pair_columns(table, HEAD_TOTAL + 2 * pair, tokens)
        state = by_head(state_ref[pl.ds(pair * 64, 64), :], 0)
        mixture = mixed_ref[:, lanes] + entry * dot(twice(query, 1), stacked(state, 0))
        square = dot(stacked(mixture * mixture, 1), average)
        inverse = lax.rsqrt(square + EPSILON)
        normed = mixture * inverse
        gain = gains[pair : pair + 1]
        layer_ref[0, :, lanes] = (normed * gain).astype(BF16)
        upstream = upstream_ref[0, :, lanes].astype(F32)
        gain_parts.append(jnp.sum(upstream * normed, axis=0, keepdims=True))
        grad_normed = upstream * gain
        shared = dot(stacked(grad_normed * normed, 1), average)
        grad_mixed = (inverse * (grad_normed - normed * shared)).astype(BF16)
        grad_mixed_ref[:, lanes] = grad_mixed
        decayed = query.astype(F32) * entry
        out_ref[pl.ds(pair * 64, 64), :] = fold(
            dot(stacked(decayed, 0), twice(grad_mixed, 0), 0, 0)
        )
    part = jnp.concatenate(gain_parts, axis=0)
    blank = jnp.zeros_like(part)
    part = jnp.where(
        half == 0,
        jnp.concatenate([part, blank], axis=0),
        jnp.concatenate([blank, part], axis=0),
    )
    out_ref[pl.ds(pairs * 64, 8), :] = part + before_ref[...]


def backward_kernel(
    half_ref,
    query_ref,
    key_ref,
    value_ref,
    grad_mixed_ref,
    state_ref,
    table_ref,
    unused_ref,
    grad_query_ref,
    grad_key_ref,
    grad_value_ref,
    later_ref,
):
    tokens = query_ref.shape[1]
    half = half_ref[0]
    table = pick_columns(table_ref[pl.ds(COLUMNS, 128), :], half)
    cum_rows = pick_rows(table_ref[pl.ds(CUM_ROWS, 16), :], half)
    mask = table_ref[pl.ds(MASK, 128), :]
    earlier = twice(triangle(tokens, lambda s, t: s < t).astype(F32).astype(BF16), 0)
    reached = triangle(tokens, lambda u, t: u >= t)
    chooser = twice(head_chooser(), 1)
    balance_rows = []
    entry_rows = []
    for pair in range(HEAD_TOTAL // 4):
        lanes = pl.ds(pair * LANES, LANES)
        query = query_ref[0, :, lanes]
        key = key_ref[0, :, lanes]
        value = value_ref[0, :, lanes]
        grad_mixed = grad_mixed_ref[:, lanes]
        query_rows = by_head(query, 0)
        mixed_rows = by_head(grad_mixed, 0)
        decay = pair_decays(table, cum_rows, mask, pair, tokens)
        decayed_scores = dot(query_rows, key, 1, 1) * decay
        grad_pairs = dot(mixed_rows, value, 1, 1)
        weights = decayed_scores.astype(BF16)
        grad_weights = (grad_pairs * decay).astype(BF16)
        entry = pair_columns(table, HEAD_TOTAL + 2 * pair, tokens)
        state = by_head(state_ref[pl.ds(pair * 64, 64), :], 0)
        carried = entry * dot(twice(grad_mixed, 1), stacked(state, 1), 1, 1)
        grad_query_ref[0, :, lanes] = (
            dot(side_by_side(grad_weights), by_head(key, 0)) + carried
        ).astype(BF16)
        grad_key_ref[:, lanes] = dot(grad_weights, query_rows, 0, 0)
        grad_value_ref[:, lanes] = dot(weights, mixed_rows, 0, 0)
        before = dot(stacked(decayed_scores * grad_pairs, 1), earlier)
        for head in range(2):
            part = before[head * tokens : (head + 1) * tokens]
            balance_rows.append(jnp.sum(jnp.where(reached, part, 0.0), axis=0, keepdims=True))
        terms = dot(chooser, stacked(query.astype(F32) * carried, 1), 1, 1)
        entry_rows.append(terms[:2])
    later_ref[...] = jnp.concatenate(balance_rows, axis=0) + row_sums(
        jnp.concatenate(entry_rows, axis=0), reached
    )


def head_chooser():
    rows = lax.broadcasted_iota(jnp.int32, (8, LANES), 0)
    left = left_lanes((8, LANES))
    chosen = ((rows == 0) & left) | ((rows == 1) & ~left)
    return jnp.where(chosen, 1.0, 0.0).astype(BF16)


def row_sums(rows, keep):
    first, second = halves(rows)
    third = (rows - first.astype(F32) - second.astype(F32)).astype(BF16)
    weight = jnp.where(keep, 1.0, 0.0).astype(BF16)
    return dot(
        jnp.concatenate([first, second, third], axis=1),
        jnp.concatenate([weight, weight, weight], axis=0),
    )


def final_kernel(
    half_ref,
    key_ref,
    value_ref,
    grad_key_part_ref,
    grad_value_part_ref,
    later_ref,
    state_ref,
    grad_ref,
    table_ref,
    other_ref,
    unused_key_ref,
    unused_value_ref,
    grad_key_ref,
    grad_value_ref,
    rows_ref,
    decay_ref,
):
    tokens = key_ref.shape[1]
    half = half_ref[0]
    table = pick_columns(table_ref[pl.ds(COLUMNS, 128), :], half)
    carry = pick_rows(table_ref[pl.ds(CARRY_ROWS, 16), :], half)
    chooser = twice(head_chooser(), 1)
    left = left_lanes((1, LANES))
    earlier_rows = []
    through_rows = []
    for pair in range(HEAD_TOTAL // 4):
        lanes = pl.ds(pair * LANES, LANES)
        key = key_ref[0, :, lanes]
        value = value_ref[0, :, lanes]
        leave = pair_columns(table, 2 * HEAD_TOTAL + 2 * pair, tokens)
        packed = grad_ref[pl.ds(pair * 64, 64), :]
        high, low = halves(by_head(packed, 0))
        key_part = leave * dot(twice(value, 1), jnp.concatenate([high, low], axis=1), 1, 1)
        carried = leave * dot(twice(key, 1), jnp.concatenate([high, low], axis=0))
        grad_key_ref[0, :, lanes] = (grad_key_part_ref[:, lanes] + key_part).astype(BF16)
        grad_value_ref[0, :, lanes] = (grad_value_part_ref[:, lanes] + carried).astype(BF16)
        terms = dot(chooser, stacked(carried * value.astype(F32), 1), 1, 1)
        earlier_rows.append(terms[:2])
        product = jnp.sum(packed * state_ref[pl.ds(pair * 64, 64), :], axis=0, keepdims=True)
        for side in (left, ~left):
            through_rows.append(jnp.sum(jnp.where(side, product, 0.0), axis=1, keepdims=True))
    rows = (
        later_ref[...]
        + row_sums(
            jnp.concatenate(earlier_rows, axis=0), triangle(tokens, lambda u, t: u < t)
        )
        + carry * jnp.concatenate(through_rows, axis=0)
    )
    rows_ref[...] = rows
    other = other_ref[...]
    every = jnp.where(
        half == 0,
        jnp.concatenate([rows, other], axis=0),
        jnp.concatenate([other, rows], axis=0),
    )
    decay_ref[0] = every


def call(kernel, half, operands, results, aliases=None, flops=0):
    def spec(shape, kind):
        if kind == "columns":
            return pl.BlockSpec((1, shape[1], shape[2] // 2), lambda i, h: (0, 0, h[0]))
        if kind == "unread":
            return pl.BlockSpec(memory_space=pl.ANY)
        if kind == "top":
            return pl.BlockSpec((8, shape[1]), lambda i, h: (shape[0] // 8 - 1, 0))
        return pl.BlockSpec(shape, lambda i, h: (0,) * len(shape))

    read = sum(a.size * a.dtype.itemsize for a, kind in operands if kind != "unread")
    return pl.pallas_call(
        kernel,
        grid_spec=pltpu.PrefetchScalarGridSpec(
            num_scalar_prefetch=1,
            grid=(1,),
            in_specs=[spec(a.shape, kind) for a, kind in operands],
            out_specs=[spec(shape, kind) for shape, dtype, kind in results],
        ),
        out_shape=[jax.ShapeDtypeStruct(shape, dtype) for shape, dtype, kind in results],
        input_output_aliases=aliases or {},
        compiler_params=pltpu.CompilerParams(vmem_limit_bytes=32 * 1024 * 1024),
        cost_estimate=pl.CostEstimate(flops=flops, bytes_accessed=read, transcendentals=0),
    )(half, *[a for a, kind in operands])


def local(queries, key_vectors, value_vectors, log_decay, restart, norm_gain, upstream):
    tokens, width = queries.shape[1], queries.shape[2]
    pairs = HEAD_TOTAL // 4
    state_rows = pairs * 64
    buffer_rows = state_rows + 8
    blocks = lax.axis_size("seq")
    scans = lax.axis_size("dp")
    position = lax.axis_index("seq")
    core = position & 1
    on_first = core == 0
    own = core.reshape(1).astype(jnp.int32)
    other = 1 - own
    half_width = width // 2

    def exchange(x, bit, axis="seq"):
        size = blocks if axis == "seq" else scans
        return lax.ppermute(x, axis, [(i, i ^ bit) for i in range(size)])

    def parts(buffer):
        state = buffer[:state_rows].reshape(pairs, 64, LANES)
        if buffer.shape[0] == state_rows:
            return state, None
        return state, buffer[state_rows : state_rows + pairs].reshape(pairs, 1, LANES)

    def joined(state, carry):
        return jnp.concatenate(
            [
                state.reshape(state_rows, LANES),
                carry.reshape(pairs, LANES),
                jnp.zeros((8 - pairs, LANES), F32),
            ],
            axis=0,
        )

    def flat(state):
        return state.reshape(state_rows, LANES)

    whole = (1, tokens, width)
    part = (tokens, half_width)
    buffer = (buffer_rows, LANES)

    state_other, tables = call(
        first_state_kernel,
        other,
        [
            (key_vectors, "columns"),
            (value_vectors, "columns"),
            (jnp.swapaxes(log_decay, 1, 2), "all"),
            (restart, "all"),
        ],
        [(buffer, F32, "all"), ((TABLE_ROWS, LANES), F32, "all")],
    )
    swapped = exchange(state_other, 1)
    (state_own,) = call(
        second_state_kernel,
        own,
        [(key_vectors, "columns"), (value_vectors, "columns"), (tables, "all")],
        [(buffer, F32, "all")],
    )
    first_state, first_carry = parts(jnp.where(on_first, state_own, swapped))
    second_state, second_carry = parts(jnp.where(on_first, swapped, state_own))
    total = second_carry * first_state + second_state
    carry = first_carry * second_carry
    prefix = jnp.zeros_like(total)
    prefix_carry = jnp.ones_like(carry)
    levels = []
    bit = 2
    while bit < blocks:
        is_upper = (position & bit) != 0
        theirs, their_carry = parts(exchange(joined(total, carry), 2 * bit - 2))
        prefix = jnp.where(is_upper, prefix_carry * theirs + prefix, prefix)
        prefix_carry = jnp.where(is_upper, prefix_carry * their_carry, prefix_carry)
        levels.append((bit, is_upper, carry, their_carry))
        total = jnp.where(is_upper, carry * theirs + total, their_carry * total + theirs)
        carry = carry * their_carry
        bit *= 2
    after_first = first_carry * prefix + first_state
    state_in_own = flat(jnp.where(on_first, prefix, after_first))
    state_in_other = exchange(flat(jnp.where(on_first, after_first, prefix)), 1)

    mixed = {}
    for name, half in (("own", own), ("other", other)):
        (mixed[name],) = call(
            mixture_kernel,
            half,
            [
                (queries, "columns"),
                (key_vectors, "columns"),
                (value_vectors, "columns"),
                (tables, "all"),
            ],
            [(part, F32, "all")],
            flops=1_000_000_000,
        )

    gain_rows = norm_gain.reshape(2 * pairs, LANES)
    layer_out = None
    results = {}
    before = jnp.zeros((8, LANES), F32)
    for name, half, state_in in (("own", own, state_in_own), ("other", other, state_in_other)):
        operands = [
            (mixed[name], "all"),
            (queries, "columns"),
            (upstream, "columns"),
            (gain_rows, "all"),
            (state_in, "all"),
            (tables, "all"),
            (before, "all" if name == "own" else "top"),
        ]
        if name == "own":
            kernel = lambda *refs: forward_kernel(*refs[:8], None, *refs[8:])
            aliases = None
        else:
            operands.append((layer_out, "unread"))
            kernel = forward_kernel
            aliases = {len(operands): 0}
        layer_out, grad_mixed, query_state = call(
            kernel,
            half,
            operands,
            [(whole, BF16, "columns"), (part, BF16, "all"), (buffer, F32, "all")],
            aliases,
        )
        before = query_state
        results[name] = (grad_mixed, query_state, state_in)

    query_state_own = results["own"][1]
    query_state_other = results["other"][1]
    swapped = exchange(query_state_other, 1)
    first_query, _ = parts(jnp.where(on_first, query_state_own, swapped))
    second_query, _ = parts(jnp.where(on_first, swapped, query_state_own))
    gain = query_state_other[state_rows:] + swapped[state_rows:]
    total = first_query + first_carry * second_query
    suffix = jnp.zeros_like(total)
    suffix_carry = jnp.ones_like(carry)
    for bit, is_upper, carry, their_carry in levels:
        partner = 2 * bit - 2
        if bit == 2:
            theirs = parts(exchange(flat(total), partner))[0]
            step = 1
            while step < scans:
                gain = gain + sum(
                    exchange(gain, k * step, "dp") for k in range(1, min(4, scans // step))
                )
                step *= 4
            if len(levels) == 1:
                gain = gain + exchange(gain, partner)
        else:
            received = exchange(jnp.concatenate([flat(total), gain], axis=0), partner)
            theirs = parts(received)[0]
            if 2 * bit == blocks:
                gain = gain + exchange(gain, 2) + exchange(gain, partner ^ 2)
            gain = gain + received[state_rows:]
        suffix = jnp.where(is_upper, suffix, suffix_carry * theirs + suffix)
        suffix_carry = jnp.where(is_upper, suffix_carry, suffix_carry * their_carry)
        total = jnp.where(is_upper, theirs + their_carry * total, total + carry * theirs)
    before_second = second_query + second_carry * suffix
    state_grad_own = flat(jnp.where(on_first, before_second, suffix))
    state_grad_other = exchange(flat(jnp.where(on_first, suffix, before_second)), 1)
    grad_query = None
    local_parts = {}
    for name, half in (("own", own), ("other", other)):
        grad_mixed, _, state_in = results[name]
        operands = [
            (queries, "columns"),
            (key_vectors, "columns"),
            (value_vectors, "columns"),
            (grad_mixed, "all"),
            (state_in, "all"),
            (tables, "all"),
        ]
        if name == "own":
            kernel = lambda *refs: backward_kernel(*refs[:7], None, *refs[7:])
            aliases = None
        else:
            operands.append((grad_query, "unread"))
            kernel = backward_kernel
            aliases = {len(operands): 0}
        grad_query, *local_parts[name] = call(
            kernel,
            half,
            operands,
            [
                (whole, BF16, "columns"),
                (part, F32, "all"),
                (part, F32, "all"),
                ((HEAD_TOTAL // 2, LANES), F32, "all"),
            ],
            aliases,
            flops=2_000_000_000,
        )

    rows = jnp.zeros((HEAD_TOTAL // 2, LANES), F32)
    for name, half, state_grad in (
        ("own", own, state_grad_own),
        ("other", other, state_grad_other),
    ):
        grad_key_part, grad_value_part, later = local_parts[name]
        operands = [
            (key_vectors, "columns"),
            (value_vectors, "columns"),
            (grad_key_part, "all"),
            (grad_value_part, "all"),
            (later, "all"),
            (results[name][2], "all"),
            (state_grad, "all"),
            (tables, "all"),
            (rows, "all"),
        ]
        if name == "own":
            kernel = lambda *refs: final_kernel(*refs[:10], None, None, *refs[10:])
            aliases = None
        else:
            operands += [(grad_key, "unread"), (grad_value, "unread")]
            kernel = final_kernel
            aliases = {len(operands) - 1: 0, len(operands): 1}
        grad_key, grad_value, rows, grad_decay = call(
            kernel,
            half,
            operands,
            [
                (whole, BF16, "columns"),
                (whole, BF16, "columns"),
                ((HEAD_TOTAL // 2, LANES), F32, "all"),
                ((1, HEAD_TOTAL, tokens), F32, "all"),
            ],
            aliases,
        )
    grad_decay = jnp.swapaxes(grad_decay, 1, 2)
    return (layer_out, grad_query, grad_key, grad_value, grad_decay, gain.reshape(-1))


def solution(mesh):
    rows = P("dp", "seq", None)
    return jax.shard_map(
        local,
        mesh=mesh,
        in_specs=(rows, rows, rows, rows, P("dp", "seq"), P(), rows),
        out_specs=(rows, rows, rows, rows, rows, P()),
        check_vma=False,
    )
```

```python
import functools

import jax
import jax.numpy as jnp
from jax import lax
from jax.experimental import pallas as pl
from jax.experimental.pallas import tpu as pltpu
from jax.sharding import PartitionSpec as P

HEAD_TOTAL = 16
EPSILON = 1e-06
LANES = 128
PAIRS = HEAD_TOTAL // 4
VMEM_BYTES = 12 * 1024 * 1024
F32 = jnp.float32
BF16 = jnp.bfloat16
COLUMNS, MASK, CUM_ROWS, CARRY_ROWS, TABLE_ROWS = 0, 128, 256, 272, 288


def dot(a, b, contract_a=1, contract_b=0):
    return lax.dot_general(
        a, b, (((contract_a,), (contract_b,)), ((), ())), preferred_element_type=F32
    )


def halves(x):
    high = x.astype(BF16)
    return high, (x - high.astype(F32)).astype(BF16)


def stacked(x, axis):
    return jnp.concatenate(halves(x), axis=axis)


def twice(x, axis):
    return jnp.concatenate([x, x], axis=axis)


def left_lanes(shape):
    return lax.broadcasted_iota(jnp.int32, shape, 1) < LANES // 2


def triangle(tokens, keep):
    rows = lax.broadcasted_iota(jnp.int32, (tokens, tokens), 0)
    columns = lax.broadcasted_iota(jnp.int32, (tokens, tokens), 1)
    return keep(rows, columns)


def by_head(x, axis):
    left = left_lanes(x.shape)
    zero = jnp.zeros_like(x)
    return jnp.concatenate([jnp.where(left, x, zero), jnp.where(left, zero, x)], axis=axis)


def fold(x):
    rows = x.shape[0] // 2
    return jnp.where(left_lanes((rows, LANES)), x[:rows], x[rows:])


def pair_columns(table, first, tokens):
    return jnp.where(
        left_lanes((tokens, LANES)),
        jnp.broadcast_to(table[:, first : first + 1], (tokens, LANES)),
        jnp.broadcast_to(table[:, first + 1 : first + 2], (tokens, LANES)),
    )


def make_tables(decay_rows, restart):
    heads, tokens = decay_rows.shape
    lower = triangle(tokens, lambda t, s: s <= t).astype(F32).astype(BF16)
    upper = triangle(tokens, lambda t, s: t <= s).astype(F32).astype(BF16)
    marks = jnp.broadcast_to(restart.astype(F32), (tokens, tokens)).astype(BF16)
    resets_column = dot(lower, marks, 1, 1)
    resets_row = dot(marks, upper)
    cum_rows = row_sums(decay_rows, triangle(tokens, lambda s, t: s <= t))
    cum = jnp.transpose(
        jnp.concatenate([cum_rows, jnp.zeros((LANES - heads, tokens), F32)], axis=0)
    )
    last = cum[tokens - 1 :, :]
    last_reset = resets_column[tokens - 1 :, :]
    entry = jnp.where(resets_column == 0.0, jnp.exp(cum), 0.0)
    leave = jnp.where(resets_column == last_reset, jnp.exp(last - cum), 0.0)
    lane = lax.broadcasted_iota(jnp.int32, (tokens, LANES), 1)
    columns = jnp.where(
        lane < heads,
        cum,
        jnp.where(lane < 2 * heads, pltpu.roll(entry, heads, 1), pltpu.roll(leave, 2 * heads, 1)),
    )
    allowed = triangle(tokens, lambda t, s: t >= s) & (resets_column == resets_row)
    mask = jnp.where(allowed, 0.0, -1e30)
    carry = jnp.where(last_reset[:, :1] == 0.0, jnp.exp(cum_rows[:, tokens - 1 :]), 0.0)
    return columns, mask, cum_rows, jnp.broadcast_to(carry, (heads, LANES))


def pick_columns(columns, half):
    return jnp.where(half == 0, columns, pltpu.roll(columns, LANES - HEAD_TOTAL // 2, 1))


def pick_rows(rows, half):
    count = HEAD_TOTAL // 2
    return jnp.where(half == 0, rows[:count], rows[count:])


def own_half(mine):
    core = lax.axis_index("seq") & 1
    return core if mine else 1 - core


def half_lanes(half, width):
    return pl.ds(pl.multiple_of(half * (width // 2), LANES), width // 2)


def pair_lanes(half, width, pair):
    return pl.ds(pl.multiple_of(half * (width // 2) + pair * LANES, LANES), LANES)


def write_states(half, columns, carry_rows, keys, values, out_ref):
    tokens = keys.shape[0]
    table = pick_columns(columns, half)
    carry = pick_rows(carry_rows, half)
    left = left_lanes((1, LANES))
    scaled = []
    for pair in range(PAIRS):
        leave = pair_columns(table, 2 * HEAD_TOTAL + 2 * pair, tokens)
        lanes = slice(pair * LANES, (pair + 1) * LANES)
        scaled.append(stacked(values[:, lanes].astype(F32) * leave, 1))
    states = []
    for pair in range(PAIRS):
        lanes = slice(pair * LANES, (pair + 1) * LANES)
        states.append(dot(keys[:, lanes], scaled[pair], 0, 0))
    rows = []
    for pair in range(PAIRS):
        out_ref[pl.ds(pair * 64, 64), :] = fold(states[pair][:, :LANES] + states[pair][:, LANES:])
        rows.append(jnp.where(left, carry[2 * pair : 2 * pair + 1], carry[2 * pair + 1 : 2 * pair + 2]))
    rows.append(jnp.zeros((8 - len(rows), LANES), F32))
    out_ref[pl.ds(PAIRS * 64, 8), :] = jnp.concatenate(rows, axis=0)


def first_state_kernel(
    key_ref,
    value_ref,
    decay_ref,
    restart_ref,
    out_ref,
    table_ref,
    keys,
    values,
    decays,
    restarts,
    arrived,
):
    half = own_half(False)
    lanes = half_lanes(half, key_ref.shape[2])
    decay_copy = pltpu.make_async_copy(decay_ref.at[0], decays, arrived.at[2])
    restart_copy = pltpu.make_async_copy(restart_ref, restarts, arrived.at[3])
    value_copy = pltpu.make_async_copy(value_ref.at[0, :, lanes], values, arrived.at[1])
    key_copy = pltpu.make_async_copy(key_ref.at[0, :, lanes], keys, arrived.at[0])
    decay_copy.start()
    restart_copy.start()
    value_copy.start()
    key_copy.start()
    decay_copy.wait()
    restart_copy.wait()
    columns, mask, cum_rows, carry_rows = make_tables(decays[...], restarts[...])
    table_ref[pl.ds(COLUMNS, 128), :] = columns
    table_ref[pl.ds(MASK, 128), :] = mask
    table_ref[pl.ds(CUM_ROWS, 16), :] = cum_rows
    table_ref[pl.ds(CARRY_ROWS, 16), :] = carry_rows
    value_copy.wait()
    key_copy.wait()
    write_states(half, columns, carry_rows, keys[...], values[...], out_ref)


def second_state_kernel(key_ref, value_ref, table_ref, out_ref):
    half = own_half(True)
    lanes = half_lanes(half, key_ref.shape[2])
    write_states(
        half,
        table_ref[pl.ds(COLUMNS, 128), :],
        table_ref[pl.ds(CARRY_ROWS, 16), :],
        key_ref[0, :, lanes],
        value_ref[0, :, lanes],
        out_ref,
    )


def pair_decays(table, cum_rows, mask, pair, tokens):
    parts = []
    for head in (2 * pair, 2 * pair + 1):
        column = jnp.broadcast_to(table[:, head : head + 1], (tokens, tokens))
        parts.append(jnp.exp(column - cum_rows[head : head + 1] + mask))
    return jnp.concatenate(parts, axis=0)


def side_by_side(x):
    rows = x.shape[0] // 2
    return jnp.concatenate([x[:rows], x[rows:]], axis=1)


def pick_gains(gain_ref, half):
    return jnp.where(half == 0, gain_ref[:PAIRS, :], gain_ref[PAIRS:, :])


def mixture_kernel(
    mine,
    query_ref,
    key_ref,
    value_ref,
    upstream_ref,
    gain_ref,
    table_ref,
    out_ref,
    turned_ref,
    entry_ref,
    grad_ref,
):
    tokens, width = query_ref.shape[1:]
    half = own_half(mine)
    table = pick_columns(table_ref[pl.ds(COLUMNS, 128), :], half)
    cum_rows = pick_rows(table_ref[pl.ds(CUM_ROWS, 16), :], half)
    mask = table_ref[pl.ds(MASK, 128), :]
    gains = pick_gains(gain_ref, half)
    for pair in range(PAIRS):
        lanes = pair_lanes(half, width, pair)
        query = query_ref[0, :, lanes]
        decay = pair_decays(table, cum_rows, mask, pair, tokens)
        scores = dot(by_head(query, 0), key_ref[0, :, lanes], 1, 1) * decay
        weights = scores.astype(BF16)
        here = pl.ds(pair * LANES, LANES)
        grad_ref[:, here] = upstream_ref[0, :, lanes].astype(F32) * gains[pair : pair + 1]
        out_ref[:, here] = dot(side_by_side(weights), by_head(value_ref[0, :, lanes], 0))
        turned_ref[here, :] = jnp.transpose(query)
        entry_ref[:, here] = pair_columns(table, HEAD_TOTAL + 2 * pair, tokens)


def forward_kernel(
    mine,
    mixed_ref,
    turned_ref,
    entry_ref,
    grad_ref,
    query_ref,
    upstream_ref,
    gain_ref,
    state_ref,
    before_ref,
    layer_ref,
    grad_mixed_ref,
    out_ref,
):
    tokens, width = query_ref.shape[1:]
    half = own_half(mine)
    gains = pick_gains(gain_ref, half)
    own = left_lanes((LANES, LANES)) == (lax.broadcasted_iota(jnp.int32, (LANES, LANES), 0) < 64)
    average = twice(jnp.where(own, 1.0 / 64.0, 0.0).astype(BF16), 0)
    places = [pl.ds(pair * LANES, LANES) for pair in range(PAIRS)]
    lanes = [pair_lanes(half, width, pair) for pair in range(PAIRS)]
    states = [
        stacked(by_head(state_ref[pl.ds(pair * 64, 64), :], 0), 0) for pair in range(PAIRS)
    ]
    carried = [
        dot(twice(query_ref[0, :, lanes[pair]], 1), states[pair]) for pair in range(PAIRS)
    ]
    mixtures = [
        mixed_ref[:, places[pair]] + entry_ref[:, places[pair]] * carried[pair]
        for pair in range(PAIRS)
    ]
    squares = dot(
        jnp.concatenate([stacked(mixture * mixture, 1) for mixture in mixtures], axis=0), average
    )
    normeds, inverses, grads, products, gain_parts = [], [], [], [], []
    for pair in range(PAIRS):
        inverse = lax.rsqrt(squares[pair * tokens : (pair + 1) * tokens] + EPSILON)
        normed = mixtures[pair] * inverse
        gain = gains[pair : pair + 1]
        upstream = upstream_ref[0, :, lanes[pair]].astype(F32)
        grad_normed = grad_ref[:, places[pair]]
        products.append(stacked(grad_normed * normed, 1))
        layer_ref[:, places[pair]] = (normed * gain).astype(BF16)
        gain_parts.append(jnp.sum(upstream * normed, axis=0, keepdims=True))
        normeds.append(normed)
        inverses.append(inverse)
        grads.append(grad_normed)
    shared = dot(jnp.concatenate(products, axis=0), average)
    sides = []
    for pair in range(PAIRS):
        part = shared[pair * tokens : (pair + 1) * tokens]
        grad_mixed = (inverses[pair] * (grads[pair] - normeds[pair] * part)).astype(BF16)
        grad_mixed_ref[:, places[pair]] = grad_mixed
        sides.append(stacked(entry_ref[:, places[pair]] * grad_mixed.astype(F32), 1))
    for pair in range(PAIRS):
        both = dot(turned_ref[places[pair], :], sides[pair])
        out_ref[pl.ds(pair * 64, 64), :] = fold(both[:, :LANES] + both[:, LANES:])
    part = jnp.concatenate(gain_parts, axis=0)
    blank = jnp.zeros_like(part)
    part = jnp.where(
        half == 0,
        jnp.concatenate([part, blank], axis=0),
        jnp.concatenate([blank, part], axis=0),
    )
    if before_ref is not None:
        part = part + before_ref[pl.ds(PAIRS * 64, 8), :]
    out_ref[pl.ds(PAIRS * 64, 8), :] = part


def backward_kernel(
    mine,
    query_ref,
    key_ref,
    value_ref,
    grad_mixed_ref,
    state_ref,
    entry_ref,
    table_ref,
    layer_part_ref,
    layer_ref,
    grad_query_ref,
    grad_key_ref,
    grad_value_ref,
    later_ref,
    leave_ref,
    grad_query_part,
    sent,
):
    tokens, width = query_ref.shape[1:]
    half = own_half(mine)
    copies = [
        pltpu.make_async_copy(
            layer_part_ref, layer_ref.at[0, :, half_lanes(half, width)], sent.at[0]
        )
    ]
    copies[0].start()
    table = pick_columns(table_ref[pl.ds(COLUMNS, 128), :], half)
    cum_rows = pick_rows(table_ref[pl.ds(CUM_ROWS, 16), :], half)
    mask = table_ref[pl.ds(MASK, 128), :]
    earlier = twice(triangle(tokens, lambda s, t: s < t).astype(F32).astype(BF16), 0)
    reached = triangle(tokens, lambda u, t: u >= t)
    chooser = twice(head_chooser(), 1)
    balance_rows = []
    entry_rows = []
    for pair in range(PAIRS):
        lanes = pair_lanes(half, width, pair)
        here = pl.ds(pair * LANES, LANES)
        query = query_ref[0, :, lanes]
        key = key_ref[0, :, lanes]
        value = value_ref[0, :, lanes]
        grad_mixed = grad_mixed_ref[:, here]
        query_rows = by_head(query, 0)
        mixed_rows = by_head(grad_mixed, 0)
        decay = pair_decays(table, cum_rows, mask, pair, tokens)
        decayed_scores = dot(query_rows, key, 1, 1) * decay
        grad_pairs = dot(mixed_rows, value, 1, 1)
        weights = decayed_scores.astype(BF16)
        grad_weights = (grad_pairs * decay).astype(BF16)
        state = by_head(state_ref[pl.ds(pair * 64, 64), :], 0)
        carried = entry_ref[:, here] * dot(twice(grad_mixed, 1), stacked(state, 1), 1, 1)
        grad_query_part[:, here] = (
            dot(side_by_side(grad_weights), by_head(key, 0)) + carried
        ).astype(BF16)
        copies.append(
            pltpu.make_async_copy(
                grad_query_part.at[:, here], grad_query_ref.at[0, :, lanes], sent.at[1 + pair]
            )
        )
        copies[-1].start()
        grad_key_ref[:, here] = dot(grad_weights, query_rows, 0, 0)
        grad_value_ref[:, here] = dot(weights, mixed_rows, 0, 0)
        leave_ref[:, here] = pair_columns(table, 2 * HEAD_TOTAL + 2 * pair, tokens)
        before = dot(stacked(decayed_scores * grad_pairs, 1), earlier)
        for head in range(2):
            part = before[head * tokens : (head + 1) * tokens]
            balance_rows.append(jnp.sum(jnp.where(reached, part, 0.0), axis=0, keepdims=True))
        terms = dot(chooser, stacked(query.astype(F32) * carried, 1), 1, 1)
        entry_rows.append(terms[:2])
    later_ref[...] = jnp.concatenate(balance_rows, axis=0) + row_sums(
        jnp.concatenate(entry_rows, axis=0), reached
    )
    for copy in copies:
        copy.wait()


def head_chooser():
    rows = lax.broadcasted_iota(jnp.int32, (8, LANES), 0)
    left = left_lanes((8, LANES))
    chosen = ((rows == 0) & left) | ((rows == 1) & ~left)
    return jnp.where(chosen, 1.0, 0.0).astype(BF16)


def row_sums(rows, keep):
    first, second = halves(rows)
    third = (rows - first.astype(F32) - second.astype(F32)).astype(BF16)
    weight = jnp.where(keep, 1.0, 0.0).astype(BF16)
    return dot(
        jnp.concatenate([first, second, third], axis=1),
        jnp.concatenate([weight, weight, weight], axis=0),
    )


def final_kernel(
    mine,
    key_ref,
    value_ref,
    grad_key_part_ref,
    grad_value_part_ref,
    later_ref,
    leave_ref,
    state_ref,
    grad_ref,
    table_ref,
    other_ref,
    gain_refs,
    grad_key_ref,
    grad_value_ref,
    rows_ref,
    decay_ref,
    gain_ref,
    key_out,
    value_out,
    decay_out,
    gain_out,
    sent,
):
    tokens, width = key_ref.shape[1:]
    half = own_half(mine)
    copies = []

    def send(source, target):
        copies.append(pltpu.make_async_copy(source, target, sent.at[len(copies)]))
        copies[-1].start()

    if gain_refs:
        gain_out[...] = sum(ref[...] for ref in gain_refs[1:]) + gain_refs[0][...]
        send(gain_out, gain_ref)
    carry = pick_rows(table_ref[pl.ds(CARRY_ROWS, 16), :], half)
    chooser = twice(head_chooser(), 1)
    left = left_lanes((1, LANES))
    lanes = [pair_lanes(half, width, pair) for pair in range(PAIRS)]
    places = [pl.ds(pair * LANES, LANES) for pair in range(PAIRS)]
    grads = [halves(by_head(grad_ref[pl.ds(pair * 64, 64), :], 0)) for pair in range(PAIRS)]
    carried, terms = [], []
    for pair in range(PAIRS):
        carried.append(
            leave_ref[:, places[pair]]
            * dot(twice(key_ref[0, :, lanes[pair]], 1), jnp.concatenate(grads[pair], axis=0))
        )
    for pair in range(PAIRS):
        value_out[:, places[pair]] = (
            grad_value_part_ref[:, places[pair]] + carried[pair]
        ).astype(BF16)
        terms.append(stacked(carried[pair] * value_ref[0, :, lanes[pair]].astype(F32), 1))
    send(value_out, grad_value_ref.at[0, :, half_lanes(half, width)])
    key_parts = [
        dot(twice(value_ref[0, :, lanes[pair]], 1), jnp.concatenate(grads[pair], axis=1), 1, 1)
        for pair in range(PAIRS)
    ]
    earlier = [dot(chooser, terms[pair], 1, 1)[:2] for pair in range(PAIRS)]
    for pair in range(PAIRS):
        key_out[:, places[pair]] = (
            grad_key_part_ref[:, places[pair]] + leave_ref[:, places[pair]] * key_parts[pair]
        ).astype(BF16)
    send(key_out, grad_key_ref.at[0, :, half_lanes(half, width)])
    through_rows = []
    for pair in range(PAIRS):
        block = pl.ds(pair * 64, 64)
        product = jnp.sum(grad_ref[block, :] * state_ref[block, :], axis=0, keepdims=True)
        for side in (left, ~left):
            through_rows.append(jnp.sum(jnp.where(side, product, 0.0), axis=1, keepdims=True))
    rows = (
        later_ref[...]
        + row_sums(jnp.concatenate(earlier, axis=0), triangle(tokens, lambda u, t: u < t))
        + carry * jnp.concatenate(through_rows, axis=0)
    )
    if rows_ref is not None:
        rows_ref[...] = rows
    else:
        other = other_ref[...]
        decay_out[...] = jnp.where(
            half == 0,
            jnp.concatenate([rows, other], axis=0),
            jnp.concatenate([other, rows], axis=0),
        )
        send(decay_out, decay_ref.at[0])
    for copy in copies:
        copy.wait()


VMEM, HBM = pltpu.VMEM, pltpu.HBM


def call(kernel, operands, results, scratch=(), aliases=None, flops=0, constrain=False):
    read = sum(a.size * a.dtype.itemsize for a, memory in operands if memory is VMEM)
    return pl.pallas_call(
        kernel,
        in_specs=[pl.BlockSpec(memory_space=memory) for a, memory in operands],
        out_specs=[pl.BlockSpec(memory_space=memory) for shape, dtype, memory in results],
        out_shape=[jax.ShapeDtypeStruct(shape, dtype) for shape, dtype, memory in results],
        scratch_shapes=list(scratch),
        input_output_aliases=aliases or {},
        compiler_params=pltpu.CompilerParams(vmem_limit_bytes=VMEM_BYTES),
        cost_estimate=pl.CostEstimate(flops=flops, bytes_accessed=read, transcendentals=0),
    )(
        *[
            pltpu.with_memory_space_constraint(a, HBM) if memory is HBM and constrain else a
            for a, memory in operands
        ]
    )


def local(queries, key_vectors, value_vectors, log_decay, restart, norm_gain, upstream):
    tokens, width = queries.shape[1], queries.shape[2]
    state_rows = PAIRS * 64
    buffer_rows = state_rows + 8
    blocks = lax.axis_size("seq")
    scans = lax.axis_size("dp")
    position = lax.axis_index("seq")
    on_first = (position & 1) == 0

    def exchange(x, bit, axis="seq"):
        size = blocks if axis == "seq" else scans
        return lax.ppermute(x, axis, [(i, i ^ bit) for i in range(size)])

    def parts(buffer):
        state = buffer[:state_rows].reshape(PAIRS, 64, LANES)
        if buffer.shape[0] == state_rows:
            return state, None
        return state, buffer[state_rows : state_rows + PAIRS].reshape(PAIRS, 1, LANES)

    def joined(state, carry):
        return jnp.concatenate(
            [
                state.reshape(state_rows, LANES),
                carry.reshape(PAIRS, LANES),
                jnp.zeros((8 - PAIRS, LANES), F32),
            ],
            axis=0,
        )

    def flat(state):
        return state.reshape(state_rows, LANES)

    whole = (1, tokens, width)
    part = (tokens, width // 2)
    buffer = (buffer_rows, LANES)
    rows = (HEAD_TOTAL // 2, LANES)
    blocks_of = [(queries, VMEM), (key_vectors, VMEM), (value_vectors, VMEM)]

    gain_rows = norm_gain.reshape(2 * PAIRS, LANES)

    state_other, tables = call(
        first_state_kernel,
        [
            (key_vectors, HBM),
            (value_vectors, HBM),
            (jnp.swapaxes(log_decay, 1, 2), HBM),
            (restart, HBM),
        ],
        [(buffer, F32, VMEM), ((TABLE_ROWS, LANES), F32, VMEM)],
        [
            pltpu.VMEM(part, BF16),
            pltpu.VMEM(part, BF16),
            pltpu.VMEM((HEAD_TOTAL, tokens), F32),
            pltpu.VMEM((1, tokens), jnp.int32),
            pltpu.SemaphoreType.DMA((4,)),
        ],
        constrain=True,
    )
    swapped = exchange(state_other, 1)
    (state_own,) = call(
        second_state_kernel,
        [(key_vectors, VMEM), (value_vectors, VMEM), (tables, VMEM)],
        [(buffer, F32, VMEM)],
    )
    first_state, first_carry = parts(jnp.where(on_first, state_own, swapped))
    second_state, second_carry = parts(jnp.where(on_first, swapped, state_own))
    total = second_carry * first_state + second_state
    carry = first_carry * second_carry
    prefix = jnp.zeros_like(total)
    prefix_carry = jnp.ones_like(carry)

    def mixture(mine, tables):
        return call(
            functools.partial(mixture_kernel, mine),
            blocks_of + [(upstream, VMEM), (gain_rows, VMEM), (tables, VMEM)],
            [
                (part, F32, VMEM),
                ((width // 2, LANES), BF16, VMEM),
                (part, F32, VMEM),
                (part, F32, VMEM),
            ],
            flops=0,
        )

    mixed = {}
    levels = []
    bit = 2
    while bit < blocks:
        is_upper = (position & bit) != 0
        sent = joined(total, carry)
        mine = not mixed
        if len(mixed) < 2:
            sent, tables = lax.optimization_barrier((sent, tables))
            mixed[mine] = mixture(mine, tables)
        received = exchange(sent, 2 * bit - 2)
        if len(levels) < 2:
            received, mixed[mine] = lax.optimization_barrier((received, mixed[mine]))
        theirs, their_carry = parts(received)
        prefix = jnp.where(is_upper, prefix_carry * theirs + prefix, prefix)
        prefix_carry = jnp.where(is_upper, prefix_carry * their_carry, prefix_carry)
        levels.append((bit, is_upper, carry, their_carry))
        total = jnp.where(is_upper, carry * theirs + total, their_carry * total + theirs)
        carry = carry * their_carry
        bit *= 2
    for mine in (True, False):
        if mine not in mixed:
            mixed[mine] = mixture(mine, tables)
    after_first = first_carry * prefix + first_state
    state_in = {True: flat(jnp.where(on_first, prefix, after_first))}
    state_in[False] = exchange(flat(jnp.where(on_first, after_first, prefix)), 1)

    layer_parts, grad_mixed, query_states = {}, {}, {}
    for mine in (True, False):
        operands = [
            *[(x, VMEM) for x in mixed[mine][:4]],
            (queries, VMEM),
            (upstream, VMEM),
            (gain_rows, VMEM),
            (state_in[mine], VMEM),
        ]
        if mine:
            kernel = lambda *refs: forward_kernel(True, *refs[:8], None, *refs[8:])
        else:
            operands.append((query_states[True], VMEM))
            kernel = functools.partial(forward_kernel, False)
        layer_parts[mine], grad_mixed[mine], query_states[mine] = call(
            kernel, operands, [(part, BF16, VMEM), (part, BF16, VMEM), (buffer, F32, VMEM)]
        )

    outputs = {}

    def backward(mine, state):
        operands = blocks_of + [
            (grad_mixed[mine], VMEM),
            (state, VMEM),
            (mixed[mine][2], VMEM),
            (tables, VMEM),
            (layer_parts[mine], VMEM),
        ]
        aliases = {}
        kernel = functools.partial(backward_kernel, mine)
        if outputs:
            kernel = lambda *refs: backward_kernel(mine, *refs[:8], *refs[10:])
            operands += [(outputs["layer"], HBM), (outputs["query"], HBM)]
            aliases = {8: 0, 9: 1}
        outputs["layer"], outputs["query"], *local_parts = call(
            kernel,
            operands,
            [
                (whole, BF16, HBM),
                (whole, BF16, HBM),
                (part, F32, VMEM),
                (part, F32, VMEM),
                (rows, F32, VMEM),
                (part, F32, VMEM),
            ],
            [pltpu.VMEM(part, BF16), pltpu.SemaphoreType.DMA((1 + PAIRS,))],
            aliases,
            flops=0,
        )
        return local_parts

    swapped = exchange(query_states[False], 1)
    first_query, _ = parts(jnp.where(on_first, query_states[True], swapped))
    second_query, _ = parts(jnp.where(on_first, swapped, query_states[True]))
    total = flat(first_query + first_carry * second_query)
    suffix = jnp.zeros_like(first_query)
    suffix_carry = jnp.ones_like(carry)
    gain = query_states[False][state_rows:] + swapped[state_rows:]
    local_parts = {}
    gains = [gain]
    for bit, is_upper, carry, their_carry in levels:
        partner = 2 * bit - 2
        mine = not local_parts
        beside = len(local_parts) < 2
        gain = sum(gains)
        state = state_in[mine]
        total, gain, state = lax.optimization_barrier((total, gain, state))
        if bit == 2:
            received = exchange(total, partner)
            gains = [gain]
            for k in range(1, min(4, scans)):
                gains.append(exchange(gain, k, "dp"))
            step = 4
            while step < scans:
                gain = sum(gains)
                gains = [gain] + [
                    exchange(gain, k * step, "dp") for k in range(1, min(4, scans // step))
                ]
                step *= 4
            if len(levels) == 1:
                gain = sum(gains)
                gains = [gain, exchange(gain, partner)]
        else:
            received = exchange(jnp.concatenate([total, gain], axis=0), partner)
            gains = [gain]
            if 2 * bit == blocks:
                gains += [exchange(gain, 2), exchange(gain, partner ^ 2)]
        if beside:
            local_parts[mine] = backward(mine, state)
            received, gains, local_parts[mine] = lax.optimization_barrier(
                (received, gains, local_parts[mine])
            )
        if bit > 2:
            gains.append(received[state_rows:])
        theirs, _ = parts(received)
        total = parts(total)[0]
        suffix = jnp.where(is_upper, suffix, suffix_carry * theirs + suffix)
        suffix_carry = jnp.where(is_upper, suffix_carry, suffix_carry * their_carry)
        total = flat(jnp.where(is_upper, theirs + their_carry * total, total + carry * theirs))
    for mine in (True, False):
        if mine not in local_parts:
            local_parts[mine] = backward(mine, state_in[mine])
    before_second = second_query + second_carry * suffix
    state_grad = {True: flat(jnp.where(on_first, before_second, suffix))}
    state_grad[False] = exchange(flat(jnp.where(on_first, suffix, before_second)), 1)

    for mine in (True, False):
        grad_key_part, grad_value_part, later, leave = local_parts[mine]
        operands = [
            (key_vectors, VMEM),
            (value_vectors, VMEM),
            (grad_key_part, VMEM),
            (grad_value_part, VMEM),
            (later, VMEM),
            (leave, VMEM),
            (state_in[mine], VMEM),
            (state_grad[mine], VMEM),
            (tables, VMEM),
        ]
        results = [(whole, BF16, HBM), (whole, BF16, HBM)]
        scratch = [pltpu.VMEM(part, BF16), pltpu.VMEM(part, BF16)]
        if mine:
            kernel = lambda *refs: final_kernel(
                True, *refs[:9], None, [], *refs[9:12], None, None, *refs[12:14], None, None, refs[14]
            )
            aliases = None
            results.append((rows, F32, VMEM))
        else:
            count = len(gains)
            operands.append((decay_rows, VMEM))
            operands += [(x, VMEM) for x in gains]
            operands += [(grad_key, HBM), (grad_value, HBM)]
            kernel = lambda *refs: final_kernel(
                False,
                *refs[:10],
                refs[10 : 10 + count],
                *refs[12 + count : 14 + count],
                None,
                *refs[14 + count :],
            )
            aliases = {10 + count: 0, 11 + count: 1}
            results += [((1, HEAD_TOTAL, tokens), F32, HBM), ((2 * PAIRS, LANES), F32, HBM)]
            scratch += [pltpu.VMEM((HEAD_TOTAL, tokens), F32), pltpu.VMEM((2 * PAIRS, LANES), F32)]
        scratch.append(pltpu.SemaphoreType.DMA((4,)))
        grad_key, grad_value, *rest = call(kernel, operands, results, scratch, aliases)
        if mine:
            (decay_rows,) = rest
        else:
            grad_decay, grad_gain = rest
    grad_decay = jnp.swapaxes(grad_decay, 1, 2)
    return (
        outputs["layer"],
        outputs["query"],
        grad_key,
        grad_value,
        grad_decay,
        grad_gain.reshape(-1),
    )


def solution(mesh):
    rows = P("dp", "seq", None)
    return jax.shard_map(
        local,
        mesh=mesh,
        in_specs=(rows, rows, rows, rows, P("dp", "seq"), P(), rows),
        out_specs=(rows, rows, rows, rows, rows, P()),
        check_vma=False,
    )
```

```python
import functools

import jax
import jax.numpy as jnp
from jax import lax
from jax.experimental import pallas as pl
from jax.experimental.pallas import tpu as pltpu
from jax.sharding import PartitionSpec as P

HEAD_TOTAL = 16
EPSILON = 1e-06
LANES = 128
PAIRS = HEAD_TOTAL // 4
VMEM_BYTES = 12 * 1024 * 1024
F32 = jnp.float32
BF16 = jnp.bfloat16
COLUMNS, MASK, CUM_ROWS, CARRY_ROWS, TABLE_ROWS = 0, 128, 256, 272, 288


def dot(a, b, contract_a=1, contract_b=0):
    return lax.dot_general(
        a, b, (((contract_a,), (contract_b,)), ((), ())), preferred_element_type=F32
    )


def halves(x):
    high = x.astype(BF16)
    return high, (x - high.astype(F32)).astype(BF16)


def stacked(x, axis):
    return jnp.concatenate(halves(x), axis=axis)


def twice(x, axis):
    return jnp.concatenate([x, x], axis=axis)


def left_lanes(shape):
    return lax.broadcasted_iota(jnp.int32, shape, 1) < LANES // 2


def triangle(tokens, keep):
    rows = lax.broadcasted_iota(jnp.int32, (tokens, tokens), 0)
    columns = lax.broadcasted_iota(jnp.int32, (tokens, tokens), 1)
    return keep(rows, columns)


def by_head(x, axis):
    left = left_lanes(x.shape)
    zero = jnp.zeros_like(x)
    return jnp.concatenate([jnp.where(left, x, zero), jnp.where(left, zero, x)], axis=axis)


def fold(x):
    rows = x.shape[0] // 2
    return jnp.where(left_lanes((rows, LANES)), x[:rows], x[rows:])


def pair_columns(table, first, tokens):
    return jnp.where(
        left_lanes((tokens, LANES)),
        jnp.broadcast_to(table[:, first : first + 1], (tokens, LANES)),
        jnp.broadcast_to(table[:, first + 1 : first + 2], (tokens, LANES)),
    )


def make_tables(decay_rows, restart):
    heads, tokens = decay_rows.shape
    lower = triangle(tokens, lambda t, s: s <= t).astype(F32).astype(BF16)
    upper = triangle(tokens, lambda t, s: t <= s).astype(F32).astype(BF16)
    marks = jnp.broadcast_to(restart.astype(F32), (tokens, tokens)).astype(BF16)
    resets_column = dot(lower, marks, 1, 1)
    resets_row = dot(marks, upper)
    cum_rows = row_sums(decay_rows, triangle(tokens, lambda s, t: s <= t))
    cum = jnp.transpose(
        jnp.concatenate([cum_rows, jnp.zeros((LANES - heads, tokens), F32)], axis=0)
    )
    last = cum[tokens - 1 :, :]
    last_reset = resets_column[tokens - 1 :, :]
    entry = jnp.where(resets_column == 0.0, jnp.exp(cum), 0.0)
    leave = jnp.where(resets_column == last_reset, jnp.exp(last - cum), 0.0)
    lane = lax.broadcasted_iota(jnp.int32, (tokens, LANES), 1)
    columns = jnp.where(
        lane < heads,
        cum,
        jnp.where(lane < 2 * heads, pltpu.roll(entry, heads, 1), pltpu.roll(leave, 2 * heads, 1)),
    )
    allowed = triangle(tokens, lambda t, s: t >= s) & (resets_column == resets_row)
    mask = jnp.where(allowed, 0.0, -1e30)
    carry = jnp.where(last_reset[:, :1] == 0.0, jnp.exp(cum_rows[:, tokens - 1 :]), 0.0)
    return columns, mask, cum_rows, jnp.broadcast_to(carry, (heads, LANES))


def pick_columns(columns, half):
    return jnp.where(half == 0, columns, pltpu.roll(columns, LANES - HEAD_TOTAL // 2, 1))


def pick_rows(rows, half):
    count = HEAD_TOTAL // 2
    return jnp.where(half == 0, rows[:count], rows[count:])


def own_half(mine):
    core = lax.axis_index("seq") & 1
    return core if mine else 1 - core


def half_lanes(half, width):
    return pl.ds(pl.multiple_of(half * (width // 2), LANES), width // 2)


def pair_lanes(half, width, pair):
    return pl.ds(pl.multiple_of(half * (width // 2) + pair * LANES, LANES), LANES)


def write_states(half, columns, carry_rows, keys, values, out_ref):
    tokens = keys.shape[0]
    table = pick_columns(columns, half)
    carry = pick_rows(carry_rows, half)
    left = left_lanes((1, LANES))
    scaled = []
    for pair in range(PAIRS):
        leave = pair_columns(table, 2 * HEAD_TOTAL + 2 * pair, tokens)
        lanes = slice(pair * LANES, (pair + 1) * LANES)
        scaled.append(stacked(values[:, lanes].astype(F32) * leave, 1))
    states = []
    for pair in range(PAIRS):
        lanes = slice(pair * LANES, (pair + 1) * LANES)
        states.append(dot(keys[:, lanes], scaled[pair], 0, 0))
    rows = []
    for pair in range(PAIRS):
        out_ref[pl.ds(pair * 64, 64), :] = fold(states[pair][:, :LANES] + states[pair][:, LANES:])
        rows.append(jnp.where(left, carry[2 * pair : 2 * pair + 1], carry[2 * pair + 1 : 2 * pair + 2]))
    rows.append(jnp.zeros((8 - len(rows), LANES), F32))
    out_ref[pl.ds(PAIRS * 64, 8), :] = jnp.concatenate(rows, axis=0)


def first_state_kernel(
    key_ref,
    value_ref,
    decay_ref,
    restart_ref,
    out_ref,
    table_ref,
    keys,
    values,
    decays,
    restarts,
    arrived,
):
    half = own_half(False)
    lanes = half_lanes(half, key_ref.shape[2])
    decay_copy = pltpu.make_async_copy(decay_ref.at[0], decays, arrived.at[2])
    restart_copy = pltpu.make_async_copy(restart_ref, restarts, arrived.at[3])
    value_copy = pltpu.make_async_copy(value_ref.at[0, :, lanes], values, arrived.at[1])
    key_copy = pltpu.make_async_copy(key_ref.at[0, :, lanes], keys, arrived.at[0])
    decay_copy.start()
    restart_copy.start()
    value_copy.start()
    key_copy.start()
    decay_copy.wait()
    restart_copy.wait()
    columns, mask, cum_rows, carry_rows = make_tables(decays[...], restarts[...])
    table_ref[pl.ds(COLUMNS, 128), :] = columns
    table_ref[pl.ds(MASK, 128), :] = mask
    table_ref[pl.ds(CUM_ROWS, 16), :] = cum_rows
    table_ref[pl.ds(CARRY_ROWS, 16), :] = carry_rows
    value_copy.wait()
    key_copy.wait()
    write_states(half, columns, carry_rows, keys[...], values[...], out_ref)


def second_state_kernel(key_ref, value_ref, table_ref, out_ref):
    half = own_half(True)
    lanes = half_lanes(half, key_ref.shape[2])
    write_states(
        half,
        table_ref[pl.ds(COLUMNS, 128), :],
        table_ref[pl.ds(CARRY_ROWS, 16), :],
        key_ref[0, :, lanes],
        value_ref[0, :, lanes],
        out_ref,
    )


def pair_decays(table, cum_rows, mask, pair, tokens):
    parts = []
    for head in (2 * pair, 2 * pair + 1):
        column = jnp.broadcast_to(table[:, head : head + 1], (tokens, tokens))
        parts.append(jnp.exp(column - cum_rows[head : head + 1] + mask))
    return jnp.concatenate(parts, axis=1)


def one_above_other(x):
    columns = x.shape[1] // 2
    return jnp.concatenate([x[:, :columns], x[:, columns:]], axis=0)


def pick_gains(gain_ref, half):
    return jnp.where(half == 0, gain_ref[:PAIRS, :], gain_ref[PAIRS:, :])


def mixture_kernel(
    mine,
    query_ref,
    key_ref,
    value_ref,
    upstream_ref,
    gain_ref,
    table_ref,
    out_ref,
    turned_ref,
    entry_ref,
    grad_ref,
):
    tokens, width = query_ref.shape[1:]
    half = own_half(mine)
    table = pick_columns(table_ref[pl.ds(COLUMNS, 128), :], half)
    cum_rows = pick_rows(table_ref[pl.ds(CUM_ROWS, 16), :], half)
    mask = table_ref[pl.ds(MASK, 128), :]
    gains = pick_gains(gain_ref, half)
    for pair in range(PAIRS):
        lanes = pair_lanes(half, width, pair)
        query = query_ref[0, :, lanes]
        decay = pair_decays(table, cum_rows, mask, pair, tokens)
        scores = dot(query, by_head(key_ref[0, :, lanes], 0), 1, 1) * decay
        weights = scores.astype(BF16)
        here = pl.ds(pair * LANES, LANES)
        grad_ref[:, here] = upstream_ref[0, :, lanes].astype(F32) * gains[pair : pair + 1]
        out_ref[:, here] = dot(weights, by_head(value_ref[0, :, lanes], 0))
        turned_ref[here, :] = jnp.transpose(query)
        entry_ref[:, here] = pair_columns(table, HEAD_TOTAL + 2 * pair, tokens)


def forward_kernel(
    mine,
    mixed_ref,
    turned_ref,
    entry_ref,
    grad_ref,
    query_ref,
    upstream_ref,
    gain_ref,
    state_ref,
    before_ref,
    layer_ref,
    grad_mixed_ref,
    out_ref,
    gain_part_ref,
):
    tokens, width = query_ref.shape[1:]
    half = own_half(mine)
    gains = pick_gains(gain_ref, half)
    own = left_lanes((LANES, LANES)) == (lax.broadcasted_iota(jnp.int32, (LANES, LANES), 0) < 64)
    average = twice(jnp.where(own, 1.0 / 64.0, 0.0).astype(BF16), 0)
    places = [pl.ds(pair * LANES, LANES) for pair in range(PAIRS)]
    lanes = [pair_lanes(half, width, pair) for pair in range(PAIRS)]
    states = [
        stacked(by_head(state_ref[pl.ds(pair * 64, 64), :], 0), 0) for pair in range(PAIRS)
    ]
    carried = [
        dot(twice(query_ref[0, :, lanes[pair]], 1), states[pair]) for pair in range(PAIRS)
    ]
    mixtures = [
        mixed_ref[:, places[pair]] + entry_ref[:, places[pair]] * carried[pair]
        for pair in range(PAIRS)
    ]
    squares = dot(
        jnp.concatenate([stacked(mixture * mixture, 1) for mixture in mixtures], axis=0), average
    )
    normeds, inverses, grads, products, gain_parts = [], [], [], [], []
    for pair in range(PAIRS):
        inverse = lax.rsqrt(squares[pair * tokens : (pair + 1) * tokens] + EPSILON)
        normed = mixtures[pair] * inverse
        gain = gains[pair : pair + 1]
        upstream = upstream_ref[0, :, lanes[pair]].astype(F32)
        grad_normed = grad_ref[:, places[pair]]
        products.append(stacked(grad_normed * normed, 1))
        layer_ref[:, places[pair]] = (normed * gain).astype(BF16)
        gain_parts.append(jnp.sum(upstream * normed, axis=0, keepdims=True))
        normeds.append(normed)
        inverses.append(inverse)
        grads.append(grad_normed)
    shared = dot(jnp.concatenate(products, axis=0), average)
    sides = []
    for pair in range(PAIRS):
        part = shared[pair * tokens : (pair + 1) * tokens]
        grad_mixed = (inverses[pair] * (grads[pair] - normeds[pair] * part)).astype(BF16)
        grad_mixed_ref[:, places[pair]] = grad_mixed
        sides.append(stacked(entry_ref[:, places[pair]] * grad_mixed.astype(F32), 1))
    for pair in range(PAIRS):
        both = dot(turned_ref[places[pair], :], sides[pair])
        out_ref[pl.ds(pair * 64, 64), :] = fold(both[:, :LANES] + both[:, LANES:])
    part = jnp.concatenate(gain_parts, axis=0)
    blank = jnp.zeros_like(part)
    part = jnp.where(
        half == 0,
        jnp.concatenate([part, blank], axis=0),
        jnp.concatenate([blank, part], axis=0),
    )
    if before_ref is not None:
        part = part + before_ref[...]
    gain_part_ref[...] = part


def backward_kernel(
    mine,
    query_ref,
    key_ref,
    value_ref,
    grad_mixed_ref,
    state_ref,
    entry_ref,
    table_ref,
    grad_query_ref,
    grad_key_ref,
    grad_value_ref,
    later_ref,
    leave_ref,
):
    tokens, width = query_ref.shape[1:]
    half = own_half(mine)
    table = pick_columns(table_ref[pl.ds(COLUMNS, 128), :], half)
    cum_rows = pick_rows(table_ref[pl.ds(CUM_ROWS, 16), :], half)
    mask = table_ref[pl.ds(MASK, 128), :]
    earlier = twice(triangle(tokens, lambda s, t: s < t).astype(F32).astype(BF16), 0)
    reached = triangle(tokens, lambda u, t: u >= t)
    chooser = twice(head_chooser(), 1)
    places = [pl.ds(pair * LANES, LANES) for pair in range(PAIRS)]
    lanes = [pair_lanes(half, width, pair) for pair in range(PAIRS)]
    balance_rows, entry_rows, carried = [], [], []
    for pair in range(PAIRS):
        state = by_head(state_ref[pl.ds(pair * 64, 64), :], 0)
        grad_mixed = grad_mixed_ref[:, places[pair]]
        carried.append(
            entry_ref[:, places[pair]] * dot(twice(grad_mixed, 1), stacked(state, 1), 1, 1)
        )
        leave_ref[:, places[pair]] = pair_columns(table, 2 * HEAD_TOTAL + 2 * pair, tokens)
    for pair in range(PAIRS):
        query = query_ref[0, :, lanes[pair]]
        grad_mixed = grad_mixed_ref[:, places[pair]]
        key_rows = by_head(key_ref[0, :, lanes[pair]], 0)
        decay = pair_decays(table, cum_rows, mask, pair, tokens)
        decayed_scores = dot(query, key_rows, 1, 1) * decay
        grad_pairs = dot(grad_mixed, by_head(value_ref[0, :, lanes[pair]], 0), 1, 1)
        weights = decayed_scores.astype(BF16)
        grad_weights = (grad_pairs * decay).astype(BF16)
        grad_query_ref[:, places[pair]] = (dot(grad_weights, key_rows) + carried[pair]).astype(
            BF16
        )
        grad_key_ref[:, places[pair]] = dot(
            one_above_other(grad_weights), by_head(query, 0), 0, 0
        )
        grad_value_ref[:, places[pair]] = dot(
            one_above_other(weights), by_head(grad_mixed, 0), 0, 0
        )
        terms = one_above_other(decayed_scores * grad_pairs)
        before = dot(stacked(terms, 1), earlier)
        for head in range(2):
            part = before[head * tokens : (head + 1) * tokens]
            balance_rows.append(jnp.sum(jnp.where(reached, part, 0.0), axis=0, keepdims=True))
        entry_rows.append(dot(chooser, stacked(query.astype(F32) * carried[pair], 1), 1, 1)[:2])
    later_ref[...] = jnp.concatenate(balance_rows, axis=0) + row_sums(
        jnp.concatenate(entry_rows, axis=0), reached
    )


def other_backward_kernel(*refs):
    inputs, (layer_own, layer_other, query_own) = refs[:7], refs[7:10]
    layer_ref, grad_query_ref = refs[10:12]
    *outs, query_part, sent = refs[12:]
    width = layer_ref.shape[2]
    half = own_half(False)
    own_lanes, lanes = half_lanes(own_half(True), width), half_lanes(half, width)
    copies = [
        pltpu.make_async_copy(source, target, sent.at[i])
        for i, (source, target) in enumerate(
            [
                (layer_own, layer_ref.at[0, :, own_lanes]),
                (layer_other, layer_ref.at[0, :, lanes]),
                (query_own, grad_query_ref.at[0, :, own_lanes]),
                (query_part, grad_query_ref.at[0, :, lanes]),
            ]
        )
    ]

    @pl.when(half >= 0)
    def _():
        for copy in copies[:3]:
            copy.start()

    backward_kernel(False, *inputs, query_part, *outs)
    copies[3].start()
    for copy in copies:
        copy.wait()


def head_chooser():
    rows = lax.broadcasted_iota(jnp.int32, (8, LANES), 0)
    left = left_lanes((8, LANES))
    chosen = ((rows == 0) & left) | ((rows == 1) & ~left)
    return jnp.where(chosen, 1.0, 0.0).astype(BF16)


def row_sums(rows, keep):
    first, second = halves(rows)
    third = (rows - first.astype(F32) - second.astype(F32)).astype(BF16)
    weight = jnp.where(keep, 1.0, 0.0).astype(BF16)
    return dot(
        jnp.concatenate([first, second, third], axis=1),
        jnp.concatenate([weight, weight, weight], axis=0),
    )


def final_parts(
    mine,
    key_ref,
    value_ref,
    grad_key_part_ref,
    grad_value_part_ref,
    later_ref,
    leave_ref,
    state_ref,
    grad_ref,
    table_ref,
    key_out,
    value_out,
):
    tokens, width = key_ref.shape[1:]
    half = own_half(mine)
    carry = pick_rows(table_ref[pl.ds(CARRY_ROWS, 16), :], half)
    chooser = twice(head_chooser(), 1)
    left = left_lanes((1, LANES))
    lanes = [pair_lanes(half, width, pair) for pair in range(PAIRS)]
    places = [pl.ds(pair * LANES, LANES) for pair in range(PAIRS)]
    grads = [halves(by_head(grad_ref[pl.ds(pair * 64, 64), :], 0)) for pair in range(PAIRS)]
    carried, terms = [], []
    for pair in range(PAIRS):
        carried.append(
            leave_ref[:, places[pair]]
            * dot(twice(key_ref[0, :, lanes[pair]], 1), jnp.concatenate(grads[pair], axis=0))
        )
    for pair in range(PAIRS):
        value_out[:, places[pair]] = (
            grad_value_part_ref[:, places[pair]] + carried[pair]
        ).astype(BF16)
        terms.append(stacked(carried[pair] * value_ref[0, :, lanes[pair]].astype(F32), 1))
    earlier = [dot(chooser, terms[pair], 1, 1)[:2] for pair in range(PAIRS)]
    key_parts = [
        dot(twice(value_ref[0, :, lanes[pair]], 1), jnp.concatenate(grads[pair], axis=1), 1, 1)
        for pair in range(PAIRS)
    ]
    through_rows = []
    for pair in range(PAIRS):
        block = pl.ds(pair * 64, 64)
        product = jnp.sum(grad_ref[block, :] * state_ref[block, :], axis=0, keepdims=True)
        for side in (left, ~left):
            through_rows.append(jnp.sum(jnp.where(side, product, 0.0), axis=1, keepdims=True))
    for pair in range(PAIRS):
        key_out[:, places[pair]] = (
            grad_key_part_ref[:, places[pair]] + leave_ref[:, places[pair]] * key_parts[pair]
        ).astype(BF16)
    return (
        later_ref[...]
        + row_sums(jnp.concatenate(earlier, axis=0), triangle(tokens, lambda u, t: u < t))
        + carry * jnp.concatenate(through_rows, axis=0)
    )


def own_final_kernel(*refs):
    *refs, rows_ref = refs
    rows_ref[...] = final_parts(True, *refs)


def other_final_kernel(*refs):
    inputs, (key_own, value_own, other_ref, gain_part_ref) = refs[:9], refs[9:13]
    grad_key_ref, grad_value_ref, decay_ref, gain_ref = refs[13:17]
    *parts, decay_out, gain_out, sent = refs[17:]
    width = grad_key_ref.shape[2]
    half = own_half(False)
    own_lanes, lanes = half_lanes(own_half(True), width), half_lanes(half, width)
    pairs = [
        (key_own, grad_key_ref.at[0, :, own_lanes]),
        (value_own, grad_value_ref.at[0, :, own_lanes]),
        (gain_out, gain_ref),
        (parts[0], grad_key_ref.at[0, :, lanes]),
        (parts[1], grad_value_ref.at[0, :, lanes]),
        (decay_out, decay_ref.at[0]),
    ]
    copies = [
        pltpu.make_async_copy(source, target, sent.at[i])
        for i, (source, target) in enumerate(pairs)
    ]
    gain_out[...] = gain_part_ref[...] + inputs[7][pl.ds(PAIRS * 64, 2 * PAIRS), :]

    @pl.when(half >= 0)
    def _():
        for copy in copies[:3]:
            copy.start()

    rows = final_parts(False, *inputs, *parts)
    other = other_ref[...]
    decay_out[...] = jnp.where(
        half == 0,
        jnp.concatenate([rows, other], axis=0),
        jnp.concatenate([other, rows], axis=0),
    )
    for copy in copies[3:]:
        copy.start()
    for copy in copies:
        copy.wait()


VMEM, HBM = pltpu.VMEM, pltpu.HBM


def call(kernel, operands, results, scratch=(), aliases=None, flops=0, constrain=False):
    read = sum(a.size * a.dtype.itemsize for a, memory in operands if memory is VMEM)
    return pl.pallas_call(
        kernel,
        in_specs=[pl.BlockSpec(memory_space=memory) for a, memory in operands],
        out_specs=[pl.BlockSpec(memory_space=memory) for shape, dtype, memory in results],
        out_shape=[jax.ShapeDtypeStruct(shape, dtype) for shape, dtype, memory in results],
        scratch_shapes=list(scratch),
        input_output_aliases=aliases or {},
        compiler_params=pltpu.CompilerParams(vmem_limit_bytes=VMEM_BYTES),
        cost_estimate=pl.CostEstimate(flops=flops, bytes_accessed=read, transcendentals=0),
    )(
        *[
            pltpu.with_memory_space_constraint(a, HBM) if memory is HBM and constrain else a
            for a, memory in operands
        ]
    )


def local(queries, key_vectors, value_vectors, log_decay, restart, norm_gain, upstream):
    tokens, width = queries.shape[1], queries.shape[2]
    state_rows = PAIRS * 64
    buffer_rows = state_rows + 8
    blocks = lax.axis_size("seq")
    scans = lax.axis_size("dp")
    position = lax.axis_index("seq")
    on_first = (position & 1) == 0

    def exchange(x, bit, axis="seq"):
        size = blocks if axis == "seq" else scans
        return lax.ppermute(x, axis, [(i, i ^ bit) for i in range(size)])

    def parts(buffer):
        state = buffer[:state_rows].reshape(PAIRS, 64, LANES)
        if buffer.shape[0] == state_rows:
            return state, None
        return state, buffer[state_rows : state_rows + PAIRS].reshape(PAIRS, 1, LANES)

    def joined(state, carry):
        return jnp.concatenate(
            [
                state.reshape(state_rows, LANES),
                carry.reshape(PAIRS, LANES),
                jnp.zeros((8 - PAIRS, LANES), F32),
            ],
            axis=0,
        )

    def flat(state):
        return state.reshape(state_rows, LANES)

    whole = (1, tokens, width)
    part = (tokens, width // 2)
    buffer = (buffer_rows, LANES)
    rows = (HEAD_TOTAL // 2, LANES)
    blocks_of = [(queries, VMEM), (key_vectors, VMEM), (value_vectors, VMEM)]

    gain_rows = norm_gain.reshape(2 * PAIRS, LANES)

    state_other, tables = call(
        first_state_kernel,
        [
            (key_vectors, HBM),
            (value_vectors, HBM),
            (jnp.swapaxes(log_decay, 1, 2), HBM),
            (restart, HBM),
        ],
        [(buffer, F32, VMEM), ((TABLE_ROWS, LANES), F32, VMEM)],
        [
            pltpu.VMEM(part, BF16),
            pltpu.VMEM(part, BF16),
            pltpu.VMEM((HEAD_TOTAL, tokens), F32),
            pltpu.VMEM((1, tokens), jnp.int32),
            pltpu.SemaphoreType.DMA((4,)),
        ],
        constrain=True,
    )
    swapped = exchange(state_other, 1)
    (state_own,) = call(
        second_state_kernel,
        [(key_vectors, VMEM), (value_vectors, VMEM), (tables, VMEM)],
        [(buffer, F32, VMEM)],
    )
    first_state, first_carry = parts(jnp.where(on_first, state_own, swapped))
    second_state, second_carry = parts(jnp.where(on_first, swapped, state_own))
    total = second_carry * first_state + second_state
    carry = first_carry * second_carry
    prefix = jnp.zeros_like(total)
    prefix_carry = jnp.ones_like(carry)

    def mixture(mine, tables):
        return call(
            functools.partial(mixture_kernel, mine),
            blocks_of + [(upstream, VMEM), (gain_rows, VMEM), (tables, VMEM)],
            [
                (part, F32, VMEM),
                ((width // 2, LANES), BF16, VMEM),
                (part, F32, VMEM),
                (part, F32, VMEM),
            ],
            flops=0,
        )

    mixed = {}
    levels = []
    bit = 2
    while bit < blocks:
        is_upper = (position & bit) != 0
        sent = joined(total, carry)
        mine = not mixed
        if len(mixed) < 2:
            sent, tables = lax.optimization_barrier((sent, tables))
            mixed[mine] = mixture(mine, tables)
        received = exchange(sent, 2 * bit - 2)
        if len(levels) < 2:
            received, mixed[mine] = lax.optimization_barrier((received, mixed[mine]))
        theirs, their_carry = parts(received)
        prefix = jnp.where(is_upper, prefix_carry * theirs + prefix, prefix)
        prefix_carry = jnp.where(is_upper, prefix_carry * their_carry, prefix_carry)
        levels.append((bit, is_upper, carry, their_carry))
        total = jnp.where(is_upper, carry * theirs + total, their_carry * total + theirs)
        carry = carry * their_carry
        bit *= 2
    for mine in (True, False):
        if mine not in mixed:
            mixed[mine] = mixture(mine, tables)
    after_first = first_carry * prefix + first_state
    state_in = {True: flat(jnp.where(on_first, prefix, after_first))}
    state_in[False] = exchange(flat(jnp.where(on_first, after_first, prefix)), 1)

    layer_parts, grad_mixed, query_states = {}, {}, {}
    for mine in (True, False):
        operands = [
            *[(x, VMEM) for x in mixed[mine][:4]],
            (queries, VMEM),
            (upstream, VMEM),
            (gain_rows, VMEM),
            (state_in[mine], VMEM),
        ]
        if mine:
            kernel = lambda *refs: forward_kernel(True, *refs[:8], None, *refs[8:])
        else:
            operands.append((gain, VMEM))
            kernel = functools.partial(forward_kernel, False)
        layer_parts[mine], grad_mixed[mine], query_states[mine], gain = call(
            kernel,
            operands,
            [
                (part, BF16, VMEM),
                (part, BF16, VMEM),
                ((state_rows, LANES), F32, VMEM),
                ((2 * PAIRS, LANES), F32, VMEM),
            ],
        )

    def backward(mine, state):
        operands = blocks_of + [
            (grad_mixed[mine], VMEM),
            (state, VMEM),
            (mixed[mine][2], VMEM),
            (tables, VMEM),
        ]
        results = [(part, F32, VMEM), (part, F32, VMEM), (rows, F32, VMEM), (part, F32, VMEM)]
        if mine:
            return call(
                functools.partial(backward_kernel, True),
                operands,
                [(part, BF16, VMEM)] + results,
            )
        finished = (layer_parts[True], layer_parts[False], local_parts[True][0])
        return call(
            other_backward_kernel,
            operands + [(x, VMEM) for x in finished],
            [(whole, BF16, HBM), (whole, BF16, HBM)] + results,
            [pltpu.VMEM(part, BF16), pltpu.SemaphoreType.DMA((4,))],
        )

    steps = []
    step = scans // 2
    while step:
        steps.append(step)
        step //= 2
    swapped = exchange(query_states[False], 1)
    gains = [gain]
    for step in steps[:1]:
        larger = jnp.concatenate([gain, query_states[False][:24]], axis=0)
        gains.append(exchange(larger, step, "dp")[: 2 * PAIRS])
    first_query, _ = parts(jnp.where(on_first, query_states[True], swapped))
    second_query, _ = parts(jnp.where(on_first, swapped, query_states[True]))
    total = flat(first_query + first_carry * second_query)
    suffix = jnp.zeros_like(first_query)
    suffix_carry = jnp.ones_like(carry)
    local_parts = {}
    for bit, is_upper, carry, their_carry in levels:
        partner = 2 * bit - 2
        mine = not local_parts
        beside = len(local_parts) < 2
        if bit == 2:
            total, state = lax.optimization_barrier((total, state_in[mine]))
            received = exchange(total, partner)
            gain = sum(gains)
            for step in steps[1:]:
                gains = [gain, exchange(gain, step, "dp")]
                gain = sum(gains)
            if len(levels) == 1:
                gains = [gain, exchange(gain, partner)]
        else:
            total, gain, state = lax.optimization_barrier((total, sum(gains), state_in[mine]))
            received = exchange(jnp.concatenate([total, gain], axis=0), partner)
            gains = [gain]
            if 2 * bit == blocks:
                gains += [exchange(gain, 2), exchange(gain, partner ^ 2)]
        if beside:
            local_parts[mine] = backward(mine, state)
            received, gains, local_parts[mine] = lax.optimization_barrier(
                (received, gains, local_parts[mine])
            )
        if bit > 2:
            gains.append(received[state_rows:])
        theirs, _ = parts(received)
        total = parts(total)[0]
        suffix = jnp.where(is_upper, suffix, suffix_carry * theirs + suffix)
        suffix_carry = jnp.where(is_upper, suffix_carry, suffix_carry * their_carry)
        total = flat(jnp.where(is_upper, theirs + their_carry * total, total + carry * theirs))
    for mine in (True, False):
        if mine not in local_parts:
            local_parts[mine] = backward(mine, state_in[mine])
    if not levels:
        gain = sum(gains)
        for step in steps[1:]:
            gain = gain + exchange(gain, step, "dp")
        gains = [gain]
    before_second = second_query + second_carry * suffix
    state_grad = {True: flat(jnp.where(on_first, before_second, suffix))}
    gain = sum(gains)
    swapped = exchange(
        jnp.concatenate([flat(jnp.where(on_first, suffix, before_second)), gain], axis=0), 1
    )
    state_grad[False] = swapped

    def final_operands(mine):
        grad_key_part, grad_value_part, later, leave = local_parts[mine][-4:]
        return [
            (x, VMEM)
            for x in (
                key_vectors,
                value_vectors,
                grad_key_part,
                grad_value_part,
                later,
                leave,
                state_in[mine],
                state_grad[mine],
                tables,
            )
        ]

    grad_key, grad_value, decay_rows = call(
        own_final_kernel,
        final_operands(True),
        [(part, BF16, VMEM), (part, BF16, VMEM), (rows, F32, VMEM)],
    )
    finished = (grad_key, grad_value, decay_rows, gain)
    grad_key, grad_value, grad_decay, grad_gain = call(
        other_final_kernel,
        final_operands(False) + [(x, VMEM) for x in finished],
        [
            (whole, BF16, HBM),
            (whole, BF16, HBM),
            ((1, HEAD_TOTAL, tokens), F32, HBM),
            ((2 * PAIRS, LANES), F32, HBM),
        ],
        [
            pltpu.VMEM(part, BF16),
            pltpu.VMEM(part, BF16),
            pltpu.VMEM((HEAD_TOTAL, tokens), F32),
            pltpu.VMEM((2 * PAIRS, LANES), F32),
            pltpu.SemaphoreType.DMA((6,)),
        ],
    )
    layer_out, grad_query = local_parts[False][:2]
    return (
        layer_out,
        grad_query,
        grad_key,
        grad_value,
        jnp.swapaxes(grad_decay, 1, 2),
        grad_gain.reshape(-1),
    )


def solution(mesh):
    rows = P("dp", "seq", None)
    return jax.shard_map(
        local,
        mesh=mesh,
        in_specs=(rows, rows, rows, rows, P("dp", "seq"), P(), rows),
        out_specs=(rows, rows, rows, rows, rows, P()),
        check_vma=False,
    )
```

```python
import functools

import jax
import jax.numpy as jnp
from jax import lax
from jax.experimental import pallas as pl
from jax.experimental.pallas import tpu as pltpu
from jax.sharding import PartitionSpec as P

HEAD_TOTAL = 16
EPSILON = 1e-06
LANES = 128
PAIRS = HEAD_TOTAL // 4
VMEM_BYTES = 12 * 1024 * 1024
F32 = jnp.float32
BF16 = jnp.bfloat16
COLUMNS, CUM_ROWS, CARRY_ROWS, RESET_ROWS, TABLE_ROWS = 0, 128, 144, 160, 168


def dot(a, b, contract_a=1, contract_b=0):
    return lax.dot_general(
        a, b, (((contract_a,), (contract_b,)), ((), ())), preferred_element_type=F32
    )


def halves(x):
    high = x.astype(BF16)
    return high, (x - high.astype(F32)).astype(BF16)


def stacked(x, axis):
    return jnp.concatenate(halves(x), axis=axis)


def twice(x, axis):
    return jnp.concatenate([x, x], axis=axis)


def left_lanes(shape):
    return lax.broadcasted_iota(jnp.int32, shape, 1) < LANES // 2


def triangle(tokens, keep):
    rows = lax.broadcasted_iota(jnp.int32, (tokens, tokens), 0)
    columns = lax.broadcasted_iota(jnp.int32, (tokens, tokens), 1)
    return keep(rows, columns)


def by_head(x, axis):
    left = left_lanes(x.shape)
    zero = jnp.zeros_like(x)
    return jnp.concatenate([jnp.where(left, x, zero), jnp.where(left, zero, x)], axis=axis)


def fold(x):
    rows = x.shape[0] // 2
    return jnp.where(left_lanes((rows, LANES)), x[:rows], x[rows:])


def pair_columns(table, first, tokens):
    return jnp.where(
        left_lanes((tokens, LANES)),
        jnp.broadcast_to(table[:, first : first + 1], (tokens, LANES)),
        jnp.broadcast_to(table[:, first + 1 : first + 2], (tokens, LANES)),
    )


def make_tables(decay_rows, restart):
    heads, tokens = decay_rows.shape
    marks = jnp.broadcast_to(restart.astype(F32), (8, tokens))
    sums = row_sums(
        jnp.concatenate([decay_rows, marks], axis=0), triangle(tokens, lambda s, t: s <= t)
    )
    cum, resets = sums[:heads], sums[heads:]
    last, last_reset = cum[:, tokens - 1 :], resets[:1, tokens - 1 :]
    entry = jnp.where(resets[:1] == 0.0, jnp.exp(cum), 0.0)
    leave = jnp.where(resets[:1] == last_reset, jnp.exp(last - cum), 0.0)
    carry = jnp.where(last_reset == 0.0, jnp.exp(last), 0.0)
    rows = [cum, entry, leave, resets]
    rows.append(jnp.zeros((LANES - sum(x.shape[0] for x in rows), tokens), F32))
    columns = jnp.transpose(jnp.concatenate(rows, axis=0))
    return columns, cum, jnp.broadcast_to(carry, (heads, LANES)), resets


def make_mask(columns, resets):
    tokens = columns.shape[0]
    column = jnp.broadcast_to(columns[:, 3 * HEAD_TOTAL : 3 * HEAD_TOTAL + 1], (tokens, tokens))
    allowed = triangle(tokens, lambda t, s: t >= s) & (column == resets[:1])
    return jnp.where(allowed, 0.0, -1e30)


def pick_columns(columns, half):
    return jnp.where(half == 0, columns, pltpu.roll(columns, LANES - HEAD_TOTAL // 2, 1))


def pick_rows(rows, half):
    count = HEAD_TOTAL // 2
    return jnp.where(half == 0, rows[:count], rows[count:])


def own_half(mine):
    core = lax.axis_index("seq") & 1
    return core if mine else 1 - core


def half_lanes(half, width):
    return pl.ds(pl.multiple_of(half * (width // 2), LANES), width // 2)


def pair_lanes(half, width, pair):
    return pl.ds(pl.multiple_of(half * (width // 2) + pair * LANES, LANES), LANES)


def once(half, work):
    def step(i, carry):
        work()
        return carry

    lax.fori_loop(0, 1 + (half >> 1), step, 0)


def write_states(half, columns, carry_rows, keys, values, out_ref):
    tokens = keys.shape[0]
    table = pick_columns(columns, half)
    carry = pick_rows(carry_rows, half)
    left = left_lanes((1, LANES))
    scaled = []
    for pair in range(PAIRS):
        leave = pair_columns(table, 2 * HEAD_TOTAL + 2 * pair, tokens)
        lanes = slice(pair * LANES, (pair + 1) * LANES)
        scaled.append(stacked(values[:, lanes].astype(F32) * leave, 1))
    states = []
    for pair in range(PAIRS):
        lanes = slice(pair * LANES, (pair + 1) * LANES)
        states.append(dot(keys[:, lanes], scaled[pair], 0, 0))
    rows = []
    for pair in range(PAIRS):
        out_ref[pl.ds(pair * 64, 64), :] = fold(states[pair][:, :LANES] + states[pair][:, LANES:])
        rows.append(jnp.where(left, carry[2 * pair : 2 * pair + 1], carry[2 * pair + 1 : 2 * pair + 2]))
    rows.append(jnp.zeros((8 - len(rows), LANES), F32))
    out_ref[pl.ds(PAIRS * 64, 8), :] = jnp.concatenate(rows, axis=0)


def first_state_kernel(
    key_ref,
    value_ref,
    decay_ref,
    restart_ref,
    out_ref,
    table_ref,
    keys_ref,
    values_ref,
    decays,
    restarts,
    arrived,
):
    half = own_half(False)
    width = key_ref.shape[2]
    lanes, later_lanes = half_lanes(half, width), half_lanes(own_half(True), width)
    decay_copy = pltpu.make_async_copy(decay_ref.at[0], decays, arrived.at[4])
    restart_copy = pltpu.make_async_copy(restart_ref, restarts, arrived.at[5])
    copies = [
        pltpu.make_async_copy(
            source.at[0, :, place], target.at[0, :, place], arrived.at[2 * first + i]
        )
        for first, place in enumerate((lanes, later_lanes))
        for i, (source, target) in enumerate(((value_ref, values_ref), (key_ref, keys_ref)))
    ]
    decay_copy.start()
    restart_copy.start()
    for copy in copies:
        copy.start()
    decay_copy.wait()
    restart_copy.wait()
    columns, cum_rows, carry_rows, reset_rows = make_tables(decays[...], restarts[...])
    table_ref[pl.ds(COLUMNS, 128), :] = columns
    table_ref[pl.ds(CUM_ROWS, 16), :] = cum_rows
    table_ref[pl.ds(CARRY_ROWS, 16), :] = carry_rows
    table_ref[pl.ds(RESET_ROWS, 8), :] = reset_rows
    for copy in copies[:2]:
        copy.wait()
    write_states(
        half, columns, carry_rows, keys_ref[0, :, lanes], values_ref[0, :, lanes], out_ref
    )
    for copy in copies[2:]:
        copy.wait()


def second_state_kernel(key_ref, value_ref, table_ref, out_ref, mask_ref):
    half = own_half(True)
    lanes = half_lanes(half, key_ref.shape[2])
    write_states(
        half,
        table_ref[pl.ds(COLUMNS, 128), :],
        table_ref[pl.ds(CARRY_ROWS, 16), :],
        key_ref[0, :, lanes],
        value_ref[0, :, lanes],
        out_ref,
    )
    mask_ref[...] = make_mask(
        table_ref[pl.ds(COLUMNS, 128), :], table_ref[pl.ds(RESET_ROWS, 8), :]
    )


def pair_decays(table, cum_rows, mask, pair, tokens):
    parts = []
    for head in (2 * pair, 2 * pair + 1):
        column = jnp.broadcast_to(table[:, head : head + 1], (tokens, tokens))
        parts.append(jnp.exp(column - cum_rows[head : head + 1] + mask))
    return jnp.concatenate(parts, axis=1)


def one_above_other(x):
    columns = x.shape[1] // 2
    return jnp.concatenate([x[:, :columns], x[:, columns:]], axis=0)


def pick_gains(gain_ref, half):
    return jnp.where(half == 0, gain_ref[:PAIRS, :], gain_ref[PAIRS:, :])


def mixture_kernel(
    mine,
    query_ref,
    key_ref,
    value_ref,
    upstream_ref,
    gain_ref,
    table_ref,
    mask_ref,
    out_ref,
    turned_ref,
    entry_ref,
    grad_ref,
):
    tokens, width = query_ref.shape[1:]
    half = own_half(mine)
    table = pick_columns(table_ref[pl.ds(COLUMNS, 128), :], half)
    cum_rows = pick_rows(table_ref[pl.ds(CUM_ROWS, 16), :], half)
    mask = mask_ref[...]
    gains = pick_gains(gain_ref, half)
    for pair in range(PAIRS):
        lanes = pair_lanes(half, width, pair)
        query = query_ref[0, :, lanes]
        decay = pair_decays(table, cum_rows, mask, pair, tokens)
        scores = dot(query, by_head(key_ref[0, :, lanes], 0), 1, 1) * decay
        weights = scores.astype(BF16)
        here = pl.ds(pair * LANES, LANES)
        grad_ref[:, here] = upstream_ref[0, :, lanes].astype(F32) * gains[pair : pair + 1]
        out_ref[:, here] = dot(weights, by_head(value_ref[0, :, lanes], 0))
        turned_ref[here, :] = jnp.transpose(query)
        entry_ref[:, here] = pair_columns(table, HEAD_TOTAL + 2 * pair, tokens)


def forward_kernel(
    mine,
    mixed_ref,
    turned_ref,
    entry_ref,
    grad_ref,
    query_ref,
    upstream_ref,
    gain_ref,
    state_ref,
    before_ref,
    layer_ref,
    grad_mixed_ref,
    out_ref,
):
    tokens, width = query_ref.shape[1:]
    half = own_half(mine)
    gains = pick_gains(gain_ref, half)
    own = left_lanes((LANES, LANES)) == (lax.broadcasted_iota(jnp.int32, (LANES, LANES), 0) < 64)
    average = twice(jnp.where(own, 1.0 / 64.0, 0.0).astype(BF16), 0)
    places = [pl.ds(pair * LANES, LANES) for pair in range(PAIRS)]
    lanes = [pair_lanes(half, width, pair) for pair in range(PAIRS)]
    states = [
        stacked(by_head(state_ref[pl.ds(pair * 64, 64), :], 0), 0) for pair in range(PAIRS)
    ]
    carried = [
        dot(twice(query_ref[0, :, lanes[pair]], 1), states[pair]) for pair in range(PAIRS)
    ]
    mixtures = [
        mixed_ref[:, places[pair]] + entry_ref[:, places[pair]] * carried[pair]
        for pair in range(PAIRS)
    ]
    squares = dot(
        jnp.concatenate([stacked(mixture * mixture, 1) for mixture in mixtures], axis=0), average
    )
    normeds, inverses, grads, products, gain_parts = [], [], [], [], []
    for pair in range(PAIRS):
        inverse = lax.rsqrt(squares[pair * tokens : (pair + 1) * tokens] + EPSILON)
        normed = mixtures[pair] * inverse
        gain = gains[pair : pair + 1]
        upstream = upstream_ref[0, :, lanes[pair]].astype(F32)
        grad_normed = grad_ref[:, places[pair]]
        products.append(stacked(grad_normed * normed, 1))
        layer_ref[:, places[pair]] = (normed * gain).astype(BF16)
        gain_parts.append(jnp.sum(upstream * normed, axis=0, keepdims=True))
        normeds.append(normed)
        inverses.append(inverse)
        grads.append(grad_normed)
    shared = dot(jnp.concatenate(products, axis=0), average)
    sides = []
    for pair in range(PAIRS):
        part = shared[pair * tokens : (pair + 1) * tokens]
        grad_mixed = (inverses[pair] * (grads[pair] - normeds[pair] * part)).astype(BF16)
        grad_mixed_ref[:, places[pair]] = grad_mixed
        sides.append(stacked(entry_ref[:, places[pair]] * grad_mixed.astype(F32), 1))
    for pair in range(PAIRS):
        both = dot(turned_ref[places[pair], :], sides[pair])
        out_ref[pl.ds(pair * 64, 64), :] = fold(both[:, :LANES] + both[:, LANES:])
    part = jnp.concatenate(gain_parts, axis=0)
    blank = jnp.zeros_like(part)
    part = jnp.where(
        half == 0,
        jnp.concatenate([part, blank], axis=0),
        jnp.concatenate([blank, part], axis=0),
    )
    if before_ref is not None:
        part = part + before_ref[pl.ds(PAIRS * 64, 2 * PAIRS), :]
    out_ref[pl.ds(PAIRS * 64, 2 * PAIRS), :] = part


def backward_kernel(
    mine,
    query_ref,
    key_ref,
    value_ref,
    grad_mixed_ref,
    state_ref,
    entry_ref,
    table_ref,
    mask_ref,
    grad_query_ref,
    grad_key_ref,
    grad_value_ref,
    later_ref,
    leave_ref,
):
    tokens, width = query_ref.shape[1:]
    half = own_half(mine)
    table = pick_columns(table_ref[pl.ds(COLUMNS, 128), :], half)
    cum_rows = pick_rows(table_ref[pl.ds(CUM_ROWS, 16), :], half)
    mask = mask_ref[...]
    earlier = twice(triangle(tokens, lambda s, t: s < t).astype(F32).astype(BF16), 0)
    reached = triangle(tokens, lambda u, t: u >= t)
    chooser = twice(head_chooser(), 1)
    places = [pl.ds(pair * LANES, LANES) for pair in range(PAIRS)]
    lanes = [pair_lanes(half, width, pair) for pair in range(PAIRS)]
    balance_rows, entry_rows, carried = [], [], []
    for pair in range(PAIRS):
        state = by_head(state_ref[pl.ds(pair * 64, 64), :], 0)
        grad_mixed = grad_mixed_ref[:, places[pair]]
        carried.append(
            entry_ref[:, places[pair]] * dot(twice(grad_mixed, 1), stacked(state, 1), 1, 1)
        )
        leave_ref[:, places[pair]] = pair_columns(table, 2 * HEAD_TOTAL + 2 * pair, tokens)
    for pair in range(PAIRS):
        query = query_ref[0, :, lanes[pair]]
        grad_mixed = grad_mixed_ref[:, places[pair]]
        key_rows = by_head(key_ref[0, :, lanes[pair]], 0)
        decay = pair_decays(table, cum_rows, mask, pair, tokens)
        decayed_scores = dot(query, key_rows, 1, 1) * decay
        grad_pairs = dot(grad_mixed, by_head(value_ref[0, :, lanes[pair]], 0), 1, 1)
        weights = decayed_scores.astype(BF16)
        grad_weights = (grad_pairs * decay).astype(BF16)
        grad_query_ref[:, places[pair]] = (dot(grad_weights, key_rows) + carried[pair]).astype(
            BF16
        )
        grad_key_ref[:, places[pair]] = dot(
            one_above_other(grad_weights), by_head(query, 0), 0, 0
        )
        grad_value_ref[:, places[pair]] = dot(
            one_above_other(weights), by_head(grad_mixed, 0), 0, 0
        )
        terms = one_above_other(decayed_scores * grad_pairs)
        before = dot(stacked(terms, 1), earlier)
        for head in range(2):
            part = before[head * tokens : (head + 1) * tokens]
            balance_rows.append(jnp.sum(jnp.where(reached, part, 0.0), axis=0, keepdims=True))
        entry_rows.append(dot(chooser, stacked(query.astype(F32) * carried[pair], 1), 1, 1)[:2])
    later_ref[...] = jnp.concatenate(balance_rows, axis=0) + row_sums(
        jnp.concatenate(entry_rows, axis=0), reached
    )


def other_backward_kernel(*refs):
    inputs, (layer_own, layer_other), layer_ref = refs[:8], refs[8:10], refs[10]
    *outs, sent = refs[11:]
    width = layer_ref.shape[2]
    half = own_half(False)
    own_lanes, lanes = half_lanes(own_half(True), width), half_lanes(half, width)
    copies = [
        pltpu.make_async_copy(source, target, sent.at[i])
        for i, (source, target) in enumerate(
            [
                (layer_own, layer_ref.at[0, :, own_lanes]),
                (layer_other, layer_ref.at[0, :, lanes]),
            ]
        )
    ]

    for copy in copies:
        copy.start()
    once(half, lambda: backward_kernel(False, *inputs, *outs))
    for copy in copies:
        copy.wait()


def head_chooser():
    rows = lax.broadcasted_iota(jnp.int32, (8, LANES), 0)
    left = left_lanes((8, LANES))
    chosen = ((rows == 0) & left) | ((rows == 1) & ~left)
    return jnp.where(chosen, 1.0, 0.0).astype(BF16)


def row_sums(rows, keep):
    first, second = halves(rows)
    third = (rows - first.astype(F32) - second.astype(F32)).astype(BF16)
    weight = jnp.where(keep, 1.0, 0.0).astype(BF16)
    return dot(
        jnp.concatenate([first, second, third], axis=1),
        jnp.concatenate([weight, weight, weight], axis=0),
    )


def final_parts(
    mine,
    key_ref,
    value_ref,
    grad_key_part_ref,
    grad_value_part_ref,
    later_ref,
    leave_ref,
    state_ref,
    grad_ref,
    table_ref,
    key_out,
    value_out,
):
    tokens, width = key_ref.shape[1:]
    half = own_half(mine)
    carry = pick_rows(table_ref[pl.ds(CARRY_ROWS, 16), :], half)
    chooser = twice(head_chooser(), 1)
    left = left_lanes((1, LANES))
    lanes = [pair_lanes(half, width, pair) for pair in range(PAIRS)]
    places = [pl.ds(pair * LANES, LANES) for pair in range(PAIRS)]
    grads = [halves(by_head(grad_ref[pl.ds(pair * 64, 64), :], 0)) for pair in range(PAIRS)]
    carried, terms = [], []
    for pair in range(PAIRS):
        carried.append(
            leave_ref[:, places[pair]]
            * dot(twice(key_ref[0, :, lanes[pair]], 1), jnp.concatenate(grads[pair], axis=0))
        )
    for pair in range(PAIRS):
        value_out[:, places[pair]] = (
            grad_value_part_ref[:, places[pair]] + carried[pair]
        ).astype(BF16)
        terms.append(stacked(carried[pair] * value_ref[0, :, lanes[pair]].astype(F32), 1))
    earlier = [dot(chooser, terms[pair], 1, 1)[:2] for pair in range(PAIRS)]
    key_parts = [
        dot(twice(value_ref[0, :, lanes[pair]], 1), jnp.concatenate(grads[pair], axis=1), 1, 1)
        for pair in range(PAIRS)
    ]
    through_rows = []
    for pair in range(PAIRS):
        block = pl.ds(pair * 64, 64)
        product = jnp.sum(grad_ref[block, :] * state_ref[block, :], axis=0, keepdims=True)
        for side in (left, ~left):
            through_rows.append(jnp.sum(jnp.where(side, product, 0.0), axis=1, keepdims=True))
    for pair in range(PAIRS):
        key_out[:, places[pair]] = (
            grad_key_part_ref[:, places[pair]] + leave_ref[:, places[pair]] * key_parts[pair]
        ).astype(BF16)
    return (
        later_ref[...]
        + row_sums(jnp.concatenate(earlier, axis=0), triangle(tokens, lambda u, t: u < t))
        + carry * jnp.concatenate(through_rows, axis=0)
    )


def own_final_kernel(*refs):
    *refs, rows_ref = refs
    rows_ref[...] = final_parts(True, *refs)


def other_final_kernel(*refs):
    inputs, done, (other_ref, gain_part_ref) = refs[:9], refs[9:13], refs[13:15]
    grad_query_ref, grad_key_ref, grad_value_ref, decay_ref, gain_ref = refs[15:20]
    *parts, decay_out, gain_out, sent = refs[20:]
    width = grad_key_ref.shape[2]
    half = own_half(False)
    own_lanes, lanes = half_lanes(own_half(True), width), half_lanes(half, width)
    pairs = [
        (done[0], grad_query_ref.at[0, :, own_lanes]),
        (done[1], grad_query_ref.at[0, :, lanes]),
        (done[2], grad_key_ref.at[0, :, own_lanes]),
        (done[3], grad_value_ref.at[0, :, own_lanes]),
        (gain_out, gain_ref),
        (parts[0], grad_key_ref.at[0, :, lanes]),
        (parts[1], grad_value_ref.at[0, :, lanes]),
        (decay_out, decay_ref.at[0]),
    ]
    copies = [
        pltpu.make_async_copy(source, target, sent.at[i])
        for i, (source, target) in enumerate(pairs)
    ]
    gain_out[...] = gain_part_ref[...] + inputs[7][pl.ds(PAIRS * 64, 2 * PAIRS), :]

    for copy in copies[:5]:
        copy.start()

    def work():
        rows = final_parts(False, *inputs, *parts)
        other = other_ref[...]
        decay_out[...] = jnp.where(
            half == 0,
            jnp.concatenate([rows, other], axis=0),
            jnp.concatenate([other, rows], axis=0),
        )

    once(half, work)
    for copy in copies[5:]:
        copy.start()
    for copy in copies:
        copy.wait()


VMEM, HBM = pltpu.VMEM, pltpu.HBM


def call(kernel, operands, results, scratch=(), aliases=None, flops=0, constrain=False):
    read = sum(a.size * a.dtype.itemsize for a, memory in operands if memory is VMEM)
    return pl.pallas_call(
        kernel,
        in_specs=[pl.BlockSpec(memory_space=memory) for a, memory in operands],
        out_specs=[pl.BlockSpec(memory_space=memory) for shape, dtype, memory in results],
        out_shape=[jax.ShapeDtypeStruct(shape, dtype) for shape, dtype, memory in results],
        scratch_shapes=list(scratch),
        input_output_aliases=aliases or {},
        compiler_params=pltpu.CompilerParams(vmem_limit_bytes=VMEM_BYTES),
        cost_estimate=pl.CostEstimate(flops=flops, bytes_accessed=read, transcendentals=0),
    )(
        *[
            pltpu.with_memory_space_constraint(a, HBM) if memory is HBM and constrain else a
            for a, memory in operands
        ]
    )


def local(queries, key_vectors, value_vectors, log_decay, restart, norm_gain, upstream):
    tokens, width = queries.shape[1], queries.shape[2]
    state_rows = PAIRS * 64
    buffer_rows = state_rows + 8
    blocks = lax.axis_size("seq")
    scans = lax.axis_size("dp")
    position = lax.axis_index("seq")
    on_first = (position & 1) == 0

    def exchange(x, bit, axis="seq"):
        size = blocks if axis == "seq" else scans
        return lax.ppermute(x, axis, [(i, i ^ bit) for i in range(size)])

    def exchange_mixed(x, *bits):
        pairs = [
            (i * scans + j, (i ^ bits[i & 1][0]) * scans + (j ^ bits[i & 1][1]))
            for i in range(blocks)
            for j in range(scans)
        ]
        return lax.ppermute(x, ("seq", "dp"), pairs)

    def parts(buffer):
        state = buffer[:state_rows].reshape(PAIRS, 64, LANES)
        if buffer.shape[0] == state_rows:
            return state, None
        return state, buffer[state_rows : state_rows + PAIRS].reshape(PAIRS, 1, LANES)

    def joined(state, carry):
        return jnp.concatenate(
            [
                state.reshape(state_rows, LANES),
                carry.reshape(PAIRS, LANES),
                jnp.zeros((8 - PAIRS, LANES), F32),
            ],
            axis=0,
        )

    def flat(state):
        return state.reshape(state_rows, LANES)

    whole = (1, tokens, width)
    part = (tokens, width // 2)
    buffer = (buffer_rows, LANES)
    rows = (HEAD_TOTAL // 2, LANES)

    gain_rows = norm_gain.reshape(2 * PAIRS, LANES)

    state_other, tables, key_vectors, value_vectors = call(
        first_state_kernel,
        [
            (key_vectors, HBM),
            (value_vectors, HBM),
            (jnp.swapaxes(log_decay, 1, 2), HBM),
            (restart, HBM),
        ],
        [
            (buffer, F32, VMEM),
            ((TABLE_ROWS, LANES), F32, VMEM),
            (whole, BF16, VMEM),
            (whole, BF16, VMEM),
        ],
        [
            pltpu.VMEM((HEAD_TOTAL, tokens), F32),
            pltpu.VMEM((1, tokens), jnp.int32),
            pltpu.SemaphoreType.DMA((6,)),
        ],
        constrain=True,
    )
    blocks_of = [(queries, VMEM), (key_vectors, VMEM), (value_vectors, VMEM)]
    swapped = exchange(state_other, 1)
    state_own, mask = call(
        second_state_kernel,
        [(key_vectors, VMEM), (value_vectors, VMEM), (tables, VMEM)],
        [(buffer, F32, VMEM), ((tokens, tokens), F32, VMEM)],
    )
    first_state, first_carry = parts(jnp.where(on_first, state_own, swapped))
    second_state, second_carry = parts(jnp.where(on_first, swapped, state_own))
    total = second_carry * first_state + second_state
    carry = first_carry * second_carry
    prefix = jnp.zeros_like(total)
    prefix_carry = jnp.ones_like(carry)

    def mixture(mine, tables):
        return call(
            functools.partial(mixture_kernel, mine),
            blocks_of + [(upstream, VMEM), (gain_rows, VMEM), (tables, VMEM), (mask, VMEM)],
            [
                (part, F32, VMEM),
                ((width // 2, LANES), BF16, VMEM),
                (part, F32, VMEM),
                (part, F32, VMEM),
            ],
            flops=0,
        )

    mixed = {}
    levels = []
    bit = 2
    while bit < blocks:
        is_upper = (position & bit) != 0
        sent = joined(total, carry)
        mine = not mixed
        if len(mixed) < 2:
            sent, tables = lax.optimization_barrier((sent, tables))
            mixed[mine] = mixture(mine, tables)
        received = exchange(sent, 2 * bit - 2)
        if len(levels) < 2:
            received, mixed[mine] = lax.optimization_barrier((received, mixed[mine]))
        theirs, their_carry = parts(received)
        prefix = jnp.where(is_upper, prefix_carry * theirs + prefix, prefix)
        prefix_carry = jnp.where(is_upper, prefix_carry * their_carry, prefix_carry)
        levels.append((bit, is_upper, carry, their_carry))
        total = jnp.where(is_upper, carry * theirs + total, their_carry * total + theirs)
        carry = carry * their_carry
        bit *= 2
    for mine in (True, False):
        if mine not in mixed:
            mixed[mine] = mixture(mine, tables)
    after_first = first_carry * prefix + first_state
    state_in = {True: flat(jnp.where(on_first, prefix, after_first))}
    state_in[False] = exchange(flat(jnp.where(on_first, after_first, prefix)), 1)

    layer_parts, grad_mixed, query_states = {}, {}, {}
    for mine in (True, False):
        operands = [
            *[(x, VMEM) for x in mixed[mine][:4]],
            (queries, VMEM),
            (upstream, VMEM),
            (gain_rows, VMEM),
            (state_in[mine], VMEM),
        ]
        if mine:
            kernel = lambda *refs: forward_kernel(True, *refs[:8], None, *refs[8:])
        else:
            operands.append((query_states[True], VMEM))
            kernel = functools.partial(forward_kernel, False)
        layer_parts[mine], grad_mixed[mine], query_states[mine] = call(
            kernel, operands, [(part, BF16, VMEM), (part, BF16, VMEM), (buffer, F32, VMEM)]
        )

    def backward(mine, state):
        operands = blocks_of + [
            (grad_mixed[mine], VMEM),
            (state, VMEM),
            (mixed[mine][2], VMEM),
            (tables, VMEM),
            (mask, VMEM),
        ]
        results = [
            (part, BF16, VMEM),
            (part, F32, VMEM),
            (part, F32, VMEM),
            (rows, F32, VMEM),
            (part, F32, VMEM),
        ]
        if mine:
            return call(functools.partial(backward_kernel, True), operands, results)
        return call(
            other_backward_kernel,
            operands + [(layer_parts[x], VMEM) for x in (True, False)],
            [(whole, BF16, HBM)] + results,
            [pltpu.SemaphoreType.DMA((2,))],
        )

    steps = []
    step = scans // 2
    while step:
        steps.append(step)
        step //= 2
    swapped = exchange(query_states[False], 1)
    chip_gain = query_states[False][state_rows:] + swapped[state_rows:]
    gains = [jnp.where(on_first, chip_gain, 0.0)]
    first_query, _ = parts(jnp.where(on_first, query_states[True], swapped))
    second_query, _ = parts(jnp.where(on_first, swapped, query_states[True]))
    total = flat(first_query + first_carry * second_query)
    suffix = jnp.zeros_like(first_query)
    suffix_carry = jnp.ones_like(carry)
    local_parts = {}
    if len(levels) == 2 and scans == 4:
        total, chip_gain = lax.optimization_barrier((total, chip_gain))
        received = exchange(jnp.concatenate([total, chip_gain], axis=0), 2)
        fetched = [exchange_mixed(chip_gain, *bits) for bits in (((0, 1), (0, 3)), ((0, 2), (2, 1)), ((2, 3), (2, 2)))]
        bit, is_upper, carry, their_carry = levels[0]
        near = parts(received)[0]
        own_query = parts(total)[0]
        total = flat(jnp.where(is_upper, near + their_carry * own_query, own_query + carry * near))
        gain = jnp.where(on_first, chip_gain + received[state_rows:], 0.0) + sum(fetched)
        total, state = lax.optimization_barrier((total, state_in[False]))
        received = exchange(total, 6)
        others = exchange(gain, 6)
        local_parts[True] = backward(True, state_in[True])
        local_parts[False] = backward(False, state)
        received, others, local_parts = lax.optimization_barrier((received, others, local_parts))
        gains = [gain, others]
        first_level, (bit, is_last, carry, their_carry) = levels
        far = parts(received)[0]
        suffix = jnp.where(
            is_last,
            jnp.where(is_upper, 0.0, near),
            jnp.where(is_upper, far, near + first_level[3] * far),
        )
        levels = []
    for bit, is_upper, carry, their_carry in levels:
        partner = 2 * bit - 2
        mine = not local_parts
        beside = len(local_parts) < 2
        if bit == 2:
            total, state = lax.optimization_barrier((total, state_in[mine]))
            received = exchange(total, partner)
            gain = sum(gains)
            for step in steps:
                gains = [gain, exchange(gain, step, "dp")]
                gain = sum(gains)
            if len(levels) == 1:
                gains = [gain, exchange(gain, partner)]
        else:
            total, gain, state = lax.optimization_barrier((total, sum(gains), state_in[mine]))
            received = exchange(jnp.concatenate([total, gain], axis=0), partner)
            gains = [gain]
            if 2 * bit == blocks:
                gains += [exchange(gain, 2), exchange(gain, partner ^ 2)]
        if beside:
            local_parts[mine] = backward(mine, state)
            received, gains, local_parts[mine] = lax.optimization_barrier(
                (received, gains, local_parts[mine])
            )
        if bit > 2:
            gains.append(received[state_rows:])
        theirs, _ = parts(received)
        total = parts(total)[0]
        suffix = jnp.where(is_upper, suffix, suffix_carry * theirs + suffix)
        suffix_carry = jnp.where(is_upper, suffix_carry, suffix_carry * their_carry)
        total = flat(jnp.where(is_upper, theirs + their_carry * total, total + carry * theirs))
    for mine in (True, False):
        if mine not in local_parts:
            local_parts[mine] = backward(mine, state_in[mine])
    if blocks == 2:
        gain = sum(gains)
        for step in steps:
            gain = gain + exchange(gain, step, "dp")
        gains = [gain]
    before_second = second_query + second_carry * suffix
    state_grad = {True: flat(jnp.where(on_first, before_second, suffix))}
    gain = sum(gains)
    swapped = exchange(
        jnp.concatenate([flat(jnp.where(on_first, suffix, before_second)), gain], axis=0), 1
    )
    state_grad[False] = swapped

    def final_operands(mine):
        grad_key_part, grad_value_part, later, leave = local_parts[mine][-4:]
        return [
            (x, VMEM)
            for x in (
                key_vectors,
                value_vectors,
                grad_key_part,
                grad_value_part,
                later,
                leave,
                state_in[mine],
                state_grad[mine],
                tables,
            )
        ]

    grad_key, grad_value, decay_rows = call(
        own_final_kernel,
        final_operands(True),
        [(part, BF16, VMEM), (part, BF16, VMEM), (rows, F32, VMEM)],
    )
    finished = [local_parts[mine][-5] for mine in (True, False)]
    finished += [grad_key, grad_value, decay_rows, gain]
    grad_query, grad_key, grad_value, grad_decay, grad_gain = call(
        other_final_kernel,
        final_operands(False) + [(x, VMEM) for x in finished],
        [
            (whole, BF16, HBM),
            (whole, BF16, HBM),
            (whole, BF16, HBM),
            ((1, HEAD_TOTAL, tokens), F32, HBM),
            ((2 * PAIRS, LANES), F32, HBM),
        ],
        [
            pltpu.VMEM(part, BF16),
            pltpu.VMEM(part, BF16),
            pltpu.VMEM((HEAD_TOTAL, tokens), F32),
            pltpu.VMEM((2 * PAIRS, LANES), F32),
            pltpu.SemaphoreType.DMA((8,)),
        ],
    )
    return (
        local_parts[False][0],
        grad_query,
        grad_key,
        grad_value,
        jnp.swapaxes(grad_decay, 1, 2),
        grad_gain.reshape(-1),
    )


def solution(mesh):
    rows = P("dp", "seq", None)
    return jax.shard_map(
        local,
        mesh=mesh,
        in_specs=(rows, rows, rows, rows, P("dp", "seq"), P(), rows),
        out_specs=(rows, rows, rows, rows, rows, P()),
        check_vma=False,
    )
```

```python
import functools

import jax
import jax.numpy as jnp
from jax import lax
from jax.experimental import pallas as pl
from jax.experimental.pallas import tpu as pltpu
from jax.sharding import PartitionSpec as P

HEAD_TOTAL = 16
EPSILON = 1e-06
LANES = 128
PAIRS = HEAD_TOTAL // 4
VMEM_BYTES = 12 * 1024 * 1024
F32 = jnp.float32
BF16 = jnp.bfloat16
COLUMNS, CUM_ROWS, CARRY_ROWS, RESET_ROWS, TABLE_ROWS = 0, 128, 144, 160, 168


def dot(a, b, contract_a=1, contract_b=0):
    return lax.dot_general(
        a, b, (((contract_a,), (contract_b,)), ((), ())), preferred_element_type=F32
    )


def halves(x):
    high = x.astype(BF16)
    return high, (x - high.astype(F32)).astype(BF16)


def stacked(x, axis):
    return jnp.concatenate(halves(x), axis=axis)


def twice(x, axis):
    return jnp.concatenate([x, x], axis=axis)


def left_lanes(shape):
    return lax.broadcasted_iota(jnp.int32, shape, 1) < LANES // 2


def triangle(tokens, keep):
    rows = lax.broadcasted_iota(jnp.int32, (tokens, tokens), 0)
    columns = lax.broadcasted_iota(jnp.int32, (tokens, tokens), 1)
    return keep(rows, columns)


def by_head(x, axis):
    left = left_lanes(x.shape)
    zero = jnp.zeros_like(x)
    return jnp.concatenate([jnp.where(left, x, zero), jnp.where(left, zero, x)], axis=axis)


def fold(x):
    rows = x.shape[0] // 2
    return jnp.where(left_lanes((rows, LANES)), x[:rows], x[rows:])


def pair_columns(table, first, tokens):
    return jnp.where(
        left_lanes((tokens, LANES)),
        jnp.broadcast_to(table[:, first : first + 1], (tokens, LANES)),
        jnp.broadcast_to(table[:, first + 1 : first + 2], (tokens, LANES)),
    )


def make_tables(decay_rows, restart):
    heads, tokens = decay_rows.shape
    marks = jnp.broadcast_to(restart.astype(F32), (8, tokens))
    sums = row_sums(
        jnp.concatenate([decay_rows, marks], axis=0), triangle(tokens, lambda s, t: s <= t)
    )
    cum, resets = sums[:heads], sums[heads:]
    last, last_reset = cum[:, tokens - 1 :], resets[:1, tokens - 1 :]
    entry = jnp.where(resets[:1] == 0.0, jnp.exp(cum), 0.0)
    leave = jnp.where(resets[:1] == last_reset, jnp.exp(last - cum), 0.0)
    carry = jnp.where(last_reset == 0.0, jnp.exp(last), 0.0)
    rows = [cum, entry, leave, resets]
    rows.append(jnp.zeros((LANES - sum(x.shape[0] for x in rows), tokens), F32))
    columns = jnp.transpose(jnp.concatenate(rows, axis=0))
    return columns, cum, jnp.broadcast_to(carry, (heads, LANES)), resets


def make_mask(columns, resets):
    tokens = columns.shape[0]
    column = jnp.broadcast_to(columns[:, 3 * HEAD_TOTAL : 3 * HEAD_TOTAL + 1], (tokens, tokens))
    allowed = triangle(tokens, lambda t, s: t >= s) & (column == resets[:1])
    return jnp.where(allowed, 0.0, -1e30)


def pick_columns(columns, half):
    return jnp.where(half == 0, columns, pltpu.roll(columns, LANES - HEAD_TOTAL // 2, 1))


def pick_rows(rows, half):
    count = HEAD_TOTAL // 2
    return jnp.where(half == 0, rows[:count], rows[count:])


def own_half(mine):
    core = lax.axis_index("seq") & 1
    return core if mine else 1 - core


def half_lanes(half, width):
    return pl.ds(pl.multiple_of(half * (width // 2), LANES), width // 2)


def pair_lanes(half, width, pair):
    return pl.ds(pl.multiple_of(half * (width // 2) + pair * LANES, LANES), LANES)


def once(half, work):
    def step(i, carry):
        work()
        return carry

    lax.fori_loop(0, 1 + (half >> 1), step, 0)


def write_states(half, columns, carry_rows, keys, values, out_ref):
    tokens = keys.shape[0]
    table = pick_columns(columns, half)
    carry = pick_rows(carry_rows, half)
    left = left_lanes((1, LANES))
    scaled = []
    for pair in range(PAIRS):
        leave = pair_columns(table, 2 * HEAD_TOTAL + 2 * pair, tokens)
        lanes = slice(pair * LANES, (pair + 1) * LANES)
        scaled.append(stacked(values[:, lanes].astype(F32) * leave, 1))
    states = []
    for pair in range(PAIRS):
        lanes = slice(pair * LANES, (pair + 1) * LANES)
        states.append(dot(keys[:, lanes], scaled[pair], 0, 0))
    rows = []
    for pair in range(PAIRS):
        out_ref[pl.ds(pair * 64, 64), :] = fold(states[pair][:, :LANES] + states[pair][:, LANES:])
        rows.append(jnp.where(left, carry[2 * pair : 2 * pair + 1], carry[2 * pair + 1 : 2 * pair + 2]))
    rows.append(jnp.zeros((8 - len(rows), LANES), F32))
    out_ref[pl.ds(PAIRS * 64, 8), :] = jnp.concatenate(rows, axis=0)


def first_state_kernel(
    key_ref,
    value_ref,
    decay_ref,
    restart_ref,
    out_ref,
    table_ref,
    keys_ref,
    values_ref,
    decays,
    restarts,
    arrived,
):
    half = own_half(False)
    width = key_ref.shape[2]
    lanes, later_lanes = half_lanes(half, width), half_lanes(own_half(True), width)
    decay_copy = pltpu.make_async_copy(decay_ref.at[0], decays, arrived.at[4])
    restart_copy = pltpu.make_async_copy(restart_ref, restarts, arrived.at[5])
    copies = [
        pltpu.make_async_copy(
            source.at[0, :, place], target.at[0, :, place], arrived.at[2 * first + i]
        )
        for first, place in enumerate((lanes, later_lanes))
        for i, (source, target) in enumerate(((value_ref, values_ref), (key_ref, keys_ref)))
    ]
    decay_copy.start()
    restart_copy.start()
    for copy in copies:
        copy.start()
    decay_copy.wait()
    restart_copy.wait()
    columns, cum_rows, carry_rows, reset_rows = make_tables(decays[...], restarts[...])
    table_ref[pl.ds(COLUMNS, 128), :] = columns
    table_ref[pl.ds(CUM_ROWS, 16), :] = cum_rows
    table_ref[pl.ds(CARRY_ROWS, 16), :] = carry_rows
    table_ref[pl.ds(RESET_ROWS, 8), :] = reset_rows
    for copy in copies[:2]:
        copy.wait()
    write_states(
        half, columns, carry_rows, keys_ref[0, :, lanes], values_ref[0, :, lanes], out_ref
    )
    for copy in copies[2:]:
        copy.wait()


def second_state_kernel(key_ref, value_ref, table_ref, out_ref, mask_ref):
    half = own_half(True)
    lanes = half_lanes(half, key_ref.shape[2])
    write_states(
        half,
        table_ref[pl.ds(COLUMNS, 128), :],
        table_ref[pl.ds(CARRY_ROWS, 16), :],
        key_ref[0, :, lanes],
        value_ref[0, :, lanes],
        out_ref,
    )
    mask_ref[...] = make_mask(
        table_ref[pl.ds(COLUMNS, 128), :], table_ref[pl.ds(RESET_ROWS, 8), :]
    )


def pair_decays(table, cum_rows, mask, pair, tokens):
    parts = []
    for head in (2 * pair, 2 * pair + 1):
        column = jnp.broadcast_to(table[:, head : head + 1], (tokens, tokens))
        parts.append(jnp.exp(column - cum_rows[head : head + 1] + mask))
    return jnp.concatenate(parts, axis=1)


def one_above_other(x):
    columns = x.shape[1] // 2
    return jnp.concatenate([x[:, :columns], x[:, columns:]], axis=0)


def pick_gains(gain_ref, half):
    return jnp.where(half == 0, gain_ref[:PAIRS, :], gain_ref[PAIRS:, :])


def mixture_kernel(
    mine,
    query_ref,
    key_ref,
    value_ref,
    upstream_ref,
    gain_ref,
    table_ref,
    mask_ref,
    out_ref,
    turned_ref,
    entry_ref,
    grad_ref,
):
    tokens, width = query_ref.shape[1:]
    half = own_half(mine)
    table = pick_columns(table_ref[pl.ds(COLUMNS, 128), :], half)
    cum_rows = pick_rows(table_ref[pl.ds(CUM_ROWS, 16), :], half)
    mask = mask_ref[...]
    gains = pick_gains(gain_ref, half)
    for pair in range(PAIRS):
        lanes = pair_lanes(half, width, pair)
        query = query_ref[0, :, lanes]
        decay = pair_decays(table, cum_rows, mask, pair, tokens)
        scores = dot(query, by_head(key_ref[0, :, lanes], 0), 1, 1) * decay
        weights = scores.astype(BF16)
        here = pl.ds(pair * LANES, LANES)
        grad_ref[:, here] = upstream_ref[0, :, lanes].astype(F32) * gains[pair : pair + 1]
        out_ref[:, here] = dot(weights, by_head(value_ref[0, :, lanes], 0))
        turned_ref[here, :] = jnp.transpose(query)
        entry_ref[:, here] = pair_columns(table, HEAD_TOTAL + 2 * pair, tokens)


def forward_kernel(
    mine,
    mixed_ref,
    turned_ref,
    entry_ref,
    grad_ref,
    query_ref,
    upstream_ref,
    gain_ref,
    state_ref,
    before_ref,
    layer_ref,
    grad_mixed_ref,
    out_ref,
):
    tokens, width = query_ref.shape[1:]
    half = own_half(mine)
    gains = pick_gains(gain_ref, half)
    own = left_lanes((LANES, LANES)) == (lax.broadcasted_iota(jnp.int32, (LANES, LANES), 0) < 64)
    average = twice(jnp.where(own, 1.0 / 64.0, 0.0).astype(BF16), 0)
    places = [pl.ds(pair * LANES, LANES) for pair in range(PAIRS)]
    lanes = [pair_lanes(half, width, pair) for pair in range(PAIRS)]
    states = [
        stacked(by_head(state_ref[pl.ds(pair * 64, 64), :], 0), 0) for pair in range(PAIRS)
    ]
    carried = [
        dot(twice(query_ref[0, :, lanes[pair]], 1), states[pair]) for pair in range(PAIRS)
    ]
    mixtures = [
        mixed_ref[:, places[pair]] + entry_ref[:, places[pair]] * carried[pair]
        for pair in range(PAIRS)
    ]
    squares = dot(
        jnp.concatenate([stacked(mixture * mixture, 1) for mixture in mixtures], axis=0), average
    )
    normeds, inverses, grads, products, gain_parts = [], [], [], [], []
    for pair in range(PAIRS):
        inverse = lax.rsqrt(squares[pair * tokens : (pair + 1) * tokens] + EPSILON)
        normed = mixtures[pair] * inverse
        gain = gains[pair : pair + 1]
        upstream = upstream_ref[0, :, lanes[pair]].astype(F32)
        grad_normed = grad_ref[:, places[pair]]
        products.append(stacked(grad_normed * normed, 1))
        layer_ref[:, places[pair]] = (normed * gain).astype(BF16)
        gain_parts.append(jnp.sum(upstream * normed, axis=0, keepdims=True))
        normeds.append(normed)
        inverses.append(inverse)
        grads.append(grad_normed)
    shared = dot(jnp.concatenate(products, axis=0), average)
    sides = []
    for pair in range(PAIRS):
        part = shared[pair * tokens : (pair + 1) * tokens]
        grad_mixed = (inverses[pair] * (grads[pair] - normeds[pair] * part)).astype(BF16)
        grad_mixed_ref[:, places[pair]] = grad_mixed
        sides.append(stacked(entry_ref[:, places[pair]] * grad_mixed.astype(F32), 1))
    for pair in range(PAIRS):
        both = dot(turned_ref[places[pair], :], sides[pair])
        out_ref[pl.ds(pair * 64, 64), :] = fold(both[:, :LANES] + both[:, LANES:])
    part = jnp.concatenate(gain_parts, axis=0)
    blank = jnp.zeros_like(part)
    part = jnp.where(
        half == 0,
        jnp.concatenate([part, blank], axis=0),
        jnp.concatenate([blank, part], axis=0),
    )
    if before_ref is not None:
        part = part + before_ref[pl.ds(PAIRS * 64, 2 * PAIRS), :]
    out_ref[pl.ds(PAIRS * 64, 2 * PAIRS), :] = part


def backward_kernel(
    mine,
    query_ref,
    key_ref,
    value_ref,
    grad_mixed_ref,
    state_ref,
    entry_ref,
    table_ref,
    mask_ref,
    grad_query_ref,
    grad_key_ref,
    grad_value_ref,
    later_ref,
    leave_ref,
):
    tokens, width = query_ref.shape[1:]
    half = own_half(mine)
    table = pick_columns(table_ref[pl.ds(COLUMNS, 128), :], half)
    cum_rows = pick_rows(table_ref[pl.ds(CUM_ROWS, 16), :], half)
    mask = mask_ref[...]
    earlier = twice(triangle(tokens, lambda s, t: s < t).astype(F32).astype(BF16), 0)
    reached = triangle(tokens, lambda u, t: u >= t)
    chooser = twice(head_chooser(), 1)
    places = [pl.ds(pair * LANES, LANES) for pair in range(PAIRS)]
    lanes = [pair_lanes(half, width, pair) for pair in range(PAIRS)]
    balance_rows, entry_rows, carried = [], [], []
    for pair in range(PAIRS):
        state = by_head(state_ref[pl.ds(pair * 64, 64), :], 0)
        grad_mixed = grad_mixed_ref[:, places[pair]]
        carried.append(
            entry_ref[:, places[pair]] * dot(twice(grad_mixed, 1), stacked(state, 1), 1, 1)
        )
        leave_ref[:, places[pair]] = pair_columns(table, 2 * HEAD_TOTAL + 2 * pair, tokens)
    for pair in range(PAIRS):
        query = query_ref[0, :, lanes[pair]]
        grad_mixed = grad_mixed_ref[:, places[pair]]
        key_rows = by_head(key_ref[0, :, lanes[pair]], 0)
        decay = pair_decays(table, cum_rows, mask, pair, tokens)
        decayed_scores = dot(query, key_rows, 1, 1) * decay
        grad_pairs = dot(grad_mixed, by_head(value_ref[0, :, lanes[pair]], 0), 1, 1)
        weights = decayed_scores.astype(BF16)
        grad_weights = (grad_pairs * decay).astype(BF16)
        grad_query_ref[:, places[pair]] = (dot(grad_weights, key_rows) + carried[pair]).astype(
            BF16
        )
        grad_key_ref[:, places[pair]] = dot(
            one_above_other(grad_weights), by_head(query, 0), 0, 0
        )
        grad_value_ref[:, places[pair]] = dot(
            one_above_other(weights), by_head(grad_mixed, 0), 0, 0
        )
        terms = one_above_other(decayed_scores * grad_pairs)
        before = dot(stacked(terms, 1), earlier)
        for head in range(2):
            part = before[head * tokens : (head + 1) * tokens]
            balance_rows.append(jnp.sum(jnp.where(reached, part, 0.0), axis=0, keepdims=True))
        entry_rows.append(dot(chooser, stacked(query.astype(F32) * carried[pair], 1), 1, 1)[:2])
    later_ref[...] = jnp.concatenate(balance_rows, axis=0) + row_sums(
        jnp.concatenate(entry_rows, axis=0), reached
    )


def other_backward_kernel(*refs):
    inputs, (layer_own, layer_other), layer_ref = refs[:8], refs[8:10], refs[10]
    *outs, sent = refs[11:]
    width = layer_ref.shape[2]
    half = own_half(False)
    own_lanes, lanes = half_lanes(own_half(True), width), half_lanes(half, width)
    copies = [
        pltpu.make_async_copy(source, target, sent.at[i])
        for i, (source, target) in enumerate(
            [
                (layer_own, layer_ref.at[0, :, own_lanes]),
                (layer_other, layer_ref.at[0, :, lanes]),
            ]
        )
    ]

    for copy in copies:
        copy.start()
    once(half, lambda: backward_kernel(False, *inputs, *outs))
    for copy in copies:
        copy.wait()


def head_chooser():
    rows = lax.broadcasted_iota(jnp.int32, (8, LANES), 0)
    left = left_lanes((8, LANES))
    chosen = ((rows == 0) & left) | ((rows == 1) & ~left)
    return jnp.where(chosen, 1.0, 0.0).astype(BF16)


def row_sums(rows, keep):
    first, second = halves(rows)
    third = (rows - first.astype(F32) - second.astype(F32)).astype(BF16)
    weight = jnp.where(keep, 1.0, 0.0).astype(BF16)
    return dot(
        jnp.concatenate([first, second, third], axis=1),
        jnp.concatenate([weight, weight, weight], axis=0),
    )


def final_parts(
    mine,
    key_ref,
    value_ref,
    grad_key_part_ref,
    grad_value_part_ref,
    later_ref,
    leave_ref,
    state_ref,
    grad_ref,
    table_ref,
    key_out,
    value_out,
):
    tokens, width = key_ref.shape[1:]
    half = own_half(mine)
    carry = pick_rows(table_ref[pl.ds(CARRY_ROWS, 16), :], half)
    chooser = twice(head_chooser(), 1)
    left = left_lanes((1, LANES))
    lanes = [pair_lanes(half, width, pair) for pair in range(PAIRS)]
    places = [pl.ds(pair * LANES, LANES) for pair in range(PAIRS)]
    grads = [halves(by_head(grad_ref[pl.ds(pair * 64, 64), :], 0)) for pair in range(PAIRS)]
    carried, terms = [], []
    for pair in range(PAIRS):
        carried.append(
            leave_ref[:, places[pair]]
            * dot(twice(key_ref[0, :, lanes[pair]], 1), jnp.concatenate(grads[pair], axis=0))
        )
    for pair in range(PAIRS):
        value_out[:, places[pair]] = (
            grad_value_part_ref[:, places[pair]] + carried[pair]
        ).astype(BF16)
        terms.append(stacked(carried[pair] * value_ref[0, :, lanes[pair]].astype(F32), 1))
    earlier = [dot(chooser, terms[pair], 1, 1)[:2] for pair in range(PAIRS)]
    key_parts = [
        dot(twice(value_ref[0, :, lanes[pair]], 1), jnp.concatenate(grads[pair], axis=1), 1, 1)
        for pair in range(PAIRS)
    ]
    through_rows = []
    for pair in range(PAIRS):
        block = pl.ds(pair * 64, 64)
        product = jnp.sum(grad_ref[block, :] * state_ref[block, :], axis=0, keepdims=True)
        for side in (left, ~left):
            through_rows.append(jnp.sum(jnp.where(side, product, 0.0), axis=1, keepdims=True))
    for pair in range(PAIRS):
        key_out[:, places[pair]] = (
            grad_key_part_ref[:, places[pair]] + leave_ref[:, places[pair]] * key_parts[pair]
        ).astype(BF16)
    return (
        later_ref[...]
        + row_sums(jnp.concatenate(earlier, axis=0), triangle(tokens, lambda u, t: u < t))
        + carry * jnp.concatenate(through_rows, axis=0)
    )


def own_final_kernel(*refs):
    *refs, rows_ref = refs
    rows_ref[...] = final_parts(True, *refs)


def other_final_kernel(*refs):
    inputs, done, (other_ref, gain_part_ref) = refs[:9], refs[9:13], refs[13:15]
    grad_query_ref, grad_key_ref, grad_value_ref, decay_ref, gain_ref = refs[15:20]
    *parts, decay_out, gain_out, sent = refs[20:]
    width = grad_key_ref.shape[2]
    half = own_half(False)
    own_lanes, lanes = half_lanes(own_half(True), width), half_lanes(half, width)
    pairs = [
        (done[0], grad_query_ref.at[0, :, own_lanes]),
        (done[1], grad_query_ref.at[0, :, lanes]),
        (done[2], grad_key_ref.at[0, :, own_lanes]),
        (done[3], grad_value_ref.at[0, :, own_lanes]),
        (gain_out, gain_ref),
        (parts[0], grad_key_ref.at[0, :, lanes]),
        (parts[1], grad_value_ref.at[0, :, lanes]),
        (decay_out, decay_ref.at[0]),
    ]
    copies = [
        pltpu.make_async_copy(source, target, sent.at[i])
        for i, (source, target) in enumerate(pairs)
    ]
    gain_out[...] = gain_part_ref[...] + inputs[7][pl.ds(PAIRS * 64, 2 * PAIRS), :]

    for copy in copies[:5]:
        copy.start()

    def work():
        rows = final_parts(False, *inputs, *parts)
        other = other_ref[...]
        decay_out[...] = jnp.where(
            half == 0,
            jnp.concatenate([rows, other], axis=0),
            jnp.concatenate([other, rows], axis=0),
        )

    once(half, work)
    for copy in copies[5:]:
        copy.start()
    for copy in copies:
        copy.wait()


VMEM, HBM = pltpu.VMEM, pltpu.HBM


def call(kernel, operands, results, scratch=(), aliases=None, flops=0, constrain=False):
    read = sum(a.size * a.dtype.itemsize for a, memory in operands if memory is VMEM)
    return pl.pallas_call(
        kernel,
        in_specs=[pl.BlockSpec(memory_space=memory) for a, memory in operands],
        out_specs=[pl.BlockSpec(memory_space=memory) for shape, dtype, memory in results],
        out_shape=[jax.ShapeDtypeStruct(shape, dtype) for shape, dtype, memory in results],
        scratch_shapes=list(scratch),
        input_output_aliases=aliases or {},
        compiler_params=pltpu.CompilerParams(vmem_limit_bytes=VMEM_BYTES),
        cost_estimate=pl.CostEstimate(flops=flops, bytes_accessed=read, transcendentals=0),
    )(
        *[
            pltpu.with_memory_space_constraint(a, HBM) if memory is HBM and constrain else a
            for a, memory in operands
        ]
    )


def local(queries, key_vectors, value_vectors, log_decay, restart, norm_gain, upstream):
    tokens, width = queries.shape[1], queries.shape[2]
    state_rows = PAIRS * 64
    buffer_rows = state_rows + 8
    blocks = lax.axis_size("seq")
    scans = lax.axis_size("dp")
    position = lax.axis_index("seq")
    on_first = (position & 1) == 0

    def exchange(x, bit, axis="seq"):
        size = blocks if axis == "seq" else scans
        return lax.ppermute(x, axis, [(i, i ^ bit) for i in range(size)])

    def exchange_mixed(x, *bits):
        pairs = [
            (i * scans + j, (i ^ bits[i & 1][0]) * scans + (j ^ bits[i & 1][1]))
            for i in range(blocks)
            for j in range(scans)
        ]
        return lax.ppermute(x, ("seq", "dp"), pairs)

    def parts(buffer):
        state = buffer[:state_rows].reshape(PAIRS, 64, LANES)
        if buffer.shape[0] == state_rows:
            return state, None
        return state, buffer[state_rows : state_rows + PAIRS].reshape(PAIRS, 1, LANES)

    def joined(state, carry):
        return jnp.concatenate(
            [
                state.reshape(state_rows, LANES),
                carry.reshape(PAIRS, LANES),
                jnp.zeros((8 - PAIRS, LANES), F32),
            ],
            axis=0,
        )

    def flat(state):
        return state.reshape(state_rows, LANES)

    whole = (1, tokens, width)
    part = (tokens, width // 2)
    buffer = (buffer_rows, LANES)
    rows = (HEAD_TOTAL // 2, LANES)

    gain_rows = norm_gain.reshape(2 * PAIRS, LANES)

    state_other, tables, key_vectors, value_vectors = call(
        first_state_kernel,
        [
            (key_vectors, HBM),
            (value_vectors, HBM),
            (jnp.swapaxes(log_decay, 1, 2), HBM),
            (restart, HBM),
        ],
        [
            (buffer, F32, VMEM),
            ((TABLE_ROWS, LANES), F32, VMEM),
            (whole, BF16, VMEM),
            (whole, BF16, VMEM),
        ],
        [
            pltpu.VMEM((HEAD_TOTAL, tokens), F32),
            pltpu.VMEM((1, tokens), jnp.int32),
            pltpu.SemaphoreType.DMA((6,)),
        ],
        constrain=True,
    )
    blocks_of = [(queries, VMEM), (key_vectors, VMEM), (value_vectors, VMEM)]
    swapped = exchange(state_other, 1)
    state_own, mask = call(
        second_state_kernel,
        [(key_vectors, VMEM), (value_vectors, VMEM), (tables, VMEM)],
        [(buffer, F32, VMEM), ((tokens, tokens), F32, VMEM)],
    )
    first_state, first_carry = parts(jnp.where(on_first, state_own, swapped))
    second_state, second_carry = parts(jnp.where(on_first, swapped, state_own))
    total = second_carry * first_state + second_state
    carry = first_carry * second_carry
    prefix = jnp.zeros_like(total)
    prefix_carry = jnp.ones_like(carry)

    def mixture(mine, tables):
        return call(
            functools.partial(mixture_kernel, mine),
            blocks_of + [(upstream, VMEM), (gain_rows, VMEM), (tables, VMEM), (mask, VMEM)],
            [
                (part, F32, VMEM),
                ((width // 2, LANES), BF16, VMEM),
                (part, F32, VMEM),
                (part, F32, VMEM),
            ],
            flops=0,
        )

    mixed = {}
    levels = []
    bit = 2
    while bit < blocks:
        is_upper = (position & bit) != 0
        sent = flat(total) if 2 * bit == blocks else joined(total, carry)
        mine = not mixed
        if len(mixed) < 2:
            sent, tables = lax.optimization_barrier((sent, tables))
            mixed[mine] = mixture(mine, tables)
        received = exchange(sent, 2 * bit - 2)
        if len(levels) < 2:
            received, mixed[mine] = lax.optimization_barrier((received, mixed[mine]))
        theirs, their_carry = parts(received)
        prefix = jnp.where(is_upper, prefix_carry * theirs + prefix, prefix)
        levels.append((bit, is_upper, carry, their_carry))
        if their_carry is None:
            break
        prefix_carry = jnp.where(is_upper, prefix_carry * their_carry, prefix_carry)
        total = jnp.where(is_upper, carry * theirs + total, their_carry * total + theirs)
        carry = carry * their_carry
        bit *= 2
    for mine in (True, False):
        if mine not in mixed:
            mixed[mine] = mixture(mine, tables)
    after_first = first_carry * prefix + first_state
    state_in = {True: flat(jnp.where(on_first, prefix, after_first))}
    state_in[False] = exchange(flat(jnp.where(on_first, after_first, prefix)), 1)

    layer_parts, grad_mixed, query_states = {}, {}, {}
    for mine in (True, False):
        operands = [
            *[(x, VMEM) for x in mixed[mine][:4]],
            (queries, VMEM),
            (upstream, VMEM),
            (gain_rows, VMEM),
            (state_in[mine], VMEM),
        ]
        if mine:
            kernel = lambda *refs: forward_kernel(True, *refs[:8], None, *refs[8:])
        else:
            operands.append((query_states[True], VMEM))
            kernel = functools.partial(forward_kernel, False)
        layer_parts[mine], grad_mixed[mine], query_states[mine] = call(
            kernel, operands, [(part, BF16, VMEM), (part, BF16, VMEM), (buffer, F32, VMEM)]
        )

    def backward(mine, state):
        operands = blocks_of + [
            (grad_mixed[mine], VMEM),
            (state, VMEM),
            (mixed[mine][2], VMEM),
            (tables, VMEM),
            (mask, VMEM),
        ]
        results = [
            (part, BF16, VMEM),
            (part, F32, VMEM),
            (part, F32, VMEM),
            (rows, F32, VMEM),
            (part, F32, VMEM),
        ]
        if mine:
            return call(functools.partial(backward_kernel, True), operands, results)
        return call(
            other_backward_kernel,
            operands + [(layer_parts[x], VMEM) for x in (True, False)],
            [(whole, BF16, HBM)] + results,
            [pltpu.SemaphoreType.DMA((2,))],
        )

    steps = []
    step = scans // 2
    while step:
        steps.append(step)
        step //= 2
    swapped = exchange(query_states[False], 1)
    chip_gain = query_states[False][state_rows:] + swapped[state_rows:]
    gains = [jnp.where(on_first, chip_gain, 0.0)]
    first_query, _ = parts(jnp.where(on_first, query_states[True], swapped))
    second_query, _ = parts(jnp.where(on_first, swapped, query_states[True]))
    total = flat(first_query + first_carry * second_query)
    suffix = jnp.zeros_like(first_query)
    suffix_carry = jnp.ones_like(carry)
    local_parts = {}
    if len(levels) == 2 and scans == 4:
        total, chip_gain = lax.optimization_barrier((total, chip_gain))
        received = exchange(jnp.concatenate([total, chip_gain], axis=0), 2)
        fetched = [
            exchange_mixed(chip_gain, *bits)
            for bits in (((0, 1), (0, 3)), ((0, 2), (2, 2)), ((2, 3), (2, 1)))
        ]
        bit, is_upper, carry, their_carry = levels[0]
        near = parts(received)[0]
        own_query = parts(total)[0]
        total = flat(jnp.where(is_upper, near + their_carry * own_query, own_query + carry * near))
        gain = jnp.where(on_first, chip_gain + received[state_rows:], 0.0) + sum(fetched)
        total, state = lax.optimization_barrier((total, state_in[False]))
        received = exchange(total, 6)
        others = exchange(gain, 6)
        local_parts[True] = backward(True, state_in[True])
        local_parts[False] = backward(False, state)
        received, others, local_parts = lax.optimization_barrier((received, others, local_parts))
        gains = [gain, others]
        first_level, (bit, is_last, carry, their_carry) = levels
        far = parts(received)[0]
        suffix = jnp.where(
            is_last,
            jnp.where(is_upper, 0.0, near),
            jnp.where(is_upper, far, near + first_level[3] * far),
        )
        levels = []
    for bit, is_upper, carry, their_carry in levels:
        partner = 2 * bit - 2
        mine = not local_parts
        beside = len(local_parts) < 2
        if bit == 2:
            total, state = lax.optimization_barrier((total, state_in[mine]))
            received = exchange(total, partner)
            gain = sum(gains)
            for step in steps:
                gains = [gain, exchange(gain, step, "dp")]
                gain = sum(gains)
            if len(levels) == 1:
                gains = [gain, exchange(gain, partner)]
        else:
            total, gain, state = lax.optimization_barrier((total, sum(gains), state_in[mine]))
            received = exchange(jnp.concatenate([total, gain], axis=0), partner)
            gains = [gain]
            if 2 * bit == blocks:
                gains += [exchange(gain, 2), exchange(gain, partner ^ 2)]
        if beside:
            local_parts[mine] = backward(mine, state)
            received, gains, local_parts[mine] = lax.optimization_barrier(
                (received, gains, local_parts[mine])
            )
        if bit > 2:
            gains.append(received[state_rows:])
        theirs, _ = parts(received)
        total = parts(total)[0]
        suffix = jnp.where(is_upper, suffix, suffix_carry * theirs + suffix)
        if their_carry is None:
            break
        suffix_carry = jnp.where(is_upper, suffix_carry, suffix_carry * their_carry)
        total = flat(jnp.where(is_upper, theirs + their_carry * total, total + carry * theirs))
    for mine in (True, False):
        if mine not in local_parts:
            local_parts[mine] = backward(mine, state_in[mine])
    if blocks == 2:
        gain = sum(gains)
        for step in steps:
            gain = gain + exchange(gain, step, "dp")
        gains = [gain]
    before_second = second_query + second_carry * suffix
    state_grad = {True: flat(jnp.where(on_first, before_second, suffix))}
    gain = sum(gains)
    swapped = exchange(
        jnp.concatenate([flat(jnp.where(on_first, suffix, before_second)), gain], axis=0), 1
    )
    state_grad[False] = swapped

    def final_operands(mine):
        grad_key_part, grad_value_part, later, leave = local_parts[mine][-4:]
        return [
            (x, VMEM)
            for x in (
                key_vectors,
                value_vectors,
                grad_key_part,
                grad_value_part,
                later,
                leave,
                state_in[mine],
                state_grad[mine],
                tables,
            )
        ]

    grad_key, grad_value, decay_rows = call(
        own_final_kernel,
        final_operands(True),
        [(part, BF16, VMEM), (part, BF16, VMEM), (rows, F32, VMEM)],
    )
    finished = [local_parts[mine][-5] for mine in (True, False)]
    finished += [grad_key, grad_value, decay_rows, gain]
    grad_query, grad_key, grad_value, grad_decay, grad_gain = call(
        other_final_kernel,
        final_operands(False) + [(x, VMEM) for x in finished],
        [
            (whole, BF16, HBM),
            (whole, BF16, HBM),
            (whole, BF16, HBM),
            ((1, HEAD_TOTAL, tokens), F32, HBM),
            ((2 * PAIRS, LANES), F32, HBM),
        ],
        [
            pltpu.VMEM(part, BF16),
            pltpu.VMEM(part, BF16),
            pltpu.VMEM((HEAD_TOTAL, tokens), F32),
            pltpu.VMEM((2 * PAIRS, LANES), F32),
            pltpu.SemaphoreType.DMA((8,)),
        ],
    )
    return (
        local_parts[False][0],
        grad_query,
        grad_key,
        grad_value,
        jnp.swapaxes(grad_decay, 1, 2),
        grad_gain.reshape(-1),
    )


def solution(mesh):
    rows = P("dp", "seq", None)
    return jax.shard_map(
        local,
        mesh=mesh,
        in_specs=(rows, rows, rows, rows, P("dp", "seq"), P(), rows),
        out_specs=(rows, rows, rows, rows, rows, P()),
        check_vma=False,
    )
```

```python
import functools

import jax
import jax.numpy as jnp
from jax import lax
from jax.experimental import pallas as pl
from jax.experimental.pallas import tpu as pltpu
from jax.sharding import PartitionSpec as P

HEAD_TOTAL = 16
EPSILON = 1e-06
LANES = 128
PAIRS = HEAD_TOTAL // 4
VMEM_BYTES = 12 * 1024 * 1024
F32 = jnp.float32
BF16 = jnp.bfloat16
COLUMNS, CUM_ROWS, CARRY_ROWS, RESET_ROWS, TABLE_ROWS = 0, 128, 144, 160, 168


def dot(a, b, contract_a=1, contract_b=0):
    return lax.dot_general(
        a, b, (((contract_a,), (contract_b,)), ((), ())), preferred_element_type=F32
    )


def halves(x):
    high = x.astype(BF16)
    return high, (x - high.astype(F32)).astype(BF16)


def stacked(x, axis):
    return jnp.concatenate(halves(x), axis=axis)


def twice(x, axis):
    return jnp.concatenate([x, x], axis=axis)


def left_lanes(shape):
    return lax.broadcasted_iota(jnp.int32, shape, 1) < LANES // 2


def triangle(tokens, keep):
    rows = lax.broadcasted_iota(jnp.int32, (tokens, tokens), 0)
    columns = lax.broadcasted_iota(jnp.int32, (tokens, tokens), 1)
    return keep(rows, columns)


def by_head(x, axis):
    left = left_lanes(x.shape)
    zero = jnp.zeros_like(x)
    return jnp.concatenate([jnp.where(left, x, zero), jnp.where(left, zero, x)], axis=axis)


def fold(x):
    rows = x.shape[0] // 2
    return jnp.where(left_lanes((rows, LANES)), x[:rows], x[rows:])


def pair_columns(table, first, tokens):
    return jnp.where(
        left_lanes((tokens, LANES)),
        jnp.broadcast_to(table[:, first : first + 1], (tokens, LANES)),
        jnp.broadcast_to(table[:, first + 1 : first + 2], (tokens, LANES)),
    )


def make_tables(decay_rows, restart):
    heads, tokens = decay_rows.shape
    marks = jnp.broadcast_to(restart.astype(F32), (8, tokens))
    sums = row_sums(
        jnp.concatenate([decay_rows, marks], axis=0), triangle(tokens, lambda s, t: s <= t)
    )
    cum, resets = sums[:heads], sums[heads:]
    last, last_reset = cum[:, tokens - 1 :], resets[:1, tokens - 1 :]
    entry = jnp.where(resets[:1] == 0.0, jnp.exp(cum), 0.0)
    leave = jnp.where(resets[:1] == last_reset, jnp.exp(last - cum), 0.0)
    carry = jnp.where(last_reset == 0.0, jnp.exp(last), 0.0)
    rows = [cum, entry, leave, resets]
    rows.append(jnp.zeros((LANES - sum(x.shape[0] for x in rows), tokens), F32))
    columns = jnp.transpose(jnp.concatenate(rows, axis=0))
    return columns, cum, jnp.broadcast_to(carry, (heads, LANES)), resets


def make_mask(columns, resets):
    tokens = columns.shape[0]
    column = jnp.broadcast_to(columns[:, 3 * HEAD_TOTAL : 3 * HEAD_TOTAL + 1], (tokens, tokens))
    allowed = triangle(tokens, lambda t, s: t >= s) & (column == resets[:1])
    return jnp.where(allowed, 0.0, -1e30)


def pick_columns(columns, half):
    return jnp.where(half == 0, columns, pltpu.roll(columns, LANES - HEAD_TOTAL // 2, 1))


def pick_rows(rows, half):
    count = HEAD_TOTAL // 2
    return jnp.where(half == 0, rows[:count], rows[count:])


def own_half(mine):
    core = lax.axis_index("seq") & 1
    return core if mine else 1 - core


def half_lanes(half, width):
    return pl.ds(pl.multiple_of(half * (width // 2), LANES), width // 2)


def pair_lanes(half, width, pair):
    return pl.ds(pl.multiple_of(half * (width // 2) + pair * LANES, LANES), LANES)


def once(half, work):
    def step(i, carry):
        work()
        return carry

    lax.fori_loop(0, 1 + (half >> 1), step, 0)


def write_states(half, columns, carry_rows, keys, values, out_ref):
    tokens = keys.shape[0]
    table = pick_columns(columns, half)
    carry = pick_rows(carry_rows, half)
    left = left_lanes((1, LANES))
    scaled = []
    for pair in range(PAIRS):
        leave = pair_columns(table, 2 * HEAD_TOTAL + 2 * pair, tokens)
        lanes = slice(pair * LANES, (pair + 1) * LANES)
        scaled.append(stacked(values[:, lanes].astype(F32) * leave, 1))
    states = []
    for pair in range(PAIRS):
        lanes = slice(pair * LANES, (pair + 1) * LANES)
        states.append(dot(keys[:, lanes], scaled[pair], 0, 0))
    rows = []
    for pair in range(PAIRS):
        out_ref[pl.ds(pair * 64, 64), :] = fold(states[pair][:, :LANES] + states[pair][:, LANES:])
        rows.append(jnp.where(left, carry[2 * pair : 2 * pair + 1], carry[2 * pair + 1 : 2 * pair + 2]))
    rows.append(jnp.zeros((8 - len(rows), LANES), F32))
    out_ref[pl.ds(PAIRS * 64, 8), :] = jnp.concatenate(rows, axis=0)


def first_state_kernel(
    key_ref,
    value_ref,
    decay_ref,
    restart_ref,
    out_ref,
    table_ref,
    keys_ref,
    values_ref,
    decays,
    restarts,
    arrived,
):
    half = own_half(False)
    width = key_ref.shape[2]
    lanes, later_lanes = half_lanes(half, width), half_lanes(own_half(True), width)
    decay_copy = pltpu.make_async_copy(decay_ref.at[0], decays, arrived.at[4])
    restart_copy = pltpu.make_async_copy(restart_ref, restarts, arrived.at[5])
    copies = [
        pltpu.make_async_copy(
            source.at[0, :, place], target.at[0, :, place], arrived.at[2 * first + i]
        )
        for first, place in enumerate((lanes, later_lanes))
        for i, (source, target) in enumerate(((value_ref, values_ref), (key_ref, keys_ref)))
    ]
    decay_copy.start()
    restart_copy.start()
    for copy in copies:
        copy.start()
    decay_copy.wait()
    restart_copy.wait()
    columns, cum_rows, carry_rows, reset_rows = make_tables(decays[...], restarts[...])
    table_ref[pl.ds(COLUMNS, 128), :] = columns
    table_ref[pl.ds(CUM_ROWS, 16), :] = cum_rows
    table_ref[pl.ds(CARRY_ROWS, 16), :] = carry_rows
    table_ref[pl.ds(RESET_ROWS, 8), :] = reset_rows
    for copy in copies[:2]:
        copy.wait()
    write_states(
        half, columns, carry_rows, keys_ref[0, :, lanes], values_ref[0, :, lanes], out_ref
    )
    for copy in copies[2:]:
        copy.wait()


def second_state_kernel(key_ref, value_ref, table_ref, out_ref, mask_ref):
    half = own_half(True)
    lanes = half_lanes(half, key_ref.shape[2])
    write_states(
        half,
        table_ref[pl.ds(COLUMNS, 128), :],
        table_ref[pl.ds(CARRY_ROWS, 16), :],
        key_ref[0, :, lanes],
        value_ref[0, :, lanes],
        out_ref,
    )
    mask_ref[...] = make_mask(
        table_ref[pl.ds(COLUMNS, 128), :], table_ref[pl.ds(RESET_ROWS, 8), :]
    )


def pair_decays(table, cum_rows, mask, pair, tokens):
    parts = []
    for head in (2 * pair, 2 * pair + 1):
        column = jnp.broadcast_to(table[:, head : head + 1], (tokens, tokens))
        parts.append(jnp.exp(column - cum_rows[head : head + 1] + mask))
    return jnp.concatenate(parts, axis=1)


def one_above_other(x):
    columns = x.shape[1] // 2
    return jnp.concatenate([x[:, :columns], x[:, columns:]], axis=0)


def pick_gains(gain_ref, half):
    return jnp.where(half == 0, gain_ref[:PAIRS, :], gain_ref[PAIRS:, :])


def mixture_kernel(
    mine,
    query_ref,
    key_ref,
    value_ref,
    upstream_ref,
    gain_ref,
    table_ref,
    mask_ref,
    out_ref,
    turned_ref,
    entry_ref,
    grad_ref,
):
    tokens, width = query_ref.shape[1:]
    half = own_half(mine)
    table = pick_columns(table_ref[pl.ds(COLUMNS, 128), :], half)
    cum_rows = pick_rows(table_ref[pl.ds(CUM_ROWS, 16), :], half)
    mask = mask_ref[...]
    gains = pick_gains(gain_ref, half)
    for pair in range(PAIRS):
        lanes = pair_lanes(half, width, pair)
        query = query_ref[0, :, lanes]
        decay = pair_decays(table, cum_rows, mask, pair, tokens)
        scores = dot(query, by_head(key_ref[0, :, lanes], 0), 1, 1) * decay
        weights = scores.astype(BF16)
        here = pl.ds(pair * LANES, LANES)
        grad_ref[:, here] = upstream_ref[0, :, lanes].astype(F32) * gains[pair : pair + 1]
        out_ref[:, here] = dot(weights, by_head(value_ref[0, :, lanes], 0))
        turned_ref[here, :] = jnp.transpose(query)
        entry_ref[:, here] = pair_columns(table, HEAD_TOTAL + 2 * pair, tokens)


def forward_kernel(
    mine,
    mixed_ref,
    turned_ref,
    entry_ref,
    grad_ref,
    query_ref,
    upstream_ref,
    gain_ref,
    state_ref,
    before_ref,
    layer_ref,
    grad_mixed_ref,
    out_ref,
):
    tokens, width = query_ref.shape[1:]
    half = own_half(mine)
    gains = pick_gains(gain_ref, half)
    own = left_lanes((LANES, LANES)) == (lax.broadcasted_iota(jnp.int32, (LANES, LANES), 0) < 64)
    average = twice(jnp.where(own, 1.0 / 64.0, 0.0).astype(BF16), 0)
    places = [pl.ds(pair * LANES, LANES) for pair in range(PAIRS)]
    lanes = [pair_lanes(half, width, pair) for pair in range(PAIRS)]
    states = [
        stacked(by_head(state_ref[pl.ds(pair * 64, 64), :], 0), 0) for pair in range(PAIRS)
    ]
    carried = [
        dot(twice(query_ref[0, :, lanes[pair]], 1), states[pair]) for pair in range(PAIRS)
    ]
    mixtures = [
        mixed_ref[:, places[pair]] + entry_ref[:, places[pair]] * carried[pair]
        for pair in range(PAIRS)
    ]
    squares = dot(
        jnp.concatenate([stacked(mixture * mixture, 1) for mixture in mixtures], axis=0), average
    )
    normeds, inverses, grads, products, gain_parts = [], [], [], [], []
    for pair in range(PAIRS):
        inverse = lax.rsqrt(squares[pair * tokens : (pair + 1) * tokens] + EPSILON)
        normed = mixtures[pair] * inverse
        gain = gains[pair : pair + 1]
        upstream = upstream_ref[0, :, lanes[pair]].astype(F32)
        grad_normed = grad_ref[:, places[pair]]
        products.append(stacked(grad_normed * normed, 1))
        layer_ref[:, places[pair]] = (normed * gain).astype(BF16)
        gain_parts.append(jnp.sum(upstream * normed, axis=0, keepdims=True))
        normeds.append(normed)
        inverses.append(inverse)
        grads.append(grad_normed)
    shared = dot(jnp.concatenate(products, axis=0), average)
    sides = []
    for pair in range(PAIRS):
        part = shared[pair * tokens : (pair + 1) * tokens]
        grad_mixed = (inverses[pair] * (grads[pair] - normeds[pair] * part)).astype(BF16)
        grad_mixed_ref[:, places[pair]] = grad_mixed
        sides.append(stacked(entry_ref[:, places[pair]] * grad_mixed.astype(F32), 1))
    for pair in range(PAIRS):
        both = dot(turned_ref[places[pair], :], sides[pair])
        out_ref[pl.ds(pair * 64, 64), :] = fold(both[:, :LANES] + both[:, LANES:])
    part = jnp.concatenate(gain_parts, axis=0)
    blank = jnp.zeros_like(part)
    part = jnp.where(
        half == 0,
        jnp.concatenate([part, blank], axis=0),
        jnp.concatenate([blank, part], axis=0),
    )
    if before_ref is not None:
        part = part + before_ref[pl.ds(PAIRS * 64, 2 * PAIRS), :]
    out_ref[pl.ds(PAIRS * 64, 2 * PAIRS), :] = part


def backward_kernel(
    mine,
    query_ref,
    key_ref,
    value_ref,
    grad_mixed_ref,
    state_ref,
    entry_ref,
    table_ref,
    mask_ref,
    grad_query_ref,
    grad_key_ref,
    grad_value_ref,
    later_ref,
    leave_ref,
):
    tokens, width = query_ref.shape[1:]
    half = own_half(mine)
    table = pick_columns(table_ref[pl.ds(COLUMNS, 128), :], half)
    cum_rows = pick_rows(table_ref[pl.ds(CUM_ROWS, 16), :], half)
    mask = mask_ref[...]
    earlier = twice(triangle(tokens, lambda s, t: s < t).astype(F32).astype(BF16), 0)
    reached = triangle(tokens, lambda u, t: u >= t)
    chooser = twice(head_chooser(), 1)
    places = [pl.ds(pair * LANES, LANES) for pair in range(PAIRS)]
    lanes = [pair_lanes(half, width, pair) for pair in range(PAIRS)]
    balance_rows, entry_rows, carried = [], [], []
    for pair in range(PAIRS):
        state = by_head(state_ref[pl.ds(pair * 64, 64), :], 0)
        grad_mixed = grad_mixed_ref[:, places[pair]]
        carried.append(
            entry_ref[:, places[pair]] * dot(twice(grad_mixed, 1), stacked(state, 1), 1, 1)
        )
        leave_ref[:, places[pair]] = pair_columns(table, 2 * HEAD_TOTAL + 2 * pair, tokens)
    for pair in range(PAIRS):
        query = query_ref[0, :, lanes[pair]]
        grad_mixed = grad_mixed_ref[:, places[pair]]
        key_rows = by_head(key_ref[0, :, lanes[pair]], 0)
        decay = pair_decays(table, cum_rows, mask, pair, tokens)
        decayed_scores = dot(query, key_rows, 1, 1) * decay
        grad_pairs = dot(grad_mixed, by_head(value_ref[0, :, lanes[pair]], 0), 1, 1)
        weights = decayed_scores.astype(BF16)
        grad_weights = (grad_pairs * decay).astype(BF16)
        grad_query_ref[:, places[pair]] = (dot(grad_weights, key_rows) + carried[pair]).astype(
            BF16
        )
        grad_key_ref[:, places[pair]] = dot(
            one_above_other(grad_weights), by_head(query, 0), 0, 0
        )
        grad_value_ref[:, places[pair]] = dot(
            one_above_other(weights), by_head(grad_mixed, 0), 0, 0
        )
        terms = one_above_other(decayed_scores * grad_pairs)
        before = dot(stacked(terms, 1), earlier)
        for head in range(2):
            part = before[head * tokens : (head + 1) * tokens]
            balance_rows.append(jnp.sum(jnp.where(reached, part, 0.0), axis=0, keepdims=True))
        entry_rows.append(dot(chooser, stacked(query.astype(F32) * carried[pair], 1), 1, 1)[:2])
    later_ref[...] = jnp.concatenate(balance_rows, axis=0) + row_sums(
        jnp.concatenate(entry_rows, axis=0), reached
    )


def other_backward_kernel(*refs):
    inputs, (layer_own, layer_other), layer_ref = refs[:8], refs[8:10], refs[10]
    *outs, sent = refs[11:]
    width = layer_ref.shape[2]
    half = own_half(False)
    own_lanes, lanes = half_lanes(own_half(True), width), half_lanes(half, width)
    copies = [
        pltpu.make_async_copy(source, target, sent.at[i])
        for i, (source, target) in enumerate(
            [
                (layer_own, layer_ref.at[0, :, own_lanes]),
                (layer_other, layer_ref.at[0, :, lanes]),
            ]
        )
    ]

    for copy in copies:
        copy.start()
    once(half, lambda: backward_kernel(False, *inputs, *outs))
    for copy in copies:
        copy.wait()


def head_chooser():
    rows = lax.broadcasted_iota(jnp.int32, (8, LANES), 0)
    left = left_lanes((8, LANES))
    chosen = ((rows == 0) & left) | ((rows == 1) & ~left)
    return jnp.where(chosen, 1.0, 0.0).astype(BF16)


def row_sums(rows, keep):
    first, second = halves(rows)
    third = (rows - first.astype(F32) - second.astype(F32)).astype(BF16)
    weight = jnp.where(keep, 1.0, 0.0).astype(BF16)
    return dot(
        jnp.concatenate([first, second, third], axis=1),
        jnp.concatenate([weight, weight, weight], axis=0),
    )


def final_parts(
    mine,
    key_ref,
    value_ref,
    grad_key_part_ref,
    grad_value_part_ref,
    later_ref,
    leave_ref,
    state_ref,
    grad_ref,
    table_ref,
    key_out,
    value_out,
):
    tokens, width = key_ref.shape[1:]
    half = own_half(mine)
    carry = pick_rows(table_ref[pl.ds(CARRY_ROWS, 16), :], half)
    chooser = twice(head_chooser(), 1)
    left = left_lanes((1, LANES))
    lanes = [pair_lanes(half, width, pair) for pair in range(PAIRS)]
    places = [pl.ds(pair * LANES, LANES) for pair in range(PAIRS)]
    grads = [halves(by_head(grad_ref[pl.ds(pair * 64, 64), :], 0)) for pair in range(PAIRS)]
    carried, terms = [], []
    for pair in range(PAIRS):
        carried.append(
            leave_ref[:, places[pair]]
            * dot(twice(key_ref[0, :, lanes[pair]], 1), jnp.concatenate(grads[pair], axis=0))
        )
    for pair in range(PAIRS):
        value_out[:, places[pair]] = (
            grad_value_part_ref[:, places[pair]] + carried[pair]
        ).astype(BF16)
        terms.append(stacked(carried[pair] * value_ref[0, :, lanes[pair]].astype(F32), 1))
    earlier = [dot(chooser, terms[pair], 1, 1)[:2] for pair in range(PAIRS)]
    key_parts = [
        dot(twice(value_ref[0, :, lanes[pair]], 1), jnp.concatenate(grads[pair], axis=1), 1, 1)
        for pair in range(PAIRS)
    ]
    through_rows = []
    for pair in range(PAIRS):
        block = pl.ds(pair * 64, 64)
        product = jnp.sum(grad_ref[block, :] * state_ref[block, :], axis=0, keepdims=True)
        for side in (left, ~left):
            through_rows.append(jnp.sum(jnp.where(side, product, 0.0), axis=1, keepdims=True))
    for pair in range(PAIRS):
        key_out[:, places[pair]] = (
            grad_key_part_ref[:, places[pair]] + leave_ref[:, places[pair]] * key_parts[pair]
        ).astype(BF16)
    return (
        later_ref[...]
        + row_sums(jnp.concatenate(earlier, axis=0), triangle(tokens, lambda u, t: u < t))
        + carry * jnp.concatenate(through_rows, axis=0)
    )


def own_final_kernel(*refs):
    *refs, rows_ref = refs
    rows_ref[...] = final_parts(True, *refs)


def other_final_kernel(*refs):
    inputs, done, (other_ref, gain_part_ref) = refs[:9], refs[9:13], refs[13:15]
    grad_query_ref, grad_key_ref, grad_value_ref, decay_ref, gain_ref = refs[15:20]
    *parts, decay_out, gain_out, sent = refs[20:]
    width = grad_key_ref.shape[2]
    half = own_half(False)
    own_lanes, lanes = half_lanes(own_half(True), width), half_lanes(half, width)
    pairs = [
        (done[0], grad_query_ref.at[0, :, own_lanes]),
        (done[1], grad_query_ref.at[0, :, lanes]),
        (done[2], grad_key_ref.at[0, :, own_lanes]),
        (done[3], grad_value_ref.at[0, :, own_lanes]),
        (gain_out, gain_ref),
        (parts[0], grad_key_ref.at[0, :, lanes]),
        (parts[1], grad_value_ref.at[0, :, lanes]),
        (decay_out, decay_ref.at[0]),
    ]
    copies = [
        pltpu.make_async_copy(source, target, sent.at[i])
        for i, (source, target) in enumerate(pairs)
    ]
    gain_out[...] = gain_part_ref[...] + inputs[7][pl.ds(PAIRS * 64, 2 * PAIRS), :]

    for copy in copies[:5]:
        copy.start()

    def work():
        rows = final_parts(False, *inputs, *parts)
        other = other_ref[...]
        decay_out[...] = jnp.where(
            half == 0,
            jnp.concatenate([rows, other], axis=0),
            jnp.concatenate([other, rows], axis=0),
        )

    once(half, work)
    for copy in copies[5:]:
        copy.start()
    for copy in copies:
        copy.wait()


VMEM, HBM = pltpu.VMEM, pltpu.HBM


def call(kernel, operands, results, scratch=(), aliases=None, flops=0, constrain=False):
    read = sum(a.size * a.dtype.itemsize for a, memory in operands if memory is VMEM)
    return pl.pallas_call(
        kernel,
        in_specs=[pl.BlockSpec(memory_space=memory) for a, memory in operands],
        out_specs=[pl.BlockSpec(memory_space=memory) for shape, dtype, memory in results],
        out_shape=[jax.ShapeDtypeStruct(shape, dtype) for shape, dtype, memory in results],
        scratch_shapes=list(scratch),
        input_output_aliases=aliases or {},
        compiler_params=pltpu.CompilerParams(vmem_limit_bytes=VMEM_BYTES),
        cost_estimate=pl.CostEstimate(flops=flops, bytes_accessed=read, transcendentals=0),
    )(
        *[
            pltpu.with_memory_space_constraint(a, HBM) if memory is HBM and constrain else a
            for a, memory in operands
        ]
    )


def local(queries, key_vectors, value_vectors, log_decay, restart, norm_gain, upstream):
    tokens, width = queries.shape[1], queries.shape[2]
    state_rows = PAIRS * 64
    buffer_rows = state_rows + 8
    blocks = lax.axis_size("seq")
    scans = lax.axis_size("dp")
    position = lax.axis_index("seq")
    on_first = (position & 1) == 0

    def exchange(x, bit, axis="seq"):
        size = blocks if axis == "seq" else scans
        return lax.ppermute(x, axis, [(i, i ^ bit) for i in range(size)])

    def exchange_mixed(x, *bits):
        pairs = [
            (i * scans + j, (i ^ bits[i & 1][0]) * scans + (j ^ bits[i & 1][1]))
            for i in range(blocks)
            for j in range(scans)
        ]
        return lax.ppermute(x, ("seq", "dp"), pairs)

    def exchange_by_core(x, first, second):
        bits = (first, second)
        return lax.ppermute(x, "seq", [(i, i ^ bits[i & 1]) for i in range(blocks)])

    def by_chip(*cases):
        return jnp.where(
            is_last,
            jnp.where(is_odd, cases[3], cases[2]),
            jnp.where(is_odd, cases[1], cases[0]),
        )

    four_chips = blocks == 8 and scans == 4
    is_last = (position & 4) != 0
    is_odd = (position & 2) != 0

    def parts(buffer):
        state = buffer[:state_rows].reshape(PAIRS, 64, LANES)
        if buffer.shape[0] == state_rows:
            return state, None
        return state, buffer[state_rows : state_rows + PAIRS].reshape(PAIRS, 1, LANES)

    def joined(state, carry):
        return jnp.concatenate(
            [
                state.reshape(state_rows, LANES),
                carry.reshape(PAIRS, LANES),
                jnp.zeros((8 - PAIRS, LANES), F32),
            ],
            axis=0,
        )

    def flat(state):
        return state.reshape(state_rows, LANES)

    whole = (1, tokens, width)
    part = (tokens, width // 2)
    buffer = (buffer_rows, LANES)
    rows = (HEAD_TOTAL // 2, LANES)

    gain_rows = norm_gain.reshape(2 * PAIRS, LANES)

    state_other, tables, key_vectors, value_vectors = call(
        first_state_kernel,
        [
            (key_vectors, HBM),
            (value_vectors, HBM),
            (jnp.swapaxes(log_decay, 1, 2), HBM),
            (restart, HBM),
        ],
        [
            (buffer, F32, VMEM),
            ((TABLE_ROWS, LANES), F32, VMEM),
            (whole, BF16, VMEM),
            (whole, BF16, VMEM),
        ],
        [
            pltpu.VMEM((HEAD_TOTAL, tokens), F32),
            pltpu.VMEM((1, tokens), jnp.int32),
            pltpu.SemaphoreType.DMA((6,)),
        ],
        constrain=True,
    )
    blocks_of = [(queries, VMEM), (key_vectors, VMEM), (value_vectors, VMEM)]
    swapped = exchange(state_other, 1)
    state_own, mask = call(
        second_state_kernel,
        [(key_vectors, VMEM), (value_vectors, VMEM), (tables, VMEM)],
        [(buffer, F32, VMEM), ((tokens, tokens), F32, VMEM)],
    )
    first_state, first_carry = parts(jnp.where(on_first, state_own, swapped))
    second_state, second_carry = parts(jnp.where(on_first, swapped, state_own))
    total = second_carry * first_state + second_state
    carry = first_carry * second_carry
    prefix = jnp.zeros_like(total)
    prefix_carry = jnp.ones_like(carry)

    def mixture(mine, tables):
        return call(
            functools.partial(mixture_kernel, mine),
            blocks_of + [(upstream, VMEM), (gain_rows, VMEM), (tables, VMEM), (mask, VMEM)],
            [
                (part, F32, VMEM),
                ((width // 2, LANES), BF16, VMEM),
                (part, F32, VMEM),
                (part, F32, VMEM),
            ],
            flops=0,
        )

    mixed = {}
    levels = []
    if four_chips:
        sent = joined(total, carry)
        sent, tables = lax.optimization_barrier((sent, tables))
        mixed[True] = mixture(True, tables)
        received = exchange_by_core(sent, 6, 2)
        received, mixed[True] = lax.optimization_barrier((received, mixed[True]))
        near, near_carry = parts(received)
        own_first = near_carry * total + near
        own_last = carry * near + total
        sent = jnp.where(
            on_first,
            by_chip(total, own_first, own_last, near),
            jnp.where(is_odd, own_last, own_first),
        )
        sent = joined(sent, carry * near_carry)
        sent, tables = lax.optimization_barrier((sent, tables))
        mixed[False] = mixture(False, tables)
        received = exchange_by_core(sent, 2, 6)
        received, mixed[False] = lax.optimization_barrier((received, mixed[False]))
        far, far_carry = parts(received)
        near_last = near_carry * far + near
        prefix = jnp.where(
            on_first,
            by_chip(0.0, far, near_last, far_carry * near + far),
            by_chip(0.0, near, far, near_last),
        )
    bit = 2
    while bit < blocks and not four_chips:
        is_upper = (position & bit) != 0
        sent = flat(total) if 2 * bit == blocks else joined(total, carry)
        mine = not mixed
        if len(mixed) < 2:
            sent, tables = lax.optimization_barrier((sent, tables))
            mixed[mine] = mixture(mine, tables)
        received = exchange(sent, 2 * bit - 2)
        if len(levels) < 2:
            received, mixed[mine] = lax.optimization_barrier((received, mixed[mine]))
        theirs, their_carry = parts(received)
        prefix = jnp.where(is_upper, prefix_carry * theirs + prefix, prefix)
        levels.append((bit, is_upper, carry, their_carry))
        if their_carry is None:
            break
        prefix_carry = jnp.where(is_upper, prefix_carry * their_carry, prefix_carry)
        total = jnp.where(is_upper, carry * theirs + total, their_carry * total + theirs)
        carry = carry * their_carry
        bit *= 2
    for mine in (True, False):
        if mine not in mixed:
            mixed[mine] = mixture(mine, tables)
    after_first = first_carry * prefix + first_state
    state_in = {True: flat(jnp.where(on_first, prefix, after_first))}
    state_in[False] = exchange(flat(jnp.where(on_first, after_first, prefix)), 1)

    layer_parts, grad_mixed, query_states = {}, {}, {}
    for mine in (True, False):
        operands = [
            *[(x, VMEM) for x in mixed[mine][:4]],
            (queries, VMEM),
            (upstream, VMEM),
            (gain_rows, VMEM),
            (state_in[mine], VMEM),
        ]
        if mine:
            kernel = lambda *refs: forward_kernel(True, *refs[:8], None, *refs[8:])
        else:
            operands.append((query_states[True], VMEM))
            kernel = functools.partial(forward_kernel, False)
        layer_parts[mine], grad_mixed[mine], query_states[mine] = call(
            kernel, operands, [(part, BF16, VMEM), (part, BF16, VMEM), (buffer, F32, VMEM)]
        )

    def backward(mine, state):
        operands = blocks_of + [
            (grad_mixed[mine], VMEM),
            (state, VMEM),
            (mixed[mine][2], VMEM),
            (tables, VMEM),
            (mask, VMEM),
        ]
        results = [
            (part, BF16, VMEM),
            (part, F32, VMEM),
            (part, F32, VMEM),
            (rows, F32, VMEM),
            (part, F32, VMEM),
        ]
        if mine:
            return call(functools.partial(backward_kernel, True), operands, results)
        return call(
            other_backward_kernel,
            operands + [(layer_parts[x], VMEM) for x in (True, False)],
            [(whole, BF16, HBM)] + results,
            [pltpu.SemaphoreType.DMA((2,))],
        )

    steps = []
    step = scans // 2
    while step:
        steps.append(step)
        step //= 2
    swapped = exchange(query_states[False], 1)
    chip_gain = query_states[False][state_rows:] + swapped[state_rows:]
    gains = [jnp.where(on_first, chip_gain, 0.0)]
    first_query, _ = parts(jnp.where(on_first, query_states[True], swapped))
    second_query, _ = parts(jnp.where(on_first, swapped, query_states[True]))
    total = flat(first_query + first_carry * second_query)
    suffix = jnp.zeros_like(first_query)
    suffix_carry = jnp.ones_like(carry)
    local_parts = {}
    if four_chips:
        total, chip_gain = lax.optimization_barrier((total, chip_gain))
        received = exchange_by_core(jnp.concatenate([total, chip_gain], axis=0), 6, 2)
        fetched = [
            exchange_mixed(chip_gain, *bits)
            for bits in (((0, 1), (0, 3)), ((0, 2), (2, 2)), ((2, 3), (2, 1)))
        ]
        near = parts(received)[0]
        own_query = parts(total)[0]
        own_first = own_query + carry * near
        total = flat(
            jnp.where(
                on_first,
                by_chip(near, own_first, own_query, own_query),
                jnp.where(is_odd, near + near_carry * own_query, own_first),
            )
        )
        gain = jnp.where(on_first, 0.0, chip_gain + received[state_rows:]) + sum(fetched)
        total, state = lax.optimization_barrier((total, state_in[False]))
        received = exchange_by_core(total, 2, 6)
        others = exchange(gain, 4)
        local_parts[True] = backward(True, state_in[True])
        local_parts[False] = backward(False, state)
        received, others, local_parts = lax.optimization_barrier((received, others, local_parts))
        gains = [gain, others]
        far = parts(received)[0]
        near_first = near + near_carry * far
        suffix = jnp.where(
            on_first,
            by_chip(far + far_carry * near, near_first, far, 0.0),
            by_chip(near_first, far, near, 0.0),
        )
    for bit, is_upper, carry, their_carry in levels:
        partner = 2 * bit - 2
        mine = not local_parts
        beside = len(local_parts) < 2
        if bit == 2:
            total, state = lax.optimization_barrier((total, state_in[mine]))
            received = exchange(total, partner)
            gain = sum(gains)
            for step in steps:
                gains = [gain, exchange(gain, step, "dp")]
                gain = sum(gains)
            if len(levels) == 1:
                gains = [gain, exchange(gain, partner)]
        else:
            total, gain, state = lax.optimization_barrier((total, sum(gains), state_in[mine]))
            received = exchange(jnp.concatenate([total, gain], axis=0), partner)
            gains = [gain]
            if 2 * bit == blocks:
                gains += [exchange(gain, 2), exchange(gain, partner ^ 2)]
        if beside:
            local_parts[mine] = backward(mine, state)
            received, gains, local_parts[mine] = lax.optimization_barrier(
                (received, gains, local_parts[mine])
            )
        if bit > 2:
            gains.append(received[state_rows:])
        theirs, _ = parts(received)
        total = parts(total)[0]
        suffix = jnp.where(is_upper, suffix, suffix_carry * theirs + suffix)
        if their_carry is None:
            break
        suffix_carry = jnp.where(is_upper, suffix_carry, suffix_carry * their_carry)
        total = flat(jnp.where(is_upper, theirs + their_carry * total, total + carry * theirs))
    for mine in (True, False):
        if mine not in local_parts:
            local_parts[mine] = backward(mine, state_in[mine])
    if blocks == 2:
        gain = sum(gains)
        for step in steps:
            gain = gain + exchange(gain, step, "dp")
        gains = [gain]
    before_second = second_query + second_carry * suffix
    state_grad = {True: flat(jnp.where(on_first, before_second, suffix))}
    gain = sum(gains)
    swapped = exchange(
        jnp.concatenate([flat(jnp.where(on_first, suffix, before_second)), gain], axis=0), 1
    )
    state_grad[False] = swapped

    def final_operands(mine):
        grad_key_part, grad_value_part, later, leave = local_parts[mine][-4:]
        return [
            (x, VMEM)
            for x in (
                key_vectors,
                value_vectors,
                grad_key_part,
                grad_value_part,
                later,
                leave,
                state_in[mine],
                state_grad[mine],
                tables,
            )
        ]

    grad_key, grad_value, decay_rows = call(
        own_final_kernel,
        final_operands(True),
        [(part, BF16, VMEM), (part, BF16, VMEM), (rows, F32, VMEM)],
    )
    finished = [local_parts[mine][-5] for mine in (True, False)]
    finished += [grad_key, grad_value, decay_rows, gain]
    grad_query, grad_key, grad_value, grad_decay, grad_gain = call(
        other_final_kernel,
        final_operands(False) + [(x, VMEM) for x in finished],
        [
            (whole, BF16, HBM),
            (whole, BF16, HBM),
            (whole, BF16, HBM),
            ((1, HEAD_TOTAL, tokens), F32, HBM),
            ((2 * PAIRS, LANES), F32, HBM),
        ],
        [
            pltpu.VMEM(part, BF16),
            pltpu.VMEM(part, BF16),
            pltpu.VMEM((HEAD_TOTAL, tokens), F32),
            pltpu.VMEM((2 * PAIRS, LANES), F32),
            pltpu.SemaphoreType.DMA((8,)),
        ],
    )
    return (
        local_parts[False][0],
        grad_query,
        grad_key,
        grad_value,
        jnp.swapaxes(grad_decay, 1, 2),
        grad_gain.reshape(-1),
    )


def solution(mesh):
    rows = P("dp", "seq", None)
    return jax.shard_map(
        local,
        mesh=mesh,
        in_specs=(rows, rows, rows, rows, P("dp", "seq"), P(), rows),
        out_specs=(rows, rows, rows, rows, rows, P()),
        check_vma=False,
    )
```

```python
import functools

import jax
import jax.numpy as jnp
from jax import lax
from jax.experimental import pallas as pl
from jax.experimental.pallas import tpu as pltpu
from jax.sharding import PartitionSpec as P

HEAD_TOTAL = 16
EPSILON = 1e-06
LANES = 128
PAIRS = HEAD_TOTAL // 4
VMEM_BYTES = 12 * 1024 * 1024
F32 = jnp.float32
BF16 = jnp.bfloat16
COLUMNS, CUM_ROWS, CARRY_ROWS, RESET_ROWS, TABLE_ROWS = 0, 128, 144, 160, 168


def dot(a, b, contract_a=1, contract_b=0):
    return lax.dot_general(
        a, b, (((contract_a,), (contract_b,)), ((), ())), preferred_element_type=F32
    )


def halves(x):
    high = x.astype(BF16)
    return high, (x - high.astype(F32)).astype(BF16)


def stacked(x, axis):
    return jnp.concatenate(halves(x), axis=axis)


def twice(x, axis):
    return jnp.concatenate([x, x], axis=axis)


def left_lanes(shape):
    return lax.broadcasted_iota(jnp.int32, shape, 1) < LANES // 2


def triangle(tokens, keep):
    rows = lax.broadcasted_iota(jnp.int32, (tokens, tokens), 0)
    columns = lax.broadcasted_iota(jnp.int32, (tokens, tokens), 1)
    return keep(rows, columns)


def by_head(x, axis):
    left = left_lanes(x.shape)
    zero = jnp.zeros_like(x)
    return jnp.concatenate([jnp.where(left, x, zero), jnp.where(left, zero, x)], axis=axis)


def fold(x):
    rows = x.shape[0] // 2
    return jnp.where(left_lanes((rows, LANES)), x[:rows], x[rows:])


def pair_columns(table, first, tokens):
    return jnp.where(
        left_lanes((tokens, LANES)),
        jnp.broadcast_to(table[:, first : first + 1], (tokens, LANES)),
        jnp.broadcast_to(table[:, first + 1 : first + 2], (tokens, LANES)),
    )


def make_tables(decay_rows, restart):
    heads, tokens = decay_rows.shape
    marks = jnp.broadcast_to(restart.astype(F32), (8, tokens))
    sums = row_sums(
        jnp.concatenate([decay_rows, marks], axis=0), triangle(tokens, lambda s, t: s <= t)
    )
    cum, resets = sums[:heads], sums[heads:]
    last, last_reset = cum[:, tokens - 1 :], resets[:1, tokens - 1 :]
    entry = jnp.where(resets[:1] == 0.0, jnp.exp(cum), 0.0)
    leave = jnp.where(resets[:1] == last_reset, jnp.exp(last - cum), 0.0)
    carry = jnp.where(last_reset == 0.0, jnp.exp(last), 0.0)
    rows = [cum, entry, leave, resets]
    rows.append(jnp.zeros((LANES - sum(x.shape[0] for x in rows), tokens), F32))
    columns = jnp.transpose(jnp.concatenate(rows, axis=0))
    return columns, cum, jnp.broadcast_to(carry, (heads, LANES)), resets


def make_mask(columns, resets):
    tokens = columns.shape[0]
    column = jnp.broadcast_to(columns[:, 3 * HEAD_TOTAL : 3 * HEAD_TOTAL + 1], (tokens, tokens))
    allowed = triangle(tokens, lambda t, s: t >= s) & (column == resets[:1])
    return jnp.where(allowed, 0.0, -1e30)


def pick_columns(columns, half):
    return jnp.where(half == 0, columns, pltpu.roll(columns, LANES - HEAD_TOTAL // 2, 1))


def pick_rows(rows, half):
    count = HEAD_TOTAL // 2
    return jnp.where(half == 0, rows[:count], rows[count:])


def own_half(mine):
    core = lax.axis_index("seq") & 1
    return core if mine else 1 - core


def half_lanes(half, width):
    return pl.ds(pl.multiple_of(half * (width // 2), LANES), width // 2)


def pair_lanes(half, width, pair):
    return pl.ds(pl.multiple_of(half * (width // 2) + pair * LANES, LANES), LANES)


def once(half, work):
    def step(i, carry):
        work()
        return carry

    lax.fori_loop(0, 1 + (half >> 1), step, 0)


def write_states(half, columns, carry_rows, keys, values, out_ref):
    tokens = keys.shape[0]
    table = pick_columns(columns, half)
    carry = pick_rows(carry_rows, half)
    left = left_lanes((1, LANES))
    scaled = []
    for pair in range(PAIRS):
        leave = pair_columns(table, 2 * HEAD_TOTAL + 2 * pair, tokens)
        lanes = slice(pair * LANES, (pair + 1) * LANES)
        scaled.append(stacked(values[:, lanes].astype(F32) * leave, 1))
    states = []
    for pair in range(PAIRS):
        lanes = slice(pair * LANES, (pair + 1) * LANES)
        states.append(dot(keys[:, lanes], scaled[pair], 0, 0))
    rows = []
    for pair in range(PAIRS):
        out_ref[pl.ds(pair * 64, 64), :] = fold(states[pair][:, :LANES] + states[pair][:, LANES:])
        rows.append(jnp.where(left, carry[2 * pair : 2 * pair + 1], carry[2 * pair + 1 : 2 * pair + 2]))
    rows.append(jnp.zeros((8 - len(rows), LANES), F32))
    out_ref[pl.ds(PAIRS * 64, 8), :] = jnp.concatenate(rows, axis=0)


def first_state_kernel(
    key_ref,
    value_ref,
    decay_ref,
    restart_ref,
    out_ref,
    table_ref,
    keys_ref,
    values_ref,
    decays,
    restarts,
    arrived,
):
    half = own_half(False)
    width = key_ref.shape[2]
    lanes, later_lanes = half_lanes(half, width), half_lanes(own_half(True), width)
    decay_copy = pltpu.make_async_copy(decay_ref.at[0], decays, arrived.at[4])
    restart_copy = pltpu.make_async_copy(restart_ref, restarts, arrived.at[5])
    copies = [
        pltpu.make_async_copy(
            source.at[0, :, place], target.at[0, :, place], arrived.at[2 * first + i]
        )
        for first, place in enumerate((lanes, later_lanes))
        for i, (source, target) in enumerate(((value_ref, values_ref), (key_ref, keys_ref)))
    ]
    decay_copy.start()
    restart_copy.start()
    for copy in copies:
        copy.start()
    decay_copy.wait()
    restart_copy.wait()
    columns, cum_rows, carry_rows, reset_rows = make_tables(decays[...], restarts[...])
    table_ref[pl.ds(COLUMNS, 128), :] = columns
    table_ref[pl.ds(CUM_ROWS, 16), :] = cum_rows
    table_ref[pl.ds(CARRY_ROWS, 16), :] = carry_rows
    table_ref[pl.ds(RESET_ROWS, 8), :] = reset_rows
    for copy in copies[:2]:
        copy.wait()
    write_states(
        half, columns, carry_rows, keys_ref[0, :, lanes], values_ref[0, :, lanes], out_ref
    )
    for copy in copies[2:]:
        copy.wait()


def second_state_kernel(key_ref, value_ref, table_ref, out_ref, mask_ref):
    half = own_half(True)
    lanes = half_lanes(half, key_ref.shape[2])
    write_states(
        half,
        table_ref[pl.ds(COLUMNS, 128), :],
        table_ref[pl.ds(CARRY_ROWS, 16), :],
        key_ref[0, :, lanes],
        value_ref[0, :, lanes],
        out_ref,
    )
    mask_ref[...] = make_mask(
        table_ref[pl.ds(COLUMNS, 128), :], table_ref[pl.ds(RESET_ROWS, 8), :]
    )


def pair_decays(table, cum_rows, mask, pair, tokens):
    parts = []
    for head in (2 * pair, 2 * pair + 1):
        column = jnp.broadcast_to(table[:, head : head + 1], (tokens, tokens))
        parts.append(jnp.exp(column - cum_rows[head : head + 1] + mask))
    return jnp.concatenate(parts, axis=1)


def one_above_other(x):
    columns = x.shape[1] // 2
    return jnp.concatenate([x[:, :columns], x[:, columns:]], axis=0)


def pick_gains(gain_ref, half):
    return jnp.where(half == 0, gain_ref[:PAIRS, :], gain_ref[PAIRS:, :])


def mixture_kernel(
    mine,
    query_ref,
    key_ref,
    value_ref,
    upstream_ref,
    gain_ref,
    table_ref,
    mask_ref,
    out_ref,
    turned_ref,
    entry_ref,
    grad_ref,
):
    tokens, width = query_ref.shape[1:]
    half = own_half(mine)
    table = pick_columns(table_ref[pl.ds(COLUMNS, 128), :], half)
    cum_rows = pick_rows(table_ref[pl.ds(CUM_ROWS, 16), :], half)
    mask = mask_ref[...]
    gains = pick_gains(gain_ref, half)
    for pair in range(PAIRS):
        lanes = pair_lanes(half, width, pair)
        query = query_ref[0, :, lanes]
        decay = pair_decays(table, cum_rows, mask, pair, tokens)
        scores = dot(query, by_head(key_ref[0, :, lanes], 0), 1, 1) * decay
        weights = scores.astype(BF16)
        here = pl.ds(pair * LANES, LANES)
        grad_ref[:, here] = upstream_ref[0, :, lanes].astype(F32) * gains[pair : pair + 1]
        out_ref[:, here] = dot(weights, by_head(value_ref[0, :, lanes], 0))
        turned_ref[here, :] = jnp.transpose(query)
        entry_ref[:, here] = pair_columns(table, HEAD_TOTAL + 2 * pair, tokens)


def forward_kernel(
    mine,
    mixed_ref,
    turned_ref,
    entry_ref,
    grad_ref,
    query_ref,
    upstream_ref,
    gain_ref,
    state_ref,
    before_ref,
    layer_ref,
    grad_mixed_ref,
    out_ref,
):
    tokens, width = query_ref.shape[1:]
    half = own_half(mine)
    gains = pick_gains(gain_ref, half)
    own = left_lanes((LANES, LANES)) == (lax.broadcasted_iota(jnp.int32, (LANES, LANES), 0) < 64)
    average = jnp.where(own, 1.0 / 64.0, 0.0).astype(BF16)
    places = [pl.ds(pair * LANES, LANES) for pair in range(PAIRS)]
    lanes = [pair_lanes(half, width, pair) for pair in range(PAIRS)]
    states = [
        stacked(by_head(state_ref[pl.ds(pair * 64, 64), :], 0), 0) for pair in range(PAIRS)
    ]
    carried = [
        dot(twice(query_ref[0, :, lanes[pair]], 1), states[pair]) for pair in range(PAIRS)
    ]
    mixtures = [
        mixed_ref[:, places[pair]] + entry_ref[:, places[pair]] * carried[pair]
        for pair in range(PAIRS)
    ]
    squares = dot(
        jnp.concatenate([(mixture * mixture).astype(BF16) for mixture in mixtures], axis=0), average
    )
    normeds, inverses, grads, products, gain_parts = [], [], [], [], []
    for pair in range(PAIRS):
        inverse = lax.rsqrt(squares[pair * tokens : (pair + 1) * tokens] + EPSILON)
        normed = mixtures[pair] * inverse
        gain = gains[pair : pair + 1]
        upstream = upstream_ref[0, :, lanes[pair]].astype(F32)
        grad_normed = grad_ref[:, places[pair]]
        products.append((grad_normed * normed).astype(BF16))
        layer_ref[:, places[pair]] = (normed * gain).astype(BF16)
        gain_parts.append(jnp.sum(upstream * normed, axis=0, keepdims=True))
        normeds.append(normed)
        inverses.append(inverse)
        grads.append(grad_normed)
    shared = dot(jnp.concatenate(products, axis=0), average)
    sides = []
    for pair in range(PAIRS):
        part = shared[pair * tokens : (pair + 1) * tokens]
        grad_mixed = (inverses[pair] * (grads[pair] - normeds[pair] * part)).astype(BF16)
        grad_mixed_ref[:, places[pair]] = grad_mixed
        sides.append(stacked(entry_ref[:, places[pair]] * grad_mixed.astype(F32), 1))
    for pair in range(PAIRS):
        both = dot(turned_ref[places[pair], :], sides[pair])
        out_ref[pl.ds(pair * 64, 64), :] = fold(both[:, :LANES] + both[:, LANES:])
    part = jnp.concatenate(gain_parts, axis=0)
    blank = jnp.zeros_like(part)
    part = jnp.where(
        half == 0,
        jnp.concatenate([part, blank], axis=0),
        jnp.concatenate([blank, part], axis=0),
    )
    if before_ref is not None:
        part = part + before_ref[pl.ds(PAIRS * 64, 2 * PAIRS), :]
    out_ref[pl.ds(PAIRS * 64, 2 * PAIRS), :] = part


def backward_kernel(
    mine,
    query_ref,
    key_ref,
    value_ref,
    grad_mixed_ref,
    state_ref,
    entry_ref,
    table_ref,
    mask_ref,
    grad_query_ref,
    grad_key_ref,
    grad_value_ref,
    later_ref,
    leave_ref,
):
    tokens, width = query_ref.shape[1:]
    half = own_half(mine)
    table = pick_columns(table_ref[pl.ds(COLUMNS, 128), :], half)
    cum_rows = pick_rows(table_ref[pl.ds(CUM_ROWS, 16), :], half)
    mask = mask_ref[...]
    earlier = twice(triangle(tokens, lambda s, t: s < t).astype(F32).astype(BF16), 0)
    reached = triangle(tokens, lambda u, t: u >= t)
    chooser = twice(head_chooser(), 1)
    places = [pl.ds(pair * LANES, LANES) for pair in range(PAIRS)]
    lanes = [pair_lanes(half, width, pair) for pair in range(PAIRS)]
    balance_rows, entry_rows, carried = [], [], []
    for pair in range(PAIRS):
        state = by_head(state_ref[pl.ds(pair * 64, 64), :], 0)
        grad_mixed = grad_mixed_ref[:, places[pair]]
        carried.append(
            entry_ref[:, places[pair]] * dot(twice(grad_mixed, 1), stacked(state, 1), 1, 1)
        )
        leave_ref[:, places[pair]] = pair_columns(table, 2 * HEAD_TOTAL + 2 * pair, tokens)
    for pair in range(PAIRS):
        query = query_ref[0, :, lanes[pair]]
        grad_mixed = grad_mixed_ref[:, places[pair]]
        key_rows = by_head(key_ref[0, :, lanes[pair]], 0)
        decay = pair_decays(table, cum_rows, mask, pair, tokens)
        decayed_scores = dot(query, key_rows, 1, 1) * decay
        grad_pairs = dot(grad_mixed, by_head(value_ref[0, :, lanes[pair]], 0), 1, 1)
        weights = decayed_scores.astype(BF16)
        grad_weights = (grad_pairs * decay).astype(BF16)
        grad_query_ref[:, places[pair]] = (dot(grad_weights, key_rows) + carried[pair]).astype(
            BF16
        )
        grad_key_ref[:, places[pair]] = dot(
            one_above_other(grad_weights), by_head(query, 0), 0, 0
        )
        grad_value_ref[:, places[pair]] = dot(
            one_above_other(weights), by_head(grad_mixed, 0), 0, 0
        )
        terms = one_above_other(decayed_scores * grad_pairs)
        before = dot(stacked(terms, 1), earlier)
        for head in range(2):
            part = before[head * tokens : (head + 1) * tokens]
            balance_rows.append(jnp.sum(jnp.where(reached, part, 0.0), axis=0, keepdims=True))
        entry_rows.append(dot(chooser, stacked(query.astype(F32) * carried[pair], 1), 1, 1)[:2])
    later_ref[...] = jnp.concatenate(balance_rows, axis=0) + row_sums(
        jnp.concatenate(entry_rows, axis=0), reached
    )


def other_backward_kernel(*refs):
    inputs, (layer_own, layer_other), layer_ref = refs[:8], refs[8:10], refs[10]
    *outs, sent = refs[11:]
    width = layer_ref.shape[2]
    half = own_half(False)
    own_lanes, lanes = half_lanes(own_half(True), width), half_lanes(half, width)
    copies = [
        pltpu.make_async_copy(source, target, sent.at[i])
        for i, (source, target) in enumerate(
            [
                (layer_own, layer_ref.at[0, :, own_lanes]),
                (layer_other, layer_ref.at[0, :, lanes]),
            ]
        )
    ]

    for copy in copies:
        copy.start()
    once(half, lambda: backward_kernel(False, *inputs, *outs))
    for copy in copies:
        copy.wait()


def head_chooser():
    rows = lax.broadcasted_iota(jnp.int32, (8, LANES), 0)
    left = left_lanes((8, LANES))
    chosen = ((rows == 0) & left) | ((rows == 1) & ~left)
    return jnp.where(chosen, 1.0, 0.0).astype(BF16)


def row_sums(rows, keep):
    first, second = halves(rows)
    third = (rows - first.astype(F32) - second.astype(F32)).astype(BF16)
    weight = jnp.where(keep, 1.0, 0.0).astype(BF16)
    return dot(
        jnp.concatenate([first, second, third], axis=1),
        jnp.concatenate([weight, weight, weight], axis=0),
    )


def final_parts(
    mine,
    key_ref,
    value_ref,
    grad_key_part_ref,
    grad_value_part_ref,
    later_ref,
    leave_ref,
    state_ref,
    grad_ref,
    table_ref,
    key_out,
    value_out,
):
    tokens, width = key_ref.shape[1:]
    half = own_half(mine)
    carry = pick_rows(table_ref[pl.ds(CARRY_ROWS, 16), :], half)
    chooser = twice(head_chooser(), 1)
    left = left_lanes((1, LANES))
    lanes = [pair_lanes(half, width, pair) for pair in range(PAIRS)]
    places = [pl.ds(pair * LANES, LANES) for pair in range(PAIRS)]
    grads = [halves(by_head(grad_ref[pl.ds(pair * 64, 64), :], 0)) for pair in range(PAIRS)]
    carried, terms = [], []
    for pair in range(PAIRS):
        carried.append(
            leave_ref[:, places[pair]]
            * dot(twice(key_ref[0, :, lanes[pair]], 1), jnp.concatenate(grads[pair], axis=0))
        )
    for pair in range(PAIRS):
        value_out[:, places[pair]] = (
            grad_value_part_ref[:, places[pair]] + carried[pair]
        ).astype(BF16)
        terms.append(stacked(carried[pair] * value_ref[0, :, lanes[pair]].astype(F32), 1))
    earlier = [dot(chooser, terms[pair], 1, 1)[:2] for pair in range(PAIRS)]
    key_parts = [
        dot(twice(value_ref[0, :, lanes[pair]], 1), jnp.concatenate(grads[pair], axis=1), 1, 1)
        for pair in range(PAIRS)
    ]
    through_rows = []
    for pair in range(PAIRS):
        block = pl.ds(pair * 64, 64)
        product = jnp.sum(grad_ref[block, :] * state_ref[block, :], axis=0, keepdims=True)
        for side in (left, ~left):
            through_rows.append(jnp.sum(jnp.where(side, product, 0.0), axis=1, keepdims=True))
    for pair in range(PAIRS):
        key_out[:, places[pair]] = (
            grad_key_part_ref[:, places[pair]] + leave_ref[:, places[pair]] * key_parts[pair]
        ).astype(BF16)
    return (
        later_ref[...]
        + row_sums(jnp.concatenate(earlier, axis=0), triangle(tokens, lambda u, t: u < t))
        + carry * jnp.concatenate(through_rows, axis=0)
    )


def own_final_kernel(*refs):
    *refs, rows_ref = refs
    rows_ref[...] = final_parts(True, *refs)


def other_final_kernel(*refs):
    inputs, done, (other_ref, gain_part_ref) = refs[:9], refs[9:13], refs[13:15]
    grad_query_ref, grad_key_ref, grad_value_ref, decay_ref, gain_ref = refs[15:20]
    *parts, decay_out, gain_out, sent = refs[20:]
    width = grad_key_ref.shape[2]
    half = own_half(False)
    own_lanes, lanes = half_lanes(own_half(True), width), half_lanes(half, width)
    pairs = [
        (done[0], grad_query_ref.at[0, :, own_lanes]),
        (done[1], grad_query_ref.at[0, :, lanes]),
        (done[2], grad_key_ref.at[0, :, own_lanes]),
        (done[3], grad_value_ref.at[0, :, own_lanes]),
        (gain_out, gain_ref),
        (parts[0], grad_key_ref.at[0, :, lanes]),
        (parts[1], grad_value_ref.at[0, :, lanes]),
        (decay_out, decay_ref.at[0]),
    ]
    copies = [
        pltpu.make_async_copy(source, target, sent.at[i])
        for i, (source, target) in enumerate(pairs)
    ]
    gain_out[...] = gain_part_ref[...] + inputs[7][pl.ds(PAIRS * 64, 2 * PAIRS), :]

    for copy in copies[:5]:
        copy.start()

    def work():
        rows = final_parts(False, *inputs, *parts)
        other = other_ref[...]
        decay_out[...] = jnp.where(
            half == 0,
            jnp.concatenate([rows, other], axis=0),
            jnp.concatenate([other, rows], axis=0),
        )

    once(half, work)
    for copy in copies[5:]:
        copy.start()
    for copy in copies:
        copy.wait()


VMEM, HBM = pltpu.VMEM, pltpu.HBM


def call(kernel, operands, results, scratch=(), aliases=None, flops=0, constrain=False):
    read = sum(a.size * a.dtype.itemsize for a, memory in operands if memory is VMEM)
    return pl.pallas_call(
        kernel,
        in_specs=[pl.BlockSpec(memory_space=memory) for a, memory in operands],
        out_specs=[pl.BlockSpec(memory_space=memory) for shape, dtype, memory in results],
        out_shape=[jax.ShapeDtypeStruct(shape, dtype) for shape, dtype, memory in results],
        scratch_shapes=list(scratch),
        input_output_aliases=aliases or {},
        compiler_params=pltpu.CompilerParams(vmem_limit_bytes=VMEM_BYTES),
        cost_estimate=pl.CostEstimate(flops=flops, bytes_accessed=read, transcendentals=0),
    )(
        *[
            pltpu.with_memory_space_constraint(a, HBM) if memory is HBM and constrain else a
            for a, memory in operands
        ]
    )


def local(queries, key_vectors, value_vectors, log_decay, restart, norm_gain, upstream):
    tokens, width = queries.shape[1], queries.shape[2]
    state_rows = PAIRS * 64
    buffer_rows = state_rows + 8
    blocks = lax.axis_size("seq")
    scans = lax.axis_size("dp")
    position = lax.axis_index("seq")
    on_first = (position & 1) == 0

    def exchange(x, bit, axis="seq"):
        size = blocks if axis == "seq" else scans
        return lax.ppermute(x, axis, [(i, i ^ bit) for i in range(size)])

    def exchange_mixed(x, *bits):
        pairs = [
            (i * scans + j, (i ^ bits[i & 1][0]) * scans + (j ^ bits[i & 1][1]))
            for i in range(blocks)
            for j in range(scans)
        ]
        return lax.ppermute(x, ("seq", "dp"), pairs)

    def exchange_by_core(x, first, second):
        bits = (first, second)
        return lax.ppermute(x, "seq", [(i, i ^ bits[i & 1]) for i in range(blocks)])

    def by_chip(*cases):
        return jnp.where(
            is_last,
            jnp.where(is_odd, cases[3], cases[2]),
            jnp.where(is_odd, cases[1], cases[0]),
        )

    four_chips = blocks == 8 and scans == 4
    is_last = (position & 4) != 0
    is_odd = (position & 2) != 0

    def parts(buffer):
        state = buffer[:state_rows].reshape(PAIRS, 64, LANES)
        if buffer.shape[0] == state_rows:
            return state, None
        return state, buffer[state_rows : state_rows + PAIRS].reshape(PAIRS, 1, LANES)

    def joined(state, carry):
        return jnp.concatenate(
            [
                state.reshape(state_rows, LANES),
                carry.reshape(PAIRS, LANES),
                jnp.zeros((8 - PAIRS, LANES), F32),
            ],
            axis=0,
        )

    def flat(state):
        return state.reshape(state_rows, LANES)

    whole = (1, tokens, width)
    part = (tokens, width // 2)
    buffer = (buffer_rows, LANES)
    rows = (HEAD_TOTAL // 2, LANES)

    gain_rows = norm_gain.reshape(2 * PAIRS, LANES)

    state_other, tables, key_vectors, value_vectors = call(
        first_state_kernel,
        [
            (key_vectors, HBM),
            (value_vectors, HBM),
            (jnp.swapaxes(log_decay, 1, 2), HBM),
            (restart, HBM),
        ],
        [
            (buffer, F32, VMEM),
            ((TABLE_ROWS, LANES), F32, VMEM),
            (whole, BF16, VMEM),
            (whole, BF16, VMEM),
        ],
        [
            pltpu.VMEM((HEAD_TOTAL, tokens), F32),
            pltpu.VMEM((1, tokens), jnp.int32),
            pltpu.SemaphoreType.DMA((6,)),
        ],
        constrain=True,
    )
    blocks_of = [(queries, VMEM), (key_vectors, VMEM), (value_vectors, VMEM)]
    swapped = exchange(state_other, 1)
    state_own, mask = call(
        second_state_kernel,
        [(key_vectors, VMEM), (value_vectors, VMEM), (tables, VMEM)],
        [(buffer, F32, VMEM), ((tokens, tokens), F32, VMEM)],
    )
    first_state, first_carry = parts(jnp.where(on_first, state_own, swapped))
    second_state, second_carry = parts(jnp.where(on_first, swapped, state_own))
    total = second_carry * first_state + second_state
    carry = first_carry * second_carry
    prefix = jnp.zeros_like(total)
    prefix_carry = jnp.ones_like(carry)

    def mixture(mine, tables):
        return call(
            functools.partial(mixture_kernel, mine),
            blocks_of + [(upstream, VMEM), (gain_rows, VMEM), (tables, VMEM), (mask, VMEM)],
            [
                (part, F32, VMEM),
                ((width // 2, LANES), BF16, VMEM),
                (part, F32, VMEM),
                (part, F32, VMEM),
            ],
            flops=0,
        )

    mixed = {}
    levels = []
    if four_chips:
        sent = joined(total, carry)
        sent, tables = lax.optimization_barrier((sent, tables))
        mixed[True] = mixture(True, tables)
        received = exchange_by_core(sent, 6, 2)
        received, mixed[True] = lax.optimization_barrier((received, mixed[True]))
        near, near_carry = parts(received)
        own_first = near_carry * total + near
        own_last = carry * near + total
        sent = jnp.where(
            on_first,
            by_chip(total, own_first, own_last, near),
            jnp.where(is_odd, own_last, own_first),
        )
        sent = joined(sent, carry * near_carry)
        sent, tables = lax.optimization_barrier((sent, tables))
        mixed[False] = mixture(False, tables)
        received = exchange_by_core(sent, 2, 6)
        received, mixed[False] = lax.optimization_barrier((received, mixed[False]))
        far, far_carry = parts(received)
        near_last = near_carry * far + near
        prefix = jnp.where(
            on_first,
            by_chip(0.0, far, near_last, far_carry * near + far),
            by_chip(0.0, near, far, near_last),
        )
    bit = 2
    while bit < blocks and not four_chips:
        is_upper = (position & bit) != 0
        sent = flat(total) if 2 * bit == blocks else joined(total, carry)
        mine = not mixed
        if len(mixed) < 2:
            sent, tables = lax.optimization_barrier((sent, tables))
            mixed[mine] = mixture(mine, tables)
        received = exchange(sent, 2 * bit - 2)
        if len(levels) < 2:
            received, mixed[mine] = lax.optimization_barrier((received, mixed[mine]))
        theirs, their_carry = parts(received)
        prefix = jnp.where(is_upper, prefix_carry * theirs + prefix, prefix)
        levels.append((bit, is_upper, carry, their_carry))
        if their_carry is None:
            break
        prefix_carry = jnp.where(is_upper, prefix_carry * their_carry, prefix_carry)
        total = jnp.where(is_upper, carry * theirs + total, their_carry * total + theirs)
        carry = carry * their_carry
        bit *= 2
    for mine in (True, False):
        if mine not in mixed:
            mixed[mine] = mixture(mine, tables)
    after_first = first_carry * prefix + first_state
    state_in = {True: flat(jnp.where(on_first, prefix, after_first))}
    state_in[False] = exchange(flat(jnp.where(on_first, after_first, prefix)), 1)

    layer_parts, grad_mixed, query_states = {}, {}, {}
    for mine in (True, False):
        operands = [
            *[(x, VMEM) for x in mixed[mine][:4]],
            (queries, VMEM),
            (upstream, VMEM),
            (gain_rows, VMEM),
            (state_in[mine], VMEM),
        ]
        if mine:
            kernel = lambda *refs: forward_kernel(True, *refs[:8], None, *refs[8:])
        else:
            operands.append((query_states[True], VMEM))
            kernel = functools.partial(forward_kernel, False)
        layer_parts[mine], grad_mixed[mine], query_states[mine] = call(
            kernel, operands, [(part, BF16, VMEM), (part, BF16, VMEM), (buffer, F32, VMEM)]
        )

    def backward(mine, state):
        operands = blocks_of + [
            (grad_mixed[mine], VMEM),
            (state, VMEM),
            (mixed[mine][2], VMEM),
            (tables, VMEM),
            (mask, VMEM),
        ]
        results = [
            (part, BF16, VMEM),
            (part, F32, VMEM),
            (part, F32, VMEM),
            (rows, F32, VMEM),
            (part, F32, VMEM),
        ]
        if mine:
            return call(functools.partial(backward_kernel, True), operands, results)
        return call(
            other_backward_kernel,
            operands + [(layer_parts[x], VMEM) for x in (True, False)],
            [(whole, BF16, HBM)] + results,
            [pltpu.SemaphoreType.DMA((2,))],
        )

    steps = []
    step = scans // 2
    while step:
        steps.append(step)
        step //= 2
    swapped = exchange(query_states[False], 1)
    chip_gain = query_states[False][state_rows:] + swapped[state_rows:]
    gains = [jnp.where(on_first, chip_gain, 0.0)]
    first_query, _ = parts(jnp.where(on_first, query_states[True], swapped))
    second_query, _ = parts(jnp.where(on_first, swapped, query_states[True]))
    total = flat(first_query + first_carry * second_query)
    suffix = jnp.zeros_like(first_query)
    suffix_carry = jnp.ones_like(carry)
    local_parts = {}
    if four_chips:
        total, chip_gain = lax.optimization_barrier((total, chip_gain))
        received = exchange_by_core(jnp.concatenate([total, chip_gain], axis=0), 6, 2)
        fetched = [
            exchange_mixed(chip_gain, *bits)
            for bits in (((0, 1), (0, 3)), ((0, 2), (2, 2)), ((2, 3), (2, 1)))
        ]
        near = parts(received)[0]
        own_query = parts(total)[0]
        own_first = own_query + carry * near
        total = flat(
            jnp.where(
                on_first,
                by_chip(near, own_first, own_query, own_query),
                jnp.where(is_odd, near + near_carry * own_query, own_first),
            )
        )
        gain = jnp.where(on_first, 0.0, chip_gain + received[state_rows:]) + sum(fetched)
        total, state = lax.optimization_barrier((total, state_in[False]))
        received = exchange_by_core(total, 2, 6)
        others = exchange(gain, 4)
        local_parts[True] = backward(True, state_in[True])
        local_parts[False] = backward(False, state)
        received, others, local_parts = lax.optimization_barrier((received, others, local_parts))
        gains = [gain, others]
        far = parts(received)[0]
        near_first = near + near_carry * far
        suffix = jnp.where(
            on_first,
            by_chip(far + far_carry * near, near_first, far, 0.0),
            by_chip(near_first, far, near, 0.0),
        )
    for bit, is_upper, carry, their_carry in levels:
        partner = 2 * bit - 2
        mine = not local_parts
        beside = len(local_parts) < 2
        if bit == 2:
            total, state = lax.optimization_barrier((total, state_in[mine]))
            received = exchange(total, partner)
            gain = sum(gains)
            for step in steps:
                gains = [gain, exchange(gain, step, "dp")]
                gain = sum(gains)
            if len(levels) == 1:
                gains = [gain, exchange(gain, partner)]
        else:
            total, gain, state = lax.optimization_barrier((total, sum(gains), state_in[mine]))
            received = exchange(jnp.concatenate([total, gain], axis=0), partner)
            gains = [gain]
            if 2 * bit == blocks:
                gains += [exchange(gain, 2), exchange(gain, partner ^ 2)]
        if beside:
            local_parts[mine] = backward(mine, state)
            received, gains, local_parts[mine] = lax.optimization_barrier(
                (received, gains, local_parts[mine])
            )
        if bit > 2:
            gains.append(received[state_rows:])
        theirs, _ = parts(received)
        total = parts(total)[0]
        suffix = jnp.where(is_upper, suffix, suffix_carry * theirs + suffix)
        if their_carry is None:
            break
        suffix_carry = jnp.where(is_upper, suffix_carry, suffix_carry * their_carry)
        total = flat(jnp.where(is_upper, theirs + their_carry * total, total + carry * theirs))
    for mine in (True, False):
        if mine not in local_parts:
            local_parts[mine] = backward(mine, state_in[mine])
    if blocks == 2:
        gain = sum(gains)
        for step in steps:
            gain = gain + exchange(gain, step, "dp")
        gains = [gain]
    before_second = second_query + second_carry * suffix
    state_grad = {True: flat(jnp.where(on_first, before_second, suffix))}
    gain = sum(gains)
    swapped = exchange(
        jnp.concatenate([flat(jnp.where(on_first, suffix, before_second)), gain], axis=0), 1
    )
    state_grad[False] = swapped

    def final_operands(mine):
        grad_key_part, grad_value_part, later, leave = local_parts[mine][-4:]
        return [
            (x, VMEM)
            for x in (
                key_vectors,
                value_vectors,
                grad_key_part,
                grad_value_part,
                later,
                leave,
                state_in[mine],
                state_grad[mine],
                tables,
            )
        ]

    grad_key, grad_value, decay_rows = call(
        own_final_kernel,
        final_operands(True),
        [(part, BF16, VMEM), (part, BF16, VMEM), (rows, F32, VMEM)],
    )
    finished = [local_parts[mine][-5] for mine in (True, False)]
    finished += [grad_key, grad_value, decay_rows, gain]
    grad_query, grad_key, grad_value, grad_decay, grad_gain = call(
        other_final_kernel,
        final_operands(False) + [(x, VMEM) for x in finished],
        [
            (whole, BF16, HBM),
            (whole, BF16, HBM),
            (whole, BF16, HBM),
            ((1, HEAD_TOTAL, tokens), F32, HBM),
            ((2 * PAIRS, LANES), F32, HBM),
        ],
        [
            pltpu.VMEM(part, BF16),
            pltpu.VMEM(part, BF16),
            pltpu.VMEM((HEAD_TOTAL, tokens), F32),
            pltpu.VMEM((2 * PAIRS, LANES), F32),
            pltpu.SemaphoreType.DMA((8,)),
        ],
    )
    return (
        local_parts[False][0],
        grad_query,
        grad_key,
        grad_value,
        jnp.swapaxes(grad_decay, 1, 2),
        grad_gain.reshape(-1),
    )


def solution(mesh):
    rows = P("dp", "seq", None)
    return jax.shard_map(
        local,
        mesh=mesh,
        in_specs=(rows, rows, rows, rows, P("dp", "seq"), P(), rows),
        out_specs=(rows, rows, rows, rows, rows, P()),
        check_vma=False,
    )
```
